32 devices in a mesh: bx: 8 (over z, core), by: 4 (over y, x).
Axes of the slice: x: 2, y: 2, z: 4, core: 2. Of those that a mesh axis runs over, the one named last changes fastest.
Arguments:
- tracers: float32 [2, 20, 64, 512], P(None, None, 'bx', 'by'), may hold values from -6 to 6
- velocity: float32 [2, 20, 64, 512], P(None, None, 'bx', 'by'), may hold values from -6 to 6
- wet_levels: int32 [64, 512], P('bx', 'by'), may hold values from 0 to 20, as said below
- thickness: float32 [20], replicated, may hold values from 0.1 to 1
- diagonal: float32 [64, 512], P('bx'), may hold values from 0.05 to 1
Outputs:
- new_tracers: float32 [2, 20, 64, 512], P(None, None, 'bx', 'by')
- new_velocity: float32 [2, 20, 64, 512], P(None, None, 'bx', 'by')
- surface_pressure: float32 [64, 512], P('bx', 'by')
The draws below stay inside these ranges and needn't reach their ends.
Inputs may be any that keep to these rules, and one draw needn't show every extreme that they name: `wet_levels`: 0 marks land; a column of 20 is wet to the bottom; land covers whole blocks of 8 x 128 columns (aligned at multiples of 8 and 128), and inside ocean blocks columns may also be land.
All inputs are finite; a program needn't handle non-finite values.
Results may differ from the reference program's by a relative error of at most 0.0001.
Values sent between devices are 32-bit elements; how exact they have to be, the bound alone decides.
No kernel may reach another device: no remote copies, remote signals or barrier semaphores. Data moves between devices by JAX's collectives and lax.ppermute only.
A program may use at most 64 MiB of HBM per device.

```python
import math
import jax
import jax.numpy as jnp
from jax import lax

CX = 8
CY = 128
K = 20
ITERS = 3
NX = 64
NY = 512
N_BX = 8


def draw_wet_levels(key, part):
    key = jax.random.fold_in(key, 11)
    cell_key = jax.random.fold_in(key, 1)
    block_key = jax.random.fold_in(key, 2)
    raw_levels = jax.random.randint(cell_key, (NX, NY), -(K // 3), K + 1)
    block_draw = jax.random.randint(block_key, (NX // CX, NY // CY), 0, 10)
    block_ocean = (block_draw >= 3).astype(jnp.int32)
    ocean_cells = jnp.repeat(jnp.repeat(block_ocean, CX, axis=0), CY, axis=1)
    return (jnp.maximum(raw_levels, 0) * ocean_cells).astype(jnp.int32)


def level_of(rng, dims, pieces, least, high):
    level, own = 1.0, jax.random.fold_in(rng, 6)
    for dim, blocks in pieces:
        steps = jnp.exp(jax.random.uniform(jax.random.fold_in(own, dim), (blocks,), jnp.float32, least / len(pieces), high / len(pieces)))
        level = level * jnp.repeat(steps, dims[dim] // blocks).reshape([-1 if axis == dim else 1 for axis in range(len(dims))])
    return level


def noise(rng, shape, width, bound, pieces=(), kind=jnp.bfloat16):
    values = jax.random.normal(rng, shape, jnp.float32) * width
    if len(pieces) > 0:
        values = level_of(rng, shape, pieces, -0.22, 0.18) * values
    return jnp.clip(values, min=-bound, max=bound).astype(kind)


def setup_inputs(seed: int = 0) -> dict:
    keys = jax.random.split(jax.random.key(seed), 6)
    tracers = noise(keys[0], (2, K, NX, NY), 1.0, 6.0, ((2, 8), (3, 4)), jnp.float32)
    velocity = noise(keys[1], (2, K, NX, NY), 1.0, 6.0, ((2, 8), (3, 4)), jnp.float32)
    wet_levels = draw_wet_levels(jax.random.fold_in(keys[5], 71), 0)
    thickness = jnp.clip(jnp.exp(jax.random.uniform(keys[3], (K,), jnp.float32, math.log(0.1), math.log(1.0))), 0.1, 1.0)
    diagonal = jnp.clip(jnp.exp(math.log(1.0) - 2.9957323 * jax.random.uniform(keys[4], (NX, NY), jnp.float32) ** level_of(keys[4], (NX, NY), ((0, 8),), -0.2, 0.2)), 0.05, 1.0)
    return dict(tracers=tracers, velocity=velocity, wet_levels=wet_levels, thickness=thickness, diagonal=diagonal)


HEAT_ALPHA = 0.5
SALINITY_BETA = 0.8
KAPPA_SPREAD = 0.15
VISCOSITY = 0.1
TIME_INCREMENT = 0.2
GRAVITY = 1.0


def latitude_rate(positions, total_rows):
    return 1.5 * jnp.sin(math.pi * ((positions + 0.5) / total_rows - 0.5))


def second_derivative_sum(values, wet_indicator):
    middle = values[:, 1:-1, 1:-1]
    summed = wet_indicator[:, 2:, 1:-1] * (values[:, 2:, 1:-1] - middle)
    summed = summed + wet_indicator[:, :-2, 1:-1] * (values[:, :-2, 1:-1] - middle)
    summed = summed + wet_indicator[:, 1:-1, 2:] * (values[:, 1:-1, 2:] - middle)
    summed = summed + wet_indicator[:, 1:-1, :-2] * (values[:, 1:-1, :-2] - middle)
    return wet_indicator[:, 1:-1, 1:-1] * summed


def clinic(haloed_array, thickness, coriolis):
    theta_heat = haloed_array[0]
    salinity_amount = haloed_array[1]
    zonal_flow = haloed_array[2]
    meridional = haloed_array[3]
    wet_indicator = haloed_array[4]
    seawater_rho = SALINITY_BETA * salinity_amount - HEAT_ALPHA * theta_heat
    pressure = jnp.cumsum(thickness[:, None, None] * wet_indicator * seawater_rho, axis=0)
    wet_mid = wet_indicator[:, 1:-1, 1:-1]
    grad_x = wet_mid * wet_indicator[:, 2:, 1:-1] * wet_indicator[:, :-2, 1:-1] * (pressure[:, 2:, 1:-1] - pressure[:, :-2, 1:-1]) * 0.5
    grad_y = wet_mid * wet_indicator[:, 1:-1, 2:] * wet_indicator[:, 1:-1, :-2] * (pressure[:, 1:-1, 2:] - pressure[:, 1:-1, :-2]) * 0.5
    zonal_mid = zonal_flow[:, 1:-1, 1:-1]
    merid_mid = meridional[:, 1:-1, 1:-1]
    zonal_rate = wet_mid * (coriolis * merid_mid - grad_x + VISCOSITY * second_derivative_sum(zonal_flow, wet_indicator))
    merid_rate = wet_mid * (-coriolis * zonal_mid - grad_y + VISCOSITY * second_derivative_sum(meridional, wet_indicator))
    next_theta = theta_heat[:, 1:-1, 1:-1] + (TIME_INCREMENT * KAPPA_SPREAD) * second_derivative_sum(theta_heat, wet_indicator)
    next_salinity = salinity_amount[:, 1:-1, 1:-1] + (TIME_INCREMENT * KAPPA_SPREAD) * second_derivative_sum(salinity_amount, wet_indicator)
    next_eastward_speed = zonal_mid + TIME_INCREMENT * zonal_rate
    next_northward_speed = merid_mid + TIME_INCREMENT * merid_rate
    weights = thickness[:, None, None] * wet_mid
    eastward_current = jnp.sum(weights * next_eastward_speed, axis=0)
    northward_current = jnp.sum(weights * next_northward_speed, axis=0)
    return jnp.stack([next_theta, next_salinity]), jnp.stack([next_eastward_speed, next_northward_speed]), eastward_current, northward_current


def divergence(flow_x_wide, flow_y_wide, ocean_mask):
    return ocean_mask * (((flow_x_wide[2:, 1:-1] - flow_x_wide[:-2, 1:-1]) + (flow_y_wide[1:-1, 2:] - flow_y_wide[1:-1, :-2])) * 0.5)


def stencil(padded, values, ocean_mask, diagonal):
    neighbours = padded[2:, 1:-1] + padded[:-2, 1:-1] + padded[1:-1, 2:] + padded[1:-1, :-2]
    return ocean_mask * ((4.0 + diagonal) * values - neighbours)


def block_sum(values, block_x, block_y):
    blocked = values.reshape(values.shape[0] // block_x, block_x, values.shape[1] // block_y, block_y)
    padded = jnp.pad(blocked, ((0, 0), (1, 1), (0, 0), (1, 1)))
    summed = padded[:, 2:, :, 1:-1] + padded[:, :-2, :, 1:-1] + padded[:, 1:-1, :, 2:] + padded[:, 1:-1, :, :-2]
    return summed.reshape(values.shape)


def schwarz(residual, ocean_mask, diagonal, block_x, block_y):
    centre_coef = 4.0 + diagonal
    inverse = ocean_mask / centre_coef
    first_sweep = inverse * residual
    local_image = ocean_mask * (centre_coef * first_sweep - block_sum(first_sweep, block_x, block_y))
    return inverse * (2.0 * residual - local_image)


def reference(tracers, velocity, wet_levels, thickness, diagonal):
    wet_indicator = (jnp.arange(K, dtype=jnp.int32)[:, None, None] < wet_levels[None]).astype(jnp.float32)
    state_stack = jnp.concatenate([tracers, velocity, wet_indicator[None]], axis=0)
    padded = jnp.pad(state_stack, ((0, 0), (0, 0), (1, 1), (1, 1)))
    coriolis = latitude_rate(jnp.arange(NY, dtype=jnp.int32).astype(jnp.float32), NY)

    def stripe(index):
        piece = lax.dynamic_slice_in_dim(padded, index * CX, CX + 2, axis=2)
        return clinic(piece, thickness, coriolis)

    results = lax.map(stripe, jnp.arange(N_BX, dtype=jnp.int32))
    new_tracers = jnp.moveaxis(results[0], 0, 2).reshape(2, K, NX, NY)
    moved_velocity = jnp.moveaxis(results[1], 0, 2).reshape(2, K, NX, NY)
    eastward_current = results[2].reshape(NX, NY)
    northward_current = results[3].reshape(NX, NY)
    ocean_mask = wet_indicator[0]
    forcing = divergence(jnp.pad(eastward_current, 1), jnp.pad(northward_current, 1), ocean_mask)

    residual = forcing
    smoothed = schwarz(residual, ocean_mask, diagonal, CX, CY)
    direction = smoothed
    inner_now = jnp.sum(residual * smoothed)
    solution = jnp.zeros_like(forcing)
    for iteration in range(ITERS):
        operator_image = stencil(jnp.pad(direction, 1), direction, ocean_mask, diagonal)
        step_size = inner_now / jnp.sum(direction * operator_image)
        solution = solution + step_size * direction
        residual = residual - step_size * operator_image
        if iteration + 1 < ITERS:
            smoothed = schwarz(residual, ocean_mask, diagonal, CX, CY)
            inner_next = jnp.sum(residual * smoothed)
            direction = smoothed + (inner_next / inner_now) * direction
            inner_now = inner_next
    padded_surface = jnp.pad(solution, 1)
    slope_x = (padded_surface[2:, 1:-1] - padded_surface[:-2, 1:-1]) * 0.5
    slope_y = (padded_surface[1:-1, 2:] - padded_surface[1:-1, :-2]) * 0.5
    slopes = jnp.stack([slope_x, slope_y])
    new_velocity = moved_velocity - GRAVITY * (wet_indicator[None] * slopes[:, None])
    return new_tracers, new_velocity, solution
```

```python
import math

import jax
import jax.numpy as jnp
from jax import lax
from jax.experimental import pallas as pl
from jax.experimental.pallas import tpu as pltpu
from jax.sharding import PartitionSpec as P

ITERS = 3

HEAT_ALPHA = 0.5
SALINITY_BETA = 0.8
KAPPA_SPREAD = 0.15
VISCOSITY = 0.1
TIME_INCREMENT = 0.2
GRAVITY = 1.0

VMEM = pl.BlockSpec(memory_space=pltpu.VMEM)
SMEM = pl.BlockSpec(memory_space=pltpu.SMEM)


def lanes_of(shape):
    return lax.broadcasted_iota(jnp.int32, shape, 1)


def sublanes_of(shape):
    return lax.broadcasted_iota(jnp.int32, shape, 0)


def pack_rims(tracers, velocity, wet, first_rows, last_rows, first_cols, last_cols):
    levels, cols_x, rows_y = tracers.shape[1:]
    lane = lanes_of((cols_x, rows_y))
    counts = wet[...].astype(jnp.float32)
    first, last = jnp.zeros_like(counts), jnp.zeros_like(counts)
    for index in range(4 * levels + 1):
        field, level = divmod(index, levels)
        if field < 4:
            tile = (tracers if field < 2 else velocity)[field % 2, level]
        else:
            tile = counts
        first_rows[index : index + 1, :] = tile[0:1, :]
        last_rows[index : index + 1, :] = tile[cols_x - 1 : cols_x, :]
        first = jnp.where(lane == index, tile[:, 0:1], first)
        last = jnp.where(lane == index, tile[:, rows_y - 1 : rows_y], last)
    first_cols[...] = first
    last_cols[...] = last


def level_kernel(
    tracers, velocity, wet, diagonal, thickness, latitude, x_before, x_after, y_before, y_after,
    new_tracers, moved_velocity, surface,
):
    levels, cols_x, rows_y = tracers.shape[1:]
    shape = (cols_x, rows_y)
    lane, sublane = (lanes_of(shape), sublanes_of(shape))
    low_x, high_x = (sublane == 0, sublane == cols_x - 1)
    low_y, high_y = (lane == 0, lane == rows_y - 1)
    before_cols, after_cols = (y_before[...], y_after[...])

    def neighbours(tile, index):
        return (
            jnp.where(high_x, x_after[index : index + 1, :], pltpu.roll(tile, cols_x - 1, 0)),
            jnp.where(low_x, x_before[index : index + 1, :], pltpu.roll(tile, 1, 0)),
            jnp.where(high_y, after_cols[:, index : index + 1], pltpu.roll(tile, rows_y - 1, 1)),
            jnp.where(low_y, before_cols[:, index : index + 1], pltpu.roll(tile, 1, 1)),
        )

    counts = wet[...].astype(jnp.float32)
    around = neighbours(counts, 4 * levels)
    shared = [jnp.minimum(counts, other) for other in around]
    both_x = jnp.minimum(shared[0], shared[1])
    both_y = jnp.minimum(shared[2], shared[3])
    coriolis = jnp.broadcast_to(latitude[...], shape)
    zero = jnp.zeros(shape, jnp.float32)
    difference_x, difference_y, flow_x, flow_y = (zero, zero, zero, zero)
    for level in range(levels):
        here = counts > level
        open_to = [other > level for other in shared]
        wet_around = [other > level for other in around]
        weight = thickness[level]
        heat, salt = (tracers[0, level], tracers[1, level])
        zonal, merid = (velocity[0, level], velocity[1, level])
        heat_around = neighbours(heat, level)
        salt_around = neighbours(salt, levels + level)

        def laplacian(tile, others):
            total = zero
            for other, passable in zip(others, open_to):
                total = total + jnp.where(passable, other - tile, 0.0)
            return total

        loads = [
            jnp.where(is_wet, SALINITY_BETA * s - HEAT_ALPHA * t, 0.0)
            for is_wet, s, t in zip(wet_around, salt_around, heat_around)
        ]
        difference_x = difference_x + weight * (loads[0] - loads[1])
        difference_y = difference_y + weight * (loads[2] - loads[3])
        gradient_x = jnp.where(both_x > level, difference_x * 0.5, 0.0)
        gradient_y = jnp.where(both_y > level, difference_y * 0.5, 0.0)
        diffusivity = TIME_INCREMENT * KAPPA_SPREAD
        new_tracers[0, level] = heat + diffusivity * laplacian(heat, heat_around)
        new_tracers[1, level] = salt + diffusivity * laplacian(salt, salt_around)
        spread_x = laplacian(zonal, neighbours(zonal, 2 * levels + level))
        spread_y = laplacian(merid, neighbours(merid, 3 * levels + level))
        zonal_rate = coriolis * merid - gradient_x + VISCOSITY * spread_x
        merid_rate = -coriolis * zonal - gradient_y + VISCOSITY * spread_y
        next_zonal = zonal + jnp.where(here, TIME_INCREMENT * zonal_rate, 0.0)
        next_merid = merid + jnp.where(here, TIME_INCREMENT * merid_rate, 0.0)
        moved_velocity[0, level] = next_zonal
        moved_velocity[1, level] = next_merid
        flow_x = flow_x + jnp.where(here, weight * next_zonal, 0.0)
        flow_y = flow_y + jnp.where(here, weight * next_merid, 0.0)
    row_start = pl.multiple_of(lax.axis_index("by") * rows_y, rows_y)
    surface[0] = flow_x
    surface[1] = flow_y
    surface[2] = jnp.where(counts > 0, 1.0, 0.0)
    surface[3] = diagonal[:, pl.ds(row_start, rows_y)]


def solve_kernel(
    blocks_x, blocks_y, gathered, moved_velocity, wet,
    new_velocity, pressure,
    inverse, residual, smooth_0, smooth_1, smooth_2, image_0, image_1, direction_1,
):
    cols_x, rows_y = gathered.shape[2:]
    levels = moved_velocity.shape[1]
    shape = (cols_x, rows_y)
    lane, sublane = (lanes_of(shape), sublanes_of(shape))
    low_x, high_x = (sublane == 0, sublane == cols_x - 1)
    low_y, high_y = (lane == 0, lane == rows_y - 1)
    zero = jnp.zeros(shape, jnp.float32)

    def each_row(step, carry):
        if blocks_x <= 8:
            for row in range(blocks_x):
                carry = step(row, carry)
            return carry
        return lax.fori_loop(0, blocks_x, step, carry)

    def guarded(load, row, column):
        if isinstance(row, int):
            return load(row * blocks_y + column) if 0 <= row < blocks_x else zero
        inside = jnp.logical_and(row >= 0, row < blocks_x)
        return load(jnp.clip(row, 0, blocks_x - 1) * blocks_y + column) * inside.astype(jnp.float32)

    def after_x(load, tile, row, column):
        other = guarded(load, row + 1, column)
        return jnp.where(high_x, pltpu.roll(other, cols_x - 1, 0), pltpu.roll(tile, cols_x - 1, 0))

    def before_x(load, tile, row, column):
        other = guarded(load, row - 1, column)
        return jnp.where(low_x, pltpu.roll(other, 1, 0), pltpu.roll(tile, 1, 0))

    def along_y(tiles):
        ahead = [pltpu.roll(tile, rows_y - 1, 1) for tile in tiles] + [zero]
        behind = [zero] + [pltpu.roll(tile, 1, 1) for tile in tiles]
        after = [jnp.where(high_y, ahead[c + 1], ahead[c]) for c in range(blocks_y)]
        before = [jnp.where(low_y, behind[c], behind[c + 1]) for c in range(blocks_y)]
        return after, before

    def smoothed_by(inv, tile):
        first = inv * tile
        near = jnp.where(high_x, 0.0, pltpu.roll(first, cols_x - 1, 0))
        near = near + jnp.where(low_x, 0.0, pltpu.roll(first, 1, 0))
        near = near + jnp.where(high_y, 0.0, pltpu.roll(first, rows_y - 1, 1))
        near = near + jnp.where(low_y, 0.0, pltpu.roll(first, 1, 1))
        return inv * (tile + near)

    def total(values):
        return jnp.sum(values, axis=(0, 1), keepdims=True)

    def start(row, carry):
        flow_y = [gathered[row * blocks_y + c, 1] for c in range(blocks_y)]
        after, before = along_y(flow_y)
        for column in range(blocks_y):
            index = row * blocks_y + column
            flow = gathered[index, 0]
            load = lambda i: gathered[i, 0]
            slope = after_x(load, flow, row, column) - before_x(load, flow, row, column)
            ocean = gathered[index, 2]
            forcing = ocean * ((slope + (after[column] - before[column])) * 0.5)
            inv = ocean / (4.0 + gathered[index, 3])
            inverse[index] = inv
            residual[index] = forcing
            smooth_0[index] = smoothed_by(inv, forcing)
        return carry

    def operate(smooth, image):
        def step(row, carry):
            inner, curvature = carry
            tiles = [smooth[row * blocks_y + c] for c in range(blocks_y)]
            after, before = along_y(tiles)
            for column in range(blocks_y):
                index = row * blocks_y + column
                tile = tiles[column]
                load = lambda i: smooth[i]
                near = after_x(load, tile, row, column) + before_x(load, tile, row, column)
                near = near + after[column] + before[column]
                centre = 4.0 + gathered[index, 3]
                result = gathered[index, 2] * (centre * tile - near)
                if image is not None:
                    image[index] = result
                inner = inner + residual[index] * tile
                curvature = curvature + tile * result
            return inner, curvature

        inner, curvature = each_row(step, (zero, zero))
        return total(inner), total(curvature)

    each_row(start, 0)
    inner_0, curvature_0 = operate(smooth_0, image_0)
    step_0 = inner_0 / curvature_0

    def advance_0(row, carry):
        for column in range(blocks_y):
            index = row * blocks_y + column
            left = residual[index] - step_0 * image_0[index]
            residual[index] = left
            smooth_1[index] = smoothed_by(inverse[index], left)
        return carry

    each_row(advance_0, 0)
    inner_1, curvature_1 = operate(smooth_1, image_1)
    turn_1 = inner_1 / inner_0
    step_1 = inner_1 / (curvature_1 - turn_1 * inner_1 / step_0)

    def advance_1(row, carry):
        for column in range(blocks_y):
            index = row * blocks_y + column
            direction_1[index] = smooth_1[index] + turn_1 * smooth_0[index]
            image = image_1[index] + turn_1 * image_0[index]
            left = residual[index] - step_1 * image
            residual[index] = left
            smooth_2[index] = smoothed_by(inverse[index], left)
        return carry

    each_row(advance_1, 0)
    inner_2, curvature_2 = operate(smooth_2, None)
    turn_2 = inner_2 / inner_1
    step_2 = inner_2 / (curvature_2 - turn_2 * inner_2 / step_1)

    def iterate(index):
        previous = direction_1[index]
        result = step_0 * smooth_0[index] + step_1 * previous
        return result + step_2 * (smooth_2[index] + turn_2 * previous)

    own_x, own_y = (lax.axis_index("bx"), lax.axis_index("by"))

    def block(shift_x, shift_y):
        row, column = (own_x + shift_x, own_y + shift_y)
        inside = (row >= 0) & (row < blocks_x) & (column >= 0) & (column < blocks_y)
        row, column = (jnp.clip(row, 0, blocks_x - 1), jnp.clip(column, 0, blocks_y - 1))
        return jnp.where(inside, iterate(row * blocks_y + column), 0.0)

    own = iterate(own_x * blocks_y + own_y)
    pressure[...] = own
    upper = jnp.where(high_x, pltpu.roll(block(1, 0), cols_x - 1, 0), pltpu.roll(own, cols_x - 1, 0))
    lower = jnp.where(low_x, pltpu.roll(block(-1, 0), 1, 0), pltpu.roll(own, 1, 0))
    slope_x = GRAVITY * ((upper - lower) * 0.5)
    upper = jnp.where(high_y, pltpu.roll(block(0, 1), rows_y - 1, 1), pltpu.roll(own, rows_y - 1, 1))
    lower = jnp.where(low_y, pltpu.roll(block(0, -1), 1, 1), pltpu.roll(own, 1, 1))
    slope_y = GRAVITY * ((upper - lower) * 0.5)
    counts = wet[...]
    for level in range(levels):
        here = counts > level
        new_velocity[0, level] = moved_velocity[0, level] - jnp.where(here, slope_x, 0.0)
        new_velocity[1, level] = moved_velocity[1, level] - jnp.where(here, slope_y, 0.0)


def latitude_rate(positions, total_rows):
    return 1.5 * jnp.sin(math.pi * ((positions + 0.5) / total_rows - 0.5))


def body(tracers, velocity, wet_levels, thickness, diagonal):
    levels = tracers.shape[1]
    cols_x, rows_y = wet_levels.shape
    blocks_x, blocks_y = (lax.axis_size("bx"), lax.axis_size("by"))
    blocks = blocks_x * blocks_y
    shape = (cols_x, rows_y)
    rim_rows = 4 * levels + 1

    def like(*dims):
        return jax.ShapeDtypeStruct(dims, jnp.float32)

    first_rows, last_rows, first_cols, last_cols = pl.pallas_call(
        pack_rims,
        out_shape=[like(rim_rows, rows_y)] * 2 + [like(*shape)] * 2,
        in_specs=[VMEM] * 3,
        out_specs=[VMEM] * 4,
    )(tracers, velocity, wet_levels)

    def neighbours_of(axis, first, last):
        up = [(i, i + 1) for i in range(lax.axis_size(axis) - 1)]
        down = [(j, i) for i, j in up]
        return lax.ppermute(last, axis, up), lax.ppermute(first, axis, down)

    y_before, y_after = neighbours_of("by", first_cols, last_cols)
    x_before, x_after = neighbours_of("bx", first_rows, last_rows)
    positions = (lax.axis_index("by") * rows_y + jnp.arange(rows_y, dtype=jnp.int32)).astype(jnp.float32)
    latitude = latitude_rate(positions, blocks_y * rows_y)[None]

    new_tracers, moved_velocity, surface = pl.pallas_call(
        level_kernel,
        out_shape=[like(*tracers.shape), like(*velocity.shape), like(4, *shape)],
        in_specs=[VMEM] * 4 + [SMEM] + [VMEM] * 5,
        out_specs=[VMEM] * 3,
    )(
        tracers, velocity, wet_levels, diagonal, thickness, latitude,
        x_before, x_after, y_before, y_after,
    )
    gathered = lax.all_gather(surface, ("bx", "by"), axis=0, tiled=False)

    def solve(*refs):
        solve_kernel(blocks_x, blocks_y, *refs)

    new_velocity, pressure = pl.pallas_call(
        solve,
        out_shape=[like(*velocity.shape), like(*shape)],
        in_specs=[VMEM] * 3,
        out_specs=[VMEM] * 2,
        scratch_shapes=[pltpu.VMEM((blocks, *shape), jnp.float32)] * 8,
        compiler_params=pltpu.CompilerParams(vmem_limit_bytes=(4 + 52 * blocks // 1024) * 2**20),
    )(gathered, moved_velocity, wet_levels)
    return new_tracers, new_velocity, pressure


def solution(mesh):
    placed = (
        P(None, None, "bx", "by"),
        P(None, None, "bx", "by"),
        P("bx", "by"),
        P(),
        P("bx", None),
    )
    return jax.shard_map(
        body,
        mesh=mesh,
        in_specs=placed,
        out_specs=(P(None, None, "bx", "by"), P(None, None, "bx", "by"), P("bx", "by")),
        check_vma=False,
    )
```

```python
import math

import jax
import jax.numpy as jnp
from jax import lax
from jax.experimental import pallas as pl
from jax.experimental.pallas import tpu as pltpu
from jax.sharding import PartitionSpec as P

ITERS = 3

HEAT_ALPHA = 0.5
SALINITY_BETA = 0.8
KAPPA_SPREAD = 0.15
VISCOSITY = 0.1
TIME_INCREMENT = 0.2
GRAVITY = 1.0

VMEM = pl.BlockSpec(memory_space=pltpu.VMEM)
SMEM = pl.BlockSpec(memory_space=pltpu.SMEM)


def lanes_of(shape):
    return lax.broadcasted_iota(jnp.int32, shape, 1)


def sublanes_of(shape):
    return lax.broadcasted_iota(jnp.int32, shape, 0)


def pack_rims(tracers, velocity, wet, first_rows, last_rows, first_cols, last_cols):
    levels, cols_x, rows_y = tracers.shape[1:]
    lane = lanes_of((cols_x, rows_y))
    counts = wet[...].astype(jnp.float32)
    first, last = jnp.zeros_like(counts), jnp.zeros_like(counts)
    for index in range(4 * levels + 1):
        field, level = divmod(index, levels)
        if field < 4:
            tile = (tracers if field < 2 else velocity)[field % 2, level]
        else:
            tile = counts
        first_rows[index : index + 1, :] = tile[0:1, :]
        last_rows[index : index + 1, :] = tile[cols_x - 1 : cols_x, :]
        first = jnp.where(lane == index, tile[:, 0:1], first)
        last = jnp.where(lane == index, tile[:, rows_y - 1 : rows_y], last)
    first_cols[...] = first
    last_cols[...] = last


def level_kernel(
    tracers, velocity, wet, diagonal, thickness, latitude, x_before, x_after, y_before, y_after,
    new_tracers, moved_velocity, surface,
):
    levels, cols_x, rows_y = tracers.shape[1:]
    shape = (cols_x, rows_y)
    lane, sublane = (lanes_of(shape), sublanes_of(shape))
    low_x, high_x = (sublane == 0, sublane == cols_x - 1)
    low_y, high_y = (lane == 0, lane == rows_y - 1)
    before_cols, after_cols = (y_before[...], y_after[...])

    def neighbours(tile, index):
        return (
            jnp.where(high_x, x_after[index : index + 1, :], pltpu.roll(tile, cols_x - 1, 0)),
            jnp.where(low_x, x_before[index : index + 1, :], pltpu.roll(tile, 1, 0)),
            jnp.where(high_y, after_cols[:, index : index + 1], pltpu.roll(tile, rows_y - 1, 1)),
            jnp.where(low_y, before_cols[:, index : index + 1], pltpu.roll(tile, 1, 1)),
        )

    counts = wet[...].astype(jnp.float32)
    around = neighbours(counts, 4 * levels)
    shared = [jnp.minimum(counts, other) for other in around]
    both_x = jnp.minimum(shared[0], shared[1])
    both_y = jnp.minimum(shared[2], shared[3])
    coriolis = jnp.broadcast_to(latitude[...], shape)
    zero = jnp.zeros(shape, jnp.float32)
    difference_x, difference_y, flow_x, flow_y = (zero, zero, zero, zero)
    for level in range(levels):
        here = counts > level
        open_to = [other > level for other in shared]
        wet_around = [other > level for other in around]
        weight = thickness[level]
        heat, salt = (tracers[0, level], tracers[1, level])
        zonal, merid = (velocity[0, level], velocity[1, level])
        heat_around = neighbours(heat, level)
        salt_around = neighbours(salt, levels + level)

        def laplacian(tile, others):
            total = zero
            for other, passable in zip(others, open_to):
                total = total + jnp.where(passable, other - tile, 0.0)
            return total

        loads = [
            jnp.where(is_wet, SALINITY_BETA * s - HEAT_ALPHA * t, 0.0)
            for is_wet, s, t in zip(wet_around, salt_around, heat_around)
        ]
        difference_x = difference_x + weight * (loads[0] - loads[1])
        difference_y = difference_y + weight * (loads[2] - loads[3])
        gradient_x = jnp.where(both_x > level, difference_x * 0.5, 0.0)
        gradient_y = jnp.where(both_y > level, difference_y * 0.5, 0.0)
        diffusivity = TIME_INCREMENT * KAPPA_SPREAD
        new_tracers[0, level] = heat + diffusivity * laplacian(heat, heat_around)
        new_tracers[1, level] = salt + diffusivity * laplacian(salt, salt_around)
        spread_x = laplacian(zonal, neighbours(zonal, 2 * levels + level))
        spread_y = laplacian(merid, neighbours(merid, 3 * levels + level))
        zonal_rate = coriolis * merid - gradient_x + VISCOSITY * spread_x
        merid_rate = -coriolis * zonal - gradient_y + VISCOSITY * spread_y
        next_zonal = zonal + jnp.where(here, TIME_INCREMENT * zonal_rate, 0.0)
        next_merid = merid + jnp.where(here, TIME_INCREMENT * merid_rate, 0.0)
        moved_velocity[0, level] = next_zonal
        moved_velocity[1, level] = next_merid
        flow_x = flow_x + jnp.where(here, weight * next_zonal, 0.0)
        flow_y = flow_y + jnp.where(here, weight * next_merid, 0.0)
    row_start = pl.multiple_of(lax.axis_index("by") * rows_y, rows_y)
    ocean = jnp.where(counts > 0, 1.0, 0.0)
    own_diagonal = diagonal[:, pl.ds(row_start, rows_y)]

    def place(target):
        surface[target, 0] = flow_x
        surface[target, 1] = flow_y
        surface[target, 2] = ocean
        surface[target, 3] = own_diagonal

    pl.loop(0, surface.shape[0], unroll=8)(place)


def solve_kernel(
    blocks_x, blocks_y, gathered, moved_velocity, wet,
    new_velocity, pressure,
    inverse, residual, smooth_0, smooth_1, smooth_2, image_0, image_1, direction_1,
):
    cols_x, rows_y = gathered.shape[2:]
    levels = moved_velocity.shape[1]
    shape = (cols_x, rows_y)
    lane, sublane = (lanes_of(shape), sublanes_of(shape))
    low_x, high_x = (sublane == 0, sublane == cols_x - 1)
    low_y, high_y = (lane == 0, lane == rows_y - 1)
    zero = jnp.zeros(shape, jnp.float32)

    def each_row(step, carry):
        if blocks_x <= 8:
            for row in range(blocks_x):
                carry = step(row, carry)
            return carry
        return lax.fori_loop(0, blocks_x, step, carry)

    def guarded(load, row, column):
        if isinstance(row, int):
            return load(row * blocks_y + column) if 0 <= row < blocks_x else zero
        inside = jnp.logical_and(row >= 0, row < blocks_x)
        return load(jnp.clip(row, 0, blocks_x - 1) * blocks_y + column) * inside.astype(jnp.float32)

    def after_x(load, tile, row, column):
        other = guarded(load, row + 1, column)
        return jnp.where(high_x, pltpu.roll(other, cols_x - 1, 0), pltpu.roll(tile, cols_x - 1, 0))

    def before_x(load, tile, row, column):
        other = guarded(load, row - 1, column)
        return jnp.where(low_x, pltpu.roll(other, 1, 0), pltpu.roll(tile, 1, 0))

    def along_y(tiles):
        ahead = [pltpu.roll(tile, rows_y - 1, 1) for tile in tiles] + [zero]
        behind = [zero] + [pltpu.roll(tile, 1, 1) for tile in tiles]
        after = [jnp.where(high_y, ahead[c + 1], ahead[c]) for c in range(blocks_y)]
        before = [jnp.where(low_y, behind[c], behind[c + 1]) for c in range(blocks_y)]
        return after, before

    def smoothed_by(inv, tile):
        first = inv * tile
        near = jnp.where(high_x, 0.0, pltpu.roll(first, cols_x - 1, 0))
        near = near + jnp.where(low_x, 0.0, pltpu.roll(first, 1, 0))
        near = near + jnp.where(high_y, 0.0, pltpu.roll(first, rows_y - 1, 1))
        near = near + jnp.where(low_y, 0.0, pltpu.roll(first, 1, 1))
        return inv * (tile + near)

    def total(values):
        return jnp.sum(values, axis=(0, 1), keepdims=True)

    def start(row, carry):
        flow_y = [gathered[row * blocks_y + c, 1] for c in range(blocks_y)]
        after, before = along_y(flow_y)
        for column in range(blocks_y):
            index = row * blocks_y + column
            flow = gathered[index, 0]
            load = lambda i: gathered[i, 0]
            slope = after_x(load, flow, row, column) - before_x(load, flow, row, column)
            ocean = gathered[index, 2]
            forcing = ocean * ((slope + (after[column] - before[column])) * 0.5)
            inv = ocean / (4.0 + gathered[index, 3])
            inverse[index] = inv
            residual[index] = forcing
            smooth_0[index] = smoothed_by(inv, forcing)
        return carry

    def operate(smooth, image):
        def step(row, carry):
            inner, curvature = carry
            tiles = [smooth[row * blocks_y + c] for c in range(blocks_y)]
            after, before = along_y(tiles)
            for column in range(blocks_y):
                index = row * blocks_y + column
                tile = tiles[column]
                load = lambda i: smooth[i]
                near = after_x(load, tile, row, column) + before_x(load, tile, row, column)
                near = near + after[column] + before[column]
                centre = 4.0 + gathered[index, 3]
                result = gathered[index, 2] * (centre * tile - near)
                if image is not None:
                    image[index] = result
                inner = inner + residual[index] * tile
                curvature = curvature + tile * result
            return inner, curvature

        inner, curvature = each_row(step, (zero, zero))
        return total(inner), total(curvature)

    each_row(start, 0)
    inner_0, curvature_0 = operate(smooth_0, image_0)
    step_0 = inner_0 / curvature_0

    def advance_0(row, carry):
        for column in range(blocks_y):
            index = row * blocks_y + column
            left = residual[index] - step_0 * image_0[index]
            residual[index] = left
            smooth_1[index] = smoothed_by(inverse[index], left)
        return carry

    each_row(advance_0, 0)
    inner_1, curvature_1 = operate(smooth_1, image_1)
    turn_1 = inner_1 / inner_0
    step_1 = inner_1 / (curvature_1 - turn_1 * inner_1 / step_0)

    def advance_1(row, carry):
        for column in range(blocks_y):
            index = row * blocks_y + column
            direction_1[index] = smooth_1[index] + turn_1 * smooth_0[index]
            image = image_1[index] + turn_1 * image_0[index]
            left = residual[index] - step_1 * image
            residual[index] = left
            smooth_2[index] = smoothed_by(inverse[index], left)
        return carry

    each_row(advance_1, 0)
    inner_2, curvature_2 = operate(smooth_2, None)
    turn_2 = inner_2 / inner_1
    step_2 = inner_2 / (curvature_2 - turn_2 * inner_2 / step_1)

    def iterate(index):
        previous = direction_1[index]
        result = step_0 * smooth_0[index] + step_1 * previous
        return result + step_2 * (smooth_2[index] + turn_2 * previous)

    own_x, own_y = (lax.axis_index("bx"), lax.axis_index("by"))

    def block(shift_x, shift_y):
        row, column = (own_x + shift_x, own_y + shift_y)
        inside = (row >= 0) & (row < blocks_x) & (column >= 0) & (column < blocks_y)
        row, column = (jnp.clip(row, 0, blocks_x - 1), jnp.clip(column, 0, blocks_y - 1))
        return jnp.where(inside, iterate(row * blocks_y + column), 0.0)

    own = iterate(own_x * blocks_y + own_y)
    pressure[...] = own
    upper = jnp.where(high_x, pltpu.roll(block(1, 0), cols_x - 1, 0), pltpu.roll(own, cols_x - 1, 0))
    lower = jnp.where(low_x, pltpu.roll(block(-1, 0), 1, 0), pltpu.roll(own, 1, 0))
    slope_x = GRAVITY * ((upper - lower) * 0.5)
    upper = jnp.where(high_y, pltpu.roll(block(0, 1), rows_y - 1, 1), pltpu.roll(own, rows_y - 1, 1))
    lower = jnp.where(low_y, pltpu.roll(block(0, -1), 1, 1), pltpu.roll(own, 1, 1))
    slope_y = GRAVITY * ((upper - lower) * 0.5)
    counts = wet[...]
    for level in range(levels):
        here = counts > level
        new_velocity[0, level] = moved_velocity[0, level] - jnp.where(here, slope_x, 0.0)
        new_velocity[1, level] = moved_velocity[1, level] - jnp.where(here, slope_y, 0.0)


def latitude_rate(positions, total_rows):
    return 1.5 * jnp.sin(math.pi * ((positions + 0.5) / total_rows - 0.5))


def body(tracers, velocity, wet_levels, thickness, diagonal):
    levels = tracers.shape[1]
    cols_x, rows_y = wet_levels.shape
    blocks_x, blocks_y = (lax.axis_size("bx"), lax.axis_size("by"))
    blocks = blocks_x * blocks_y
    shape = (cols_x, rows_y)
    rim_rows = 4 * levels + 1

    def like(*dims):
        return jax.ShapeDtypeStruct(dims, jnp.float32)

    first_rows, last_rows, first_cols, last_cols = pl.pallas_call(
        pack_rims,
        out_shape=[like(rim_rows, rows_y)] * 2 + [like(*shape)] * 2,
        in_specs=[VMEM] * 3,
        out_specs=[VMEM] * 4,
    )(tracers, velocity, wet_levels)

    def neighbours_of(axis, first, last):
        up = [(i, i + 1) for i in range(lax.axis_size(axis) - 1)]
        down = [(j, i) for i, j in up]
        return lax.ppermute(last, axis, up), lax.ppermute(first, axis, down)

    y_before, y_after = neighbours_of("by", first_cols, last_cols)
    x_before, x_after = neighbours_of("bx", first_rows, last_rows)
    positions = (lax.axis_index("by") * rows_y + jnp.arange(rows_y, dtype=jnp.int32)).astype(jnp.float32)
    latitude = latitude_rate(positions, blocks_y * rows_y)[None]

    new_tracers, moved_velocity, surface = pl.pallas_call(
        level_kernel,
        out_shape=[like(*tracers.shape), like(*velocity.shape), like(blocks, 4, *shape)],
        in_specs=[VMEM] * 4 + [SMEM] + [VMEM] * 5,
        out_specs=[VMEM] * 3,
    )(
        tracers, velocity, wet_levels, diagonal, thickness, latitude,
        x_before, x_after, y_before, y_after,
    )
    gathered = lax.all_to_all(surface, ("bx", "by"), split_axis=0, concat_axis=0, tiled=True)

    def solve(*refs):
        solve_kernel(blocks_x, blocks_y, *refs)

    new_velocity, pressure = pl.pallas_call(
        solve,
        out_shape=[like(*velocity.shape), like(*shape)],
        in_specs=[VMEM] * 3,
        out_specs=[VMEM] * 2,
        scratch_shapes=[pltpu.VMEM((blocks, *shape), jnp.float32)] * 8,
        compiler_params=pltpu.CompilerParams(vmem_limit_bytes=(4 + 52 * blocks // 1024) * 2**20),
    )(gathered, moved_velocity, wet_levels)
    return new_tracers, new_velocity, pressure


def solution(mesh):
    placed = (
        P(None, None, "bx", "by"),
        P(None, None, "bx", "by"),
        P("bx", "by"),
        P(),
        P("bx", None),
    )
    return jax.shard_map(
        body,
        mesh=mesh,
        in_specs=placed,
        out_specs=(P(None, None, "bx", "by"), P(None, None, "bx", "by"), P("bx", "by")),
        check_vma=False,
    )
```

```python
import math

import jax
import jax.numpy as jnp
from jax import lax
from jax.experimental import pallas as pl
from jax.experimental.pallas import tpu as pltpu
from jax.sharding import PartitionSpec as P

ITERS = 3

HEAT_ALPHA = 0.5
SALINITY_BETA = 0.8
KAPPA_SPREAD = 0.15
VISCOSITY = 0.1
TIME_INCREMENT = 0.2
GRAVITY = 1.0

VMEM = pl.BlockSpec(memory_space=pltpu.VMEM)
SMEM = pl.BlockSpec(memory_space=pltpu.SMEM)


def lanes_of(shape):
    return lax.broadcasted_iota(jnp.int32, shape, 1)


def sublanes_of(shape):
    return lax.broadcasted_iota(jnp.int32, shape, 0)


def pack_rims(tracers, velocity, wet, rows_a, rows_b, cols_a, cols_b):
    levels, cols_x, rows_y = tracers.shape[1:]
    even_x, even_y = (lax.axis_index("bx") % 2 == 0, lax.axis_index("by") % 2 == 0)
    lane = lanes_of((cols_x, rows_y))
    counts = wet[...].astype(jnp.float32)
    first, last = jnp.zeros_like(counts), jnp.zeros_like(counts)
    for index in range(4 * levels + 1):
        field, level = divmod(index, levels)
        if field < 4:
            tile = (tracers if field < 2 else velocity)[field % 2, level]
        else:
            tile = counts
        top, bottom = (tile[0:1, :], tile[cols_x - 1 : cols_x, :])
        rows_a[index : index + 1, :] = jnp.where(even_x, bottom, top)
        rows_b[index : index + 1, :] = jnp.where(even_x, top, bottom)
        first = jnp.where(lane == index, tile[:, 0:1], first)
        last = jnp.where(lane == index, tile[:, rows_y - 1 : rows_y], last)
    cols_a[...] = jnp.where(even_y, last, first)
    cols_b[...] = jnp.where(even_y, first, last)


def level_kernel(
    tracers, velocity, wet, diagonal, thickness, latitude, rows_a, rows_b, cols_a, cols_b,
    new_tracers, moved_velocity, surface,
):
    levels, cols_x, rows_y = tracers.shape[1:]
    shape = (cols_x, rows_y)
    lane, sublane = (lanes_of(shape), sublanes_of(shape))
    low_x, high_x = (sublane == 0, sublane == cols_x - 1)
    low_y, high_y = (lane == 0, lane == rows_y - 1)
    even_x, even_y = (lax.axis_index("bx") % 2 == 0, lax.axis_index("by") % 2 == 0)
    after_cols = jnp.where(even_y, cols_a[...], cols_b[...])
    before_cols = jnp.where(even_y, cols_b[...], cols_a[...])

    def neighbours(tile, index):
        row_a, row_b = (rows_a[index : index + 1, :], rows_b[index : index + 1, :])
        after_row, before_row = (jnp.where(even_x, row_a, row_b), jnp.where(even_x, row_b, row_a))
        return (
            jnp.where(high_x, after_row, pltpu.roll(tile, cols_x - 1, 0)),
            jnp.where(low_x, before_row, pltpu.roll(tile, 1, 0)),
            jnp.where(high_y, after_cols[:, index : index + 1], pltpu.roll(tile, rows_y - 1, 1)),
            jnp.where(low_y, before_cols[:, index : index + 1], pltpu.roll(tile, 1, 1)),
        )

    counts = wet[...].astype(jnp.float32)
    around = neighbours(counts, 4 * levels)
    shared = [jnp.minimum(counts, other) for other in around]
    both_x = jnp.minimum(shared[0], shared[1])
    both_y = jnp.minimum(shared[2], shared[3])
    coriolis = jnp.broadcast_to(latitude[...], shape)
    zero = jnp.zeros(shape, jnp.float32)
    difference_x, difference_y, flow_x, flow_y = (zero, zero, zero, zero)
    for level in range(levels):
        here = counts > level
        open_to = [other > level for other in shared]
        wet_around = [other > level for other in around]
        weight = thickness[level]
        heat, salt = (tracers[0, level], tracers[1, level])
        zonal, merid = (velocity[0, level], velocity[1, level])
        heat_around = neighbours(heat, level)
        salt_around = neighbours(salt, levels + level)

        def laplacian(tile, others):
            total = zero
            for other, passable in zip(others, open_to):
                total = total + jnp.where(passable, other - tile, 0.0)
            return total

        loads = [
            jnp.where(is_wet, SALINITY_BETA * s - HEAT_ALPHA * t, 0.0)
            for is_wet, s, t in zip(wet_around, salt_around, heat_around)
        ]
        difference_x = difference_x + weight * (loads[0] - loads[1])
        difference_y = difference_y + weight * (loads[2] - loads[3])
        gradient_x = jnp.where(both_x > level, difference_x * 0.5, 0.0)
        gradient_y = jnp.where(both_y > level, difference_y * 0.5, 0.0)
        diffusivity = TIME_INCREMENT * KAPPA_SPREAD
        new_tracers[0, level] = heat + diffusivity * laplacian(heat, heat_around)
        new_tracers[1, level] = salt + diffusivity * laplacian(salt, salt_around)
        spread_x = laplacian(zonal, neighbours(zonal, 2 * levels + level))
        spread_y = laplacian(merid, neighbours(merid, 3 * levels + level))
        zonal_rate = coriolis * merid - gradient_x + VISCOSITY * spread_x
        merid_rate = -coriolis * zonal - gradient_y + VISCOSITY * spread_y
        next_zonal = zonal + jnp.where(here, TIME_INCREMENT * zonal_rate, 0.0)
        next_merid = merid + jnp.where(here, TIME_INCREMENT * merid_rate, 0.0)
        moved_velocity[0, level] = next_zonal
        moved_velocity[1, level] = next_merid
        flow_x = flow_x + jnp.where(here, weight * next_zonal, 0.0)
        flow_y = flow_y + jnp.where(here, weight * next_merid, 0.0)
    row_start = pl.multiple_of(lax.axis_index("by") * rows_y, rows_y)
    inverse = jnp.where(counts > 0, 1.0, 0.0) / (4.0 + diagonal[:, pl.ds(row_start, rows_y)])
    ahead = jnp.where(high_x, 0.0, pltpu.roll(flow_x, cols_x - 1, 0))
    behind = jnp.where(low_x, 0.0, pltpu.roll(flow_x, 1, 0))
    slope = ahead - behind
    ahead = jnp.where(high_y, 0.0, pltpu.roll(flow_y, rows_y - 1, 1))
    behind = jnp.where(low_y, 0.0, pltpu.roll(flow_y, 1, 1))
    inner = (slope + (ahead - behind)) * 0.5
    edge_x = flow_x * 0.5
    edge_y = flow_y * 0.5
    first = jnp.where(lane == sublane, edge_y[:, 0:1], 0.0)
    last = jnp.where(lane == sublane + cols_x, edge_y[:, rows_y - 1 : rows_y], 0.0)
    corner = jnp.sum(first + last, axis=0, keepdims=True)

    def place(target):
        surface[target, 0:cols_x, 0, :] = inner
        surface[target, cols_x : 2 * cols_x, 0, :] = inverse
        surface[target, 2 * cols_x : 2 * cols_x + 1, 0, :] = edge_x[0:1, :]
        surface[target, 2 * cols_x + 1 : 2 * cols_x + 2, 0, :] = edge_x[cols_x - 1 : cols_x, :]
        surface[target, 2 * cols_x + 2 : 2 * cols_x + 3, 0, :] = corner

    pl.loop(0, surface.shape[0], unroll=8)(place)


def solve_kernel(
    blocks_x, blocks_y, gathered, moved_velocity, wet,
    new_velocity, pressure,
    residual, lifted_0, lifted_1, smooth_0, smooth_1, smooth_2, image_0, direction_1,
):
    levels, cols_x, rows_y = moved_velocity.shape[1:]
    shape = (cols_x, rows_y)
    lane, sublane = (lanes_of(shape), sublanes_of(shape))
    low_x, high_x = (sublane == 0, sublane == cols_x - 1)
    low_y, high_y = (lane == 0, lane == rows_y - 1)
    zero = jnp.zeros(shape, jnp.float32)

    def each_row(step, carry):
        if blocks_x <= 8:
            for row in range(blocks_x):
                carry = step(row, carry)
            return carry
        return lax.fori_loop(0, blocks_x, step, carry)

    def guarded(load, row, column):
        if isinstance(row, int):
            return load(row * blocks_y + column) if 0 <= row < blocks_x else 0.0
        inside = jnp.logical_and(row >= 0, row < blocks_x)
        return load(jnp.clip(row, 0, blocks_x - 1) * blocks_y + column) * inside.astype(jnp.float32)

    def along_x(load, row, column):
        tile = load(row * blocks_y + column)
        other = guarded(lambda i: load(i, slice(0, 1)), row + 1, column)
        after = jnp.where(high_x, other, pltpu.roll(tile, cols_x - 1, 0))
        other = guarded(lambda i: load(i, slice(cols_x - 1, cols_x)), row - 1, column)
        before = jnp.where(low_x, other, pltpu.roll(tile, 1, 0))
        return after + before

    def along_y(tiles):
        ahead = [pltpu.roll(tile, rows_y - 1, 1) for tile in tiles] + [0.0]
        behind = [0.0] + [pltpu.roll(tile, 1, 1) for tile in tiles]
        return [
            jnp.where(high_y, ahead[c + 1], ahead[c]) + jnp.where(low_y, behind[c], behind[c + 1])
            for c in range(blocks_y)
        ]

    def inverse_of(index):
        return gathered[index, cols_x : 2 * cols_x, 0, :]

    def lift(inverse, tile):
        first = inverse * tile
        near = jnp.where(high_x, 0.0, pltpu.roll(first, cols_x - 1, 0))
        near = near + jnp.where(low_x, 0.0, pltpu.roll(first, 1, 0))
        near = near + jnp.where(high_y, 0.0, pltpu.roll(first, rows_y - 1, 1))
        near = near + jnp.where(low_y, 0.0, pltpu.roll(first, 1, 1))
        return tile + near

    def total(values):
        return jnp.sum(values, axis=(0, 1), keepdims=True)

    def edge_rows(which):
        place = 2 * cols_x + which
        return lambda index: gathered[index, place : place + 1, 0, :]

    def edge_column(index, which):
        corner = jnp.where(lane == sublane + which * cols_x, edge_rows(2)(index), 0.0)
        return jnp.sum(corner, axis=1, keepdims=True)

    def start(row, carry):
        for column in range(blocks_y):
            index = row * blocks_y + column
            forcing = gathered[index, 0:cols_x, 0, :]
            forcing = forcing + jnp.where(high_x, guarded(edge_rows(0), row + 1, column), 0.0)
            forcing = forcing - jnp.where(low_x, guarded(edge_rows(1), row - 1, column), 0.0)
            if column + 1 < blocks_y:
                forcing = forcing + jnp.where(high_y, edge_column(index + 1, 0), 0.0)
            if column > 0:
                forcing = forcing - jnp.where(low_y, edge_column(index - 1, 1), 0.0)
            inverse = inverse_of(index)
            lifted = lift(inverse, forcing)
            residual[index] = forcing
            lifted_0[index] = lifted
            smooth_0[index] = inverse * lifted
        return carry

    def operate(lifted, smooth, image):
        def load(index, rows=slice(None)):
            return smooth[index, rows]

        def step(row, carry):
            inner, curvature = carry
            tiles = [smooth[row * blocks_y + c] for c in range(blocks_y)]
            beside = along_y(tiles)
            for column in range(blocks_y):
                index = row * blocks_y + column
                result = lifted[index] - (along_x(load, row, column) + beside[column])
                if image is not None:
                    image[index] = result
                inner = inner + residual[index] * tiles[column]
                curvature = curvature + tiles[column] * result
            return inner, curvature

        inner, curvature = each_row(step, (zero, zero))
        return total(inner), total(curvature)

    each_row(start, 0)
    inner_0, curvature_0 = operate(lifted_0, smooth_0, image_0)
    step_0 = inner_0 / curvature_0

    def advance_0(row, carry):
        for column in range(blocks_y):
            index = row * blocks_y + column
            left = residual[index] - step_0 * image_0[index]
            inverse = inverse_of(index)
            lifted = lift(inverse, left)
            residual[index] = left
            lifted_1[index] = lifted
            smooth_1[index] = inverse * lifted
        return carry

    each_row(advance_0, 0)
    image_1 = lifted_1
    inner_1, curvature_1 = operate(lifted_1, smooth_1, image_1)
    turn_1 = inner_1 / inner_0
    step_1 = inner_1 / (curvature_1 - turn_1 * inner_1 / step_0)

    def advance_1(row, carry):
        for column in range(blocks_y):
            index = row * blocks_y + column
            direction_1[index] = smooth_1[index] + turn_1 * smooth_0[index]
            left = residual[index] - step_1 * (image_1[index] + turn_1 * image_0[index])
            inverse = inverse_of(index)
            lifted = lift(inverse, left)
            residual[index] = left
            lifted_0[index] = lifted
            smooth_2[index] = inverse * lifted
        return carry

    each_row(advance_1, 0)
    inner_2, curvature_2 = operate(lifted_0, smooth_2, None)
    turn_2 = inner_2 / inner_1
    step_2 = inner_2 / (curvature_2 - turn_2 * inner_2 / step_1)

    def iterate(index):
        previous = direction_1[index]
        result = step_0 * smooth_0[index] + step_1 * previous
        return result + step_2 * (smooth_2[index] + turn_2 * previous)

    own_x, own_y = (lax.axis_index("bx"), lax.axis_index("by"))

    def block(shift_x, shift_y):
        row, column = (own_x + shift_x, own_y + shift_y)
        inside = (row >= 0) & (row < blocks_x) & (column >= 0) & (column < blocks_y)
        row, column = (jnp.clip(row, 0, blocks_x - 1), jnp.clip(column, 0, blocks_y - 1))
        return jnp.where(inside, iterate(row * blocks_y + column), 0.0)

    own = iterate(own_x * blocks_y + own_y)
    pressure[...] = own
    upper = jnp.where(high_x, pltpu.roll(block(1, 0), cols_x - 1, 0), pltpu.roll(own, cols_x - 1, 0))
    lower = jnp.where(low_x, pltpu.roll(block(-1, 0), 1, 0), pltpu.roll(own, 1, 0))
    slope_x = GRAVITY * ((upper - lower) * 0.5)
    upper = jnp.where(high_y, pltpu.roll(block(0, 1), rows_y - 1, 1), pltpu.roll(own, rows_y - 1, 1))
    lower = jnp.where(low_y, pltpu.roll(block(0, -1), 1, 1), pltpu.roll(own, 1, 1))
    slope_y = GRAVITY * ((upper - lower) * 0.5)
    counts = wet[...]
    for level in range(levels):
        here = counts > level
        new_velocity[0, level] = moved_velocity[0, level] - jnp.where(here, slope_x, 0.0)
        new_velocity[1, level] = moved_velocity[1, level] - jnp.where(here, slope_y, 0.0)


def latitude_rate(positions, total_rows):
    return 1.5 * jnp.sin(math.pi * ((positions + 0.5) / total_rows - 0.5))


def body(tracers, velocity, wet_levels, thickness, diagonal):
    levels = tracers.shape[1]
    cols_x, rows_y = wet_levels.shape
    blocks_x, blocks_y = (lax.axis_size("bx"), lax.axis_size("by"))
    blocks = blocks_x * blocks_y
    shape = (cols_x, rows_y)
    rim_rows = 4 * levels + 1

    def like(*dims):
        return jax.ShapeDtypeStruct(dims, jnp.float32)

    def held(*dims):
        return pltpu.VMEM(dims, jnp.float32)

    rows_a, rows_b, cols_a, cols_b = pl.pallas_call(
        pack_rims,
        out_shape=[held(rim_rows, rows_y)] * 2 + [held(*shape)] * 2,
        in_specs=[VMEM] * 3,
        out_specs=[VMEM] * 4,
    )(tracers, velocity, wet_levels)

    def exchange(message, axis, first):
        pairs = [(i, i + 1) for i in range(first, lax.axis_size(axis) - 1, 2)]
        return lax.ppermute(message, axis, pairs + [(j, i) for i, j in pairs])

    cols_a, cols_b = (exchange(cols_a, "by", 0), exchange(cols_b, "by", 1))
    rows_a, rows_b = (exchange(rows_a, "bx", 0), exchange(rows_b, "bx", 1))
    positions = (lax.axis_index("by") * rows_y + jnp.arange(rows_y, dtype=jnp.int32)).astype(jnp.float32)
    latitude = latitude_rate(positions, blocks_y * rows_y)[None]

    new_tracers, moved_velocity, surface = pl.pallas_call(
        level_kernel,
        out_shape=[like(*tracers.shape), held(*velocity.shape), held(blocks, 2 * cols_x + 3, 1, rows_y)],
        in_specs=[VMEM] * 4 + [SMEM] + [VMEM] * 5,
        out_specs=[VMEM] * 3,
    )(
        tracers, velocity, wet_levels, diagonal, thickness, latitude,
        rows_a, rows_b, cols_a, cols_b,
    )
    gathered = lax.all_to_all(surface, ("bx", "by"), split_axis=0, concat_axis=0, tiled=True)

    def solve(*refs):
        solve_kernel(blocks_x, blocks_y, *refs)

    new_velocity, pressure = pl.pallas_call(
        solve,
        out_shape=[like(*velocity.shape), like(*shape)],
        in_specs=[VMEM] * 3,
        out_specs=[VMEM] * 2,
        scratch_shapes=[pltpu.VMEM((blocks, *shape), jnp.float32)] * 8,
        compiler_params=pltpu.CompilerParams(vmem_limit_bytes=(4 + 52 * blocks // 1024) * 2**20),
    )(gathered, moved_velocity, wet_levels)
    return new_tracers, new_velocity, pressure


def solution(mesh):
    placed = (
        P(None, None, "bx", "by"),
        P(None, None, "bx", "by"),
        P("bx", "by"),
        P(),
        P("bx", None),
    )
    return jax.shard_map(
        body,
        mesh=mesh,
        in_specs=placed,
        out_specs=(P(None, None, "bx", "by"), P(None, None, "bx", "by"), P("bx", "by")),
        check_vma=False,
    )
```

```python
import math

import jax
import jax.numpy as jnp
from jax import lax
from jax.experimental import pallas as pl
from jax.experimental.pallas import tpu as pltpu
from jax.sharding import PartitionSpec as P

ITERS = 3

HEAT_ALPHA = 0.5
SALINITY_BETA = 0.8
KAPPA_SPREAD = 0.15
VISCOSITY = 0.1
TIME_INCREMENT = 0.2
GRAVITY = 1.0

HELD_SIZE = 2**18

VMEM = pl.BlockSpec(memory_space=pltpu.VMEM)
SMEM = pl.BlockSpec(memory_space=pltpu.SMEM)


def lanes_of(shape):
    return lax.broadcasted_iota(jnp.int32, shape, 1)


def sublanes_of(shape):
    return lax.broadcasted_iota(jnp.int32, shape, 0)


def pack_rims(tracers, velocity, wet, rows_a, rows_b, cols_a, cols_b):
    levels, cols_x, rows_y = tracers.shape[1:]
    even_x, even_y = (lax.axis_index("bx") % 2 == 0, lax.axis_index("by") % 2 == 0)
    lane = lanes_of((cols_x, rows_y))
    counts = wet[...].astype(jnp.float32)
    first, last = jnp.zeros_like(counts), jnp.zeros_like(counts)
    for index in range(4 * levels + 1):
        field, level = divmod(index, levels)
        if field < 4:
            tile = (tracers if field < 2 else velocity)[field % 2, level]
        else:
            tile = counts
        top, bottom = (tile[0:1, :], tile[cols_x - 1 : cols_x, :])
        rows_a[index : index + 1, :] = jnp.where(even_x, bottom, top)
        rows_b[index : index + 1, :] = jnp.where(even_x, top, bottom)
        first = jnp.where(lane == index, tile[:, 0:1], first)
        last = jnp.where(lane == index, tile[:, rows_y - 1 : rows_y], last)
    cols_a[...] = jnp.where(even_y, last, first)
    cols_b[...] = jnp.where(even_y, first, last)


def level_kernel(
    tracers, velocity, wet, diagonal, thickness, latitude, rows_a, rows_b, cols_a, cols_b,
    new_tracers, moved_velocity, surface,
):
    levels, cols_x, rows_y = tracers.shape[1:]
    shape = (cols_x, rows_y)
    lane, sublane = (lanes_of(shape), sublanes_of(shape))
    low_x, high_x = (sublane == 0, sublane == cols_x - 1)
    low_y, high_y = (lane == 0, lane == rows_y - 1)
    even_x, even_y = (lax.axis_index("bx") % 2 == 0, lax.axis_index("by") % 2 == 0)
    after_cols = jnp.where(even_y, cols_a[...], cols_b[...])
    before_cols = jnp.where(even_y, cols_b[...], cols_a[...])

    def neighbours(tile, index):
        row_a, row_b = (rows_a[index : index + 1, :], rows_b[index : index + 1, :])
        after_row, before_row = (jnp.where(even_x, row_a, row_b), jnp.where(even_x, row_b, row_a))
        return (
            jnp.where(high_x, after_row, pltpu.roll(tile, cols_x - 1, 0)),
            jnp.where(low_x, before_row, pltpu.roll(tile, 1, 0)),
            jnp.where(high_y, after_cols[:, index : index + 1], pltpu.roll(tile, rows_y - 1, 1)),
            jnp.where(low_y, before_cols[:, index : index + 1], pltpu.roll(tile, 1, 1)),
        )

    counts = wet[...].astype(jnp.float32)
    around = neighbours(counts, 4 * levels)
    shared = [jnp.minimum(counts, other) for other in around]
    both_x = jnp.minimum(shared[0], shared[1])
    both_y = jnp.minimum(shared[2], shared[3])
    coriolis = jnp.broadcast_to(latitude[...], shape)
    zero = jnp.zeros(shape, jnp.float32)
    difference_x, difference_y, flow_x, flow_y = (zero, zero, zero, zero)
    for level in range(levels):
        here = counts > level
        open_to = [other > level for other in shared]
        wet_around = [other > level for other in around]
        weight = thickness[level]
        heat, salt = (tracers[0, level], tracers[1, level])
        zonal, merid = (velocity[0, level], velocity[1, level])
        heat_around = neighbours(heat, level)
        salt_around = neighbours(salt, levels + level)

        def laplacian(tile, others):
            total = zero
            for other, passable in zip(others, open_to):
                total = total + jnp.where(passable, other - tile, 0.0)
            return total

        loads = [
            jnp.where(is_wet, SALINITY_BETA * s - HEAT_ALPHA * t, 0.0)
            for is_wet, s, t in zip(wet_around, salt_around, heat_around)
        ]
        difference_x = difference_x + weight * (loads[0] - loads[1])
        difference_y = difference_y + weight * (loads[2] - loads[3])
        gradient_x = jnp.where(both_x > level, difference_x * 0.5, 0.0)
        gradient_y = jnp.where(both_y > level, difference_y * 0.5, 0.0)
        diffusivity = TIME_INCREMENT * KAPPA_SPREAD
        new_tracers[0, level] = heat + diffusivity * laplacian(heat, heat_around)
        new_tracers[1, level] = salt + diffusivity * laplacian(salt, salt_around)
        spread_x = laplacian(zonal, neighbours(zonal, 2 * levels + level))
        spread_y = laplacian(merid, neighbours(merid, 3 * levels + level))
        zonal_rate = coriolis * merid - gradient_x + VISCOSITY * spread_x
        merid_rate = -coriolis * zonal - gradient_y + VISCOSITY * spread_y
        next_zonal = zonal + jnp.where(here, TIME_INCREMENT * zonal_rate, 0.0)
        next_merid = merid + jnp.where(here, TIME_INCREMENT * merid_rate, 0.0)
        moved_velocity[0, level] = next_zonal
        moved_velocity[1, level] = next_merid
        flow_x = flow_x + jnp.where(here, weight * next_zonal, 0.0)
        flow_y = flow_y + jnp.where(here, weight * next_merid, 0.0)
    row_start = pl.multiple_of(lax.axis_index("by") * rows_y, rows_y)
    inverse = jnp.where(counts > 0, 1.0, 0.0) / (4.0 + diagonal[:, pl.ds(row_start, rows_y)])
    ahead = jnp.where(high_x, 0.0, pltpu.roll(flow_x, cols_x - 1, 0))
    behind = jnp.where(low_x, 0.0, pltpu.roll(flow_x, 1, 0))
    slope = ahead - behind
    ahead = jnp.where(high_y, 0.0, pltpu.roll(flow_y, rows_y - 1, 1))
    behind = jnp.where(low_y, 0.0, pltpu.roll(flow_y, 1, 1))
    inner = (slope + (ahead - behind)) * 0.5
    edge_x = flow_x * 0.5
    edge_y = flow_y * 0.5
    first = jnp.where(lane == sublane, edge_y[:, 0:1], 0.0)
    last = jnp.where(lane == sublane + cols_x, edge_y[:, rows_y - 1 : rows_y], 0.0)
    corner = jnp.sum(first + last, axis=0, keepdims=True)

    def place(target):
        surface[target, 0:cols_x, 0, :] = inner
        surface[target, cols_x : 2 * cols_x, 0, :] = inverse
        surface[target, 2 * cols_x : 2 * cols_x + 1, 0, :] = edge_x[0:1, :]
        surface[target, 2 * cols_x + 1 : 2 * cols_x + 2, 0, :] = edge_x[cols_x - 1 : cols_x, :]
        surface[target, 2 * cols_x + 2 : 2 * cols_x + 3, 0, :] = corner

    pl.loop(0, surface.shape[0], unroll=8)(place)


def solve_kernel(
    blocks_x, blocks_y, gathered, moved_velocity, wet,
    new_velocity, pressure,
    residual, inverses, lifted_0, lifted_1, smooth_0, smooth_1, smooth_2, image_0, direction_1,
):
    levels, cols_x, rows_y = moved_velocity.shape[1:]
    shape = (cols_x, rows_y)
    lane, sublane = (lanes_of(shape), sublanes_of(shape))
    low_x, high_x = (sublane == 0, sublane == cols_x - 1)
    low_y, high_y = (lane == 0, lane == rows_y - 1)
    zero = jnp.zeros(shape, jnp.float32)

    def each_row(step, carry):
        if blocks_x <= 8:
            for row in range(blocks_x):
                carry = step(row, carry)
            return carry
        return lax.fori_loop(0, blocks_x, step, carry)

    def guarded(load, row, column):
        if isinstance(row, int):
            return load(row * blocks_y + column) if 0 <= row < blocks_x else 0.0
        inside = jnp.logical_and(row >= 0, row < blocks_x)
        return load(jnp.clip(row, 0, blocks_x - 1) * blocks_y + column) * inside.astype(jnp.float32)

    def along_x(load, row, column):
        tile = load(row * blocks_y + column)
        other = guarded(lambda i: load(i, slice(0, 1)), row + 1, column)
        after = jnp.where(high_x, other, pltpu.roll(tile, cols_x - 1, 0))
        other = guarded(lambda i: load(i, slice(cols_x - 1, cols_x)), row - 1, column)
        before = jnp.where(low_x, other, pltpu.roll(tile, 1, 0))
        return after + before

    def along_y(tiles):
        ahead = [pltpu.roll(tile, rows_y - 1, 1) for tile in tiles] + [0.0]
        behind = [0.0] + [pltpu.roll(tile, 1, 1) for tile in tiles]
        return [
            jnp.where(high_y, ahead[c + 1], ahead[c]) + jnp.where(low_y, behind[c], behind[c + 1])
            for c in range(blocks_y)
        ]

    def lift(inverse, tile):
        first = inverse * tile
        near = jnp.where(high_x, 0.0, pltpu.roll(first, cols_x - 1, 0))
        near = near + jnp.where(low_x, 0.0, pltpu.roll(first, 1, 0))
        near = near + jnp.where(high_y, 0.0, pltpu.roll(first, rows_y - 1, 1))
        near = near + jnp.where(low_y, 0.0, pltpu.roll(first, 1, 1))
        return tile + near

    def total(values):
        return jnp.sum(values, axis=(0, 1), keepdims=True)

    def edge_rows(which):
        place = 2 * cols_x + which
        return lambda index: gathered[index, place : place + 1, 0, :]

    def edge_column(index, which):
        corner = jnp.where(lane == sublane + which * cols_x, edge_rows(2)(index), 0.0)
        return jnp.sum(corner, axis=1, keepdims=True)

    def start(row, carry):
        for column in range(blocks_y):
            index = row * blocks_y + column
            forcing = gathered[index, 0:cols_x, 0, :]
            forcing = forcing + jnp.where(high_x, guarded(edge_rows(0), row + 1, column), 0.0)
            forcing = forcing - jnp.where(low_x, guarded(edge_rows(1), row - 1, column), 0.0)
            if column + 1 < blocks_y:
                forcing = forcing + jnp.where(high_y, edge_column(index + 1, 0), 0.0)
            if column > 0:
                forcing = forcing - jnp.where(low_y, edge_column(index - 1, 1), 0.0)
            inverse = gathered[index, cols_x : 2 * cols_x, 0, :]
            lifted = lift(inverse, forcing)
            inverses[index] = inverse
            residual[index] = forcing
            lifted_0[index] = lifted
            smooth_0[index] = inverse * lifted
        return carry

    def operate(lifted, smooth, image):
        def load(index, rows=slice(None)):
            return smooth[index, rows]

        def step(row, carry):
            inner, curvature = carry
            tiles = [smooth[row * blocks_y + c] for c in range(blocks_y)]
            beside = along_y(tiles)
            for column in range(blocks_y):
                index = row * blocks_y + column
                result = lifted[index] - (along_x(load, row, column) + beside[column])
                if image is not None:
                    image[index] = result
                inner = inner + residual[index] * tiles[column]
                curvature = curvature + tiles[column] * result
            return inner, curvature

        inner, curvature = each_row(step, (zero, zero))
        return total(inner), total(curvature)

    each_row(start, 0)
    inner_0, curvature_0 = operate(lifted_0, smooth_0, image_0)
    step_0 = inner_0 / curvature_0

    def advance_0(row, carry):
        for column in range(blocks_y):
            index = row * blocks_y + column
            left = residual[index] - step_0 * image_0[index]
            inverse = inverses[index]
            lifted = lift(inverse, left)
            residual[index] = left
            lifted_1[index] = lifted
            smooth_1[index] = inverse * lifted
        return carry

    each_row(advance_0, 0)
    image_1 = lifted_1
    inner_1, curvature_1 = operate(lifted_1, smooth_1, image_1)
    turn_1 = inner_1 / inner_0
    step_1 = inner_1 / (curvature_1 - turn_1 * inner_1 / step_0)

    def advance_1(row, carry):
        for column in range(blocks_y):
            index = row * blocks_y + column
            direction_1[index] = smooth_1[index] + turn_1 * smooth_0[index]
            left = residual[index] - step_1 * (image_1[index] + turn_1 * image_0[index])
            inverse = inverses[index]
            lifted = lift(inverse, left)
            residual[index] = left
            lifted_0[index] = lifted
            smooth_2[index] = inverse * lifted
        return carry

    each_row(advance_1, 0)
    inner_2, curvature_2 = operate(lifted_0, smooth_2, None)
    turn_2 = inner_2 / inner_1
    step_2 = inner_2 / (curvature_2 - turn_2 * inner_2 / step_1)

    def iterate(index):
        previous = direction_1[index]
        result = step_0 * smooth_0[index] + step_1 * previous
        return result + step_2 * (smooth_2[index] + turn_2 * previous)

    own_x, own_y = (lax.axis_index("bx"), lax.axis_index("by"))

    def block(shift_x, shift_y):
        row, column = (own_x + shift_x, own_y + shift_y)
        inside = (row >= 0) & (row < blocks_x) & (column >= 0) & (column < blocks_y)
        row, column = (jnp.clip(row, 0, blocks_x - 1), jnp.clip(column, 0, blocks_y - 1))
        return jnp.where(inside, iterate(row * blocks_y + column), 0.0)

    own = iterate(own_x * blocks_y + own_y)
    pressure[...] = own
    upper = jnp.where(high_x, pltpu.roll(block(1, 0), cols_x - 1, 0), pltpu.roll(own, cols_x - 1, 0))
    lower = jnp.where(low_x, pltpu.roll(block(-1, 0), 1, 0), pltpu.roll(own, 1, 0))
    slope_x = GRAVITY * ((upper - lower) * 0.5)
    upper = jnp.where(high_y, pltpu.roll(block(0, 1), rows_y - 1, 1), pltpu.roll(own, rows_y - 1, 1))
    lower = jnp.where(low_y, pltpu.roll(block(0, -1), 1, 1), pltpu.roll(own, 1, 1))
    slope_y = GRAVITY * ((upper - lower) * 0.5)
    counts = wet[...]
    for level in range(levels):
        here = counts > level
        new_velocity[0, level] = moved_velocity[0, level] - jnp.where(here, slope_x, 0.0)
        new_velocity[1, level] = moved_velocity[1, level] - jnp.where(here, slope_y, 0.0)


def latitude_rate(positions, total_rows):
    return 1.5 * jnp.sin(math.pi * ((positions + 0.5) / total_rows - 0.5))


def body(tracers, velocity, wet_levels, thickness, diagonal):
    levels = tracers.shape[1]
    cols_x, rows_y = wet_levels.shape
    blocks_x, blocks_y = (lax.axis_size("bx"), lax.axis_size("by"))
    blocks = blocks_x * blocks_y
    shape = (cols_x, rows_y)
    rim_rows = 4 * levels + 1

    def like(*dims):
        return jax.ShapeDtypeStruct(dims, jnp.float32)

    def held(*dims):
        return pltpu.VMEM(dims, jnp.float32) if math.prod(dims) <= HELD_SIZE else like(*dims)

    def kept(array):
        if array.size > HELD_SIZE:
            return array
        return pltpu.with_memory_space_constraint(array, pltpu.VMEM)

    tracers, velocity, wet_levels = (kept(tracers), kept(velocity), kept(wet_levels))
    rows_a, rows_b, cols_a, cols_b = pl.pallas_call(
        pack_rims,
        out_shape=[held(rim_rows, rows_y)] * 2 + [held(*shape)] * 2,
        in_specs=[VMEM] * 3,
        out_specs=[VMEM] * 4,
    )(tracers, velocity, wet_levels)

    def exchange(message, axis, first):
        pairs = [(i, i + 1) for i in range(first, lax.axis_size(axis) - 1, 2)]
        return lax.ppermute(message, axis, pairs + [(j, i) for i, j in pairs])

    rows_b, rows_a = (exchange(rows_b, "bx", 1), exchange(rows_a, "bx", 0))
    cols_b, cols_a = (exchange(cols_b, "by", 1), exchange(cols_a, "by", 0))
    positions = (lax.axis_index("by") * rows_y + jnp.arange(rows_y, dtype=jnp.int32)).astype(jnp.float32)
    latitude = latitude_rate(positions, blocks_y * rows_y)[None]

    new_tracers, moved_velocity, surface = pl.pallas_call(
        level_kernel,
        out_shape=[like(*tracers.shape), held(*velocity.shape), held(blocks, 2 * cols_x + 3, 1, rows_y)],
        in_specs=[VMEM] * 4 + [SMEM] + [VMEM] * 5,
        out_specs=[VMEM] * 3,
    )(
        tracers, velocity, wet_levels, kept(diagonal), thickness, kept(latitude),
        kept(rows_a), kept(rows_b), kept(cols_a), kept(cols_b),
    )
    gathered = lax.all_to_all(surface, ("bx", "by"), split_axis=0, concat_axis=0, tiled=True)

    def solve(*refs):
        solve_kernel(blocks_x, blocks_y, *refs)

    new_velocity, pressure = pl.pallas_call(
        solve,
        out_shape=[like(*velocity.shape), like(*shape)],
        in_specs=[VMEM] * 3,
        out_specs=[VMEM] * 2,
        scratch_shapes=[pltpu.VMEM((blocks, *shape), jnp.float32)] * 9,
        compiler_params=pltpu.CompilerParams(vmem_limit_bytes=(4 + 52 * blocks // 1024) * 2**20),
    )(kept(gathered), kept(moved_velocity), wet_levels)
    return new_tracers, new_velocity, pressure


def solution(mesh):
    placed = (
        P(None, None, "bx", "by"),
        P(None, None, "bx", "by"),
        P("bx", "by"),
        P(),
        P("bx", None),
    )
    return jax.shard_map(
        body,
        mesh=mesh,
        in_specs=placed,
        out_specs=(P(None, None, "bx", "by"), P(None, None, "bx", "by"), P("bx", "by")),
        check_vma=False,
    )
```

```python
import math

import jax
import jax.numpy as jnp
from jax import lax
from jax.experimental import pallas as pl
from jax.experimental.pallas import tpu as pltpu
from jax.sharding import PartitionSpec as P

ITERS = 3

HEAT_ALPHA = 0.5
SALINITY_BETA = 0.8
KAPPA_SPREAD = 0.15
VISCOSITY = 0.1
TIME_INCREMENT = 0.2
GRAVITY = 1.0

HELD_SIZE = 2**18

VMEM = pl.BlockSpec(memory_space=pltpu.VMEM)
ANY = pl.BlockSpec(memory_space=pl.ANY)
SMEM = pl.BlockSpec(memory_space=pltpu.SMEM)


def lanes_of(shape):
    return lax.broadcasted_iota(jnp.int32, shape, 1)


def sublanes_of(shape):
    return lax.broadcasted_iota(jnp.int32, shape, 0)


def position_x():
    return lax.axis_index("z") * lax.axis_size("core") + lax.axis_index("core")


def pack_rims(
    tracers_in, velocity_in, wet_in, diagonal_in, thickness,
    rows_a, rows_b, cols_a, cols_b, tracers, velocity, wet, diagonal, weights,
    semaphores,
):
    levels, cols_x, rows_y = tracers.shape[1:]
    row_start = pl.multiple_of(lax.axis_index("by") * rows_y, rows_y)
    copies = [
        pltpu.make_async_copy(source, target, semaphores.at[number])
        for number, (source, target) in enumerate((
            (tracers_in, tracers),
            (velocity_in, velocity),
            (wet_in, wet),
            (diagonal_in.at[:, pl.ds(row_start, rows_y)], diagonal),
        ))
    ]
    for copy in copies:
        copy.start()
    for level in range(levels):
        weights[level : level + 1, :] = jnp.full((1, rows_y), thickness[level], jnp.float32)
    even_x, even_y = (lax.axis_index("core") == 0, lax.axis_index("by") % 2 == 0)
    lane = lanes_of((cols_x, rows_y))
    for copy in copies:
        copy.wait()
    counts = wet[...].astype(jnp.float32)
    first, last = jnp.zeros_like(counts), jnp.zeros_like(counts)
    for index in range(4 * levels + 1):
        field, level = divmod(index, levels)
        if field < 4:
            tile = (tracers if field < 2 else velocity)[field % 2, level]
        else:
            tile = counts
        top, bottom = (tile[0:1, :], tile[cols_x - 1 : cols_x, :])
        rows_a[index : index + 1, :] = jnp.where(even_x, bottom, top)
        rows_b[index : index + 1, :] = jnp.where(even_x, top, bottom)
        first = jnp.where(lane == index, tile[:, 0:1], first)
        last = jnp.where(lane == index, tile[:, rows_y - 1 : rows_y], last)
    cols_a[...] = jnp.where(even_y, last, first)
    cols_b[...] = jnp.where(even_y, first, last)


def level_kernel(
    tracers, velocity, wet, diagonal, weights, latitude, rows_a, rows_b, cols_a, cols_b,
    new_tracers, moved_velocity, surface,
    next_tracers, gradients, semaphore,
):
    levels, cols_x, rows_y = tracers.shape[1:]
    shape = (cols_x, rows_y)
    lane, sublane = (lanes_of(shape), sublanes_of(shape))
    low_x, high_x = (sublane == 0, sublane == cols_x - 1)
    low_y, high_y = (lane == 0, lane == rows_y - 1)
    even_x, even_y = (lax.axis_index("core") == 0, lax.axis_index("by") % 2 == 0)
    after_cols = jnp.where(even_y, cols_a[...], cols_b[...])
    before_cols = jnp.where(even_y, cols_b[...], cols_a[...])

    def neighbours(tile, index):
        row_a, row_b = (rows_a[index : index + 1, :], rows_b[index : index + 1, :])
        after_row, before_row = (jnp.where(even_x, row_a, row_b), jnp.where(even_x, row_b, row_a))
        return (
            jnp.where(high_x, after_row, pltpu.roll(tile, cols_x - 1, 0)),
            jnp.where(low_x, before_row, pltpu.roll(tile, 1, 0)),
            jnp.where(high_y, after_cols[:, index : index + 1], pltpu.roll(tile, rows_y - 1, 1)),
            jnp.where(low_y, before_cols[:, index : index + 1], pltpu.roll(tile, 1, 1)),
        )

    counts = wet[...].astype(jnp.float32)
    around = neighbours(counts, 4 * levels)
    shared = [jnp.minimum(counts, other) for other in around]
    both_x = jnp.minimum(shared[0], shared[1])
    both_y = jnp.minimum(shared[2], shared[3])
    zero = jnp.zeros(shape, jnp.float32)

    def laplacian(tile, others, level):
        total = zero
        for other, limit in zip(others, shared):
            total = total + jnp.where(limit > level, other - tile, 0.0)
        return total

    difference_x, difference_y = (zero, zero)
    for level in range(levels):
        weight = weights[level : level + 1, :]
        heat, salt = (tracers[0, level], tracers[1, level])
        heat_around = neighbours(heat, level)
        salt_around = neighbours(salt, levels + level)
        loads = [
            jnp.where(count > level, SALINITY_BETA * s - HEAT_ALPHA * t, 0.0)
            for count, s, t in zip(around, salt_around, heat_around)
        ]
        difference_x = difference_x + weight * (loads[0] - loads[1])
        difference_y = difference_y + weight * (loads[2] - loads[3])
        gradients[0, level] = jnp.where(both_x > level, difference_x * 0.5, 0.0)
        gradients[1, level] = jnp.where(both_y > level, difference_y * 0.5, 0.0)
        diffusivity = TIME_INCREMENT * KAPPA_SPREAD
        next_tracers[0, level] = heat + diffusivity * laplacian(heat, heat_around, level)
        next_tracers[1, level] = salt + diffusivity * laplacian(salt, salt_around, level)
    leaving = pltpu.make_async_copy(next_tracers, new_tracers, semaphore)
    leaving.start()

    coriolis = jnp.broadcast_to(latitude[...], shape)
    flow_x, flow_y = (zero, zero)
    for level in range(levels):
        here = counts > level
        weight = weights[level : level + 1, :]
        zonal, merid = (velocity[0, level], velocity[1, level])
        spread_x = laplacian(zonal, neighbours(zonal, 2 * levels + level), level)
        spread_y = laplacian(merid, neighbours(merid, 3 * levels + level), level)
        zonal_rate = coriolis * merid - gradients[0, level] + VISCOSITY * spread_x
        merid_rate = -coriolis * zonal - gradients[1, level] + VISCOSITY * spread_y
        next_zonal = zonal + jnp.where(here, TIME_INCREMENT * zonal_rate, 0.0)
        next_merid = merid + jnp.where(here, TIME_INCREMENT * merid_rate, 0.0)
        moved_velocity[0, level] = next_zonal
        moved_velocity[1, level] = next_merid
        flow_x = flow_x + jnp.where(here, weight * next_zonal, 0.0)
        flow_y = flow_y + jnp.where(here, weight * next_merid, 0.0)
    inverse = jnp.where(counts > 0, 1.0, 0.0) / (4.0 + diagonal[...])
    ahead = jnp.where(high_x, 0.0, pltpu.roll(flow_x, cols_x - 1, 0))
    behind = jnp.where(low_x, 0.0, pltpu.roll(flow_x, 1, 0))
    slope = ahead - behind
    ahead = jnp.where(high_y, 0.0, pltpu.roll(flow_y, rows_y - 1, 1))
    behind = jnp.where(low_y, 0.0, pltpu.roll(flow_y, 1, 1))
    inner = (slope + (ahead - behind)) * 0.5
    edge_x = flow_x * 0.5
    edge_y = flow_y * 0.5
    first = jnp.where(lane == sublane, edge_y[:, 0:1], 0.0)
    last = jnp.where(lane == sublane + cols_x, edge_y[:, rows_y - 1 : rows_y], 0.0)
    corner = jnp.sum(first + last, axis=0, keepdims=True)

    def place(target):
        surface[target, 0:cols_x, 0, :] = inner
        surface[target, cols_x : 2 * cols_x, 0, :] = inverse
        surface[target, 2 * cols_x : 2 * cols_x + 1, 0, :] = edge_x[0:1, :]
        surface[target, 2 * cols_x + 1 : 2 * cols_x + 2, 0, :] = edge_x[cols_x - 1 : cols_x, :]
        surface[target, 2 * cols_x + 2 : 2 * cols_x + 3, 0, :] = corner

    pl.loop(0, surface.shape[0], unroll=8)(place)
    leaving.wait()


def solve_kernel(
    blocks_x, blocks_y, gathered, swapped, moved_velocity, wet,
    new_velocity, pressure,
    residual, inverses, lifted_0, lifted_1, smooth_0, smooth_1, smooth_2, image_0, direction_1,
):
    levels, cols_x, rows_y = moved_velocity.shape[1:]
    shape = (cols_x, rows_y)
    lane, sublane = (lanes_of(shape), sublanes_of(shape))
    low_x, high_x = (sublane == 0, sublane == cols_x - 1)
    low_y, high_y = (lane == 0, lane == rows_y - 1)
    zero = jnp.zeros(shape, jnp.float32)

    def each_row(step, carry):
        if blocks_x <= 8:
            for row in range(blocks_x):
                carry = step(row, carry)
            return carry
        return lax.fori_loop(0, blocks_x, step, carry)

    def guarded(load, row, column):
        if isinstance(row, int):
            return load(row * blocks_y + column) if 0 <= row < blocks_x else 0.0
        inside = jnp.logical_and(row >= 0, row < blocks_x)
        return load(jnp.clip(row, 0, blocks_x - 1) * blocks_y + column) * inside.astype(jnp.float32)

    def along_x(load, row, column):
        tile = load(row * blocks_y + column)
        other = guarded(lambda i: load(i, slice(0, 1)), row + 1, column)
        after = jnp.where(high_x, other, pltpu.roll(tile, cols_x - 1, 0))
        other = guarded(lambda i: load(i, slice(cols_x - 1, cols_x)), row - 1, column)
        before = jnp.where(low_x, other, pltpu.roll(tile, 1, 0))
        return after + before

    def along_y(tiles):
        ahead = [pltpu.roll(tile, rows_y - 1, 1) for tile in tiles] + [0.0]
        behind = [0.0] + [pltpu.roll(tile, 1, 1) for tile in tiles]
        return [
            jnp.where(high_y, ahead[c + 1], ahead[c]) + jnp.where(low_y, behind[c], behind[c + 1])
            for c in range(blocks_y)
        ]

    def lift(inverse, tile):
        first = inverse * tile
        near = jnp.where(high_x, 0.0, pltpu.roll(first, cols_x - 1, 0))
        near = near + jnp.where(low_x, 0.0, pltpu.roll(first, 1, 0))
        near = near + jnp.where(high_y, 0.0, pltpu.roll(first, rows_y - 1, 1))
        near = near + jnp.where(low_y, 0.0, pltpu.roll(first, 1, 1))
        return tile + near

    def total(values):
        return jnp.sum(values, axis=(0, 1), keepdims=True)

    height = 2 * cols_x + 3

    def start_from(by_core):
        def rows_of(row, column, first, count):
            if isinstance(row, int):
                place = (row // 2 * blocks_y + column) * height + first
                return by_core[row % 2][place : place + count, :]
            place = (row // 2 * blocks_y + column) * height + first
            found = [blocks[pl.ds(place, count), :] for blocks in by_core]
            return jnp.where(row % 2 == 0, *found)

        def edge_row(which, row, column):
            if isinstance(row, int):
                inside = 0 <= row < blocks_x
                return rows_of(row, column, 2 * cols_x + which, 1) if inside else 0.0
            inside = jnp.logical_and(row >= 0, row < blocks_x).astype(jnp.float32)
            row = jnp.clip(row, 0, blocks_x - 1)
            return rows_of(row, column, 2 * cols_x + which, 1) * inside

        def step(row, carry):
            corners = [rows_of(row, c, 2 * cols_x + 2, 1) for c in range(blocks_y)]
            filler = [jnp.zeros((1, rows_y), jnp.float32)] * (-blocks_y % 8)
            corners = jnp.transpose(jnp.concatenate(corners + filler, axis=0))
            for column in range(blocks_y):
                index = row * blocks_y + column
                forcing = rows_of(row, column, 0, cols_x)
                forcing = forcing + jnp.where(high_x, edge_row(0, row + 1, column), 0.0)
                forcing = forcing - jnp.where(low_x, edge_row(1, row - 1, column), 0.0)
                if column + 1 < blocks_y:
                    beyond = corners[0:cols_x, column + 1 : column + 2]
                    forcing = forcing + jnp.where(high_y, beyond, 0.0)
                if column > 0:
                    beyond = corners[cols_x : 2 * cols_x, column - 1 : column]
                    forcing = forcing - jnp.where(low_y, beyond, 0.0)
                inverse = rows_of(row, column, cols_x, cols_x)
                lifted = lift(inverse, forcing)
                inverses[index] = inverse
                residual[index] = forcing
                lifted_0[index] = lifted
                smooth_0[index] = inverse * lifted
            return carry

        each_row(step, 0)

    def operate(lifted, smooth, image):
        def load(index, rows=slice(None)):
            return smooth[index, rows]

        def step(row, carry):
            inner, curvature = carry
            tiles = [smooth[row * blocks_y + c] for c in range(blocks_y)]
            beside = along_y(tiles)
            for column in range(blocks_y):
                index = row * blocks_y + column
                result = lifted[index] - (along_x(load, row, column) + beside[column])
                if image is not None:
                    image[index] = result
                inner = inner + residual[index] * tiles[column]
                curvature = curvature + tiles[column] * result
            return inner, curvature

        inner, curvature = each_row(step, (zero, zero))
        return total(inner), total(curvature)

    own_core = lax.axis_index("core")
    pl.when(own_core == 0)(lambda: start_from((gathered, swapped)))
    pl.when(own_core == 1)(lambda: start_from((swapped, gathered)))
    inner_0, curvature_0 = operate(lifted_0, smooth_0, image_0)
    step_0 = inner_0 / curvature_0

    def advance_0(row, carry):
        for column in range(blocks_y):
            index = row * blocks_y + column
            left = residual[index] - step_0 * image_0[index]
            inverse = inverses[index]
            lifted = lift(inverse, left)
            residual[index] = left
            lifted_1[index] = lifted
            smooth_1[index] = inverse * lifted
        return carry

    each_row(advance_0, 0)
    image_1 = lifted_1
    inner_1, curvature_1 = operate(lifted_1, smooth_1, image_1)
    turn_1 = inner_1 / inner_0
    step_1 = inner_1 / (curvature_1 - turn_1 * inner_1 / step_0)

    def advance_1(row, carry):
        for column in range(blocks_y):
            index = row * blocks_y + column
            direction_1[index] = smooth_1[index] + turn_1 * smooth_0[index]
            left = residual[index] - step_1 * (image_1[index] + turn_1 * image_0[index])
            inverse = inverses[index]
            lifted = lift(inverse, left)
            residual[index] = left
            lifted_0[index] = lifted
            smooth_2[index] = inverse * lifted
        return carry

    each_row(advance_1, 0)
    inner_2, curvature_2 = operate(lifted_0, smooth_2, None)
    turn_2 = inner_2 / inner_1
    step_2 = inner_2 / (curvature_2 - turn_2 * inner_2 / step_1)

    def iterate(index):
        previous = direction_1[index]
        result = step_0 * smooth_0[index] + step_1 * previous
        return result + step_2 * (smooth_2[index] + turn_2 * previous)

    own_x, own_y = (position_x(), lax.axis_index("by"))

    def block(shift_x, shift_y):
        row, column = (own_x + shift_x, own_y + shift_y)
        inside = (row >= 0) & (row < blocks_x) & (column >= 0) & (column < blocks_y)
        row, column = (jnp.clip(row, 0, blocks_x - 1), jnp.clip(column, 0, blocks_y - 1))
        return jnp.where(inside, iterate(row * blocks_y + column), 0.0)

    own = iterate(own_x * blocks_y + own_y)
    pressure[...] = own
    upper = jnp.where(high_x, pltpu.roll(block(1, 0), cols_x - 1, 0), pltpu.roll(own, cols_x - 1, 0))
    lower = jnp.where(low_x, pltpu.roll(block(-1, 0), 1, 0), pltpu.roll(own, 1, 0))
    slope_x = GRAVITY * ((upper - lower) * 0.5)
    upper = jnp.where(high_y, pltpu.roll(block(0, 1), rows_y - 1, 1), pltpu.roll(own, rows_y - 1, 1))
    lower = jnp.where(low_y, pltpu.roll(block(0, -1), 1, 1), pltpu.roll(own, 1, 1))
    slope_y = GRAVITY * ((upper - lower) * 0.5)
    counts = wet[...]
    for level in range(levels):
        here = counts > level
        new_velocity[0, level] = moved_velocity[0, level] - jnp.where(here, slope_x, 0.0)
        new_velocity[1, level] = moved_velocity[1, level] - jnp.where(here, slope_y, 0.0)


def latitude_rate(positions, total_rows):
    return 1.5 * jnp.sin(math.pi * ((positions + 0.5) / total_rows - 0.5))


def body(tracers, velocity, wet_levels, thickness, diagonal):
    levels = tracers.shape[1]
    cols_x, rows_y = wet_levels.shape
    chips_z, cores, blocks_y = (lax.axis_size("z"), lax.axis_size("core"), lax.axis_size("by"))
    blocks_x = chips_z * cores
    shape = (cols_x, rows_y)
    height = 2 * cols_x + 3
    rim_rows = 4 * levels + 1

    def like(*dims):
        return jax.ShapeDtypeStruct(dims, jnp.float32)

    def held(*dims):
        return pltpu.VMEM(dims, jnp.float32) if math.prod(dims) <= HELD_SIZE else like(*dims)

    def kept(array):
        if array.size > HELD_SIZE:
            return array
        return pltpu.with_memory_space_constraint(array, pltpu.VMEM)

    fields = (tracers, velocity, wet_levels, diagonal)
    rows_a, rows_b, cols_a, cols_b, *block = pl.pallas_call(
        pack_rims,
        out_shape=[
            held(rim_rows, rows_y), held(rim_rows, rows_y), held(*shape), held(*shape),
            held(*tracers.shape), held(*velocity.shape), pltpu.VMEM(shape, wet_levels.dtype),
            held(*shape), held(levels, rows_y),
        ],
        in_specs=[ANY] * 4 + [SMEM],
        out_specs=[VMEM] * 9,
        scratch_shapes=[pltpu.SemaphoreType.DMA((4,))],
    )(*(pltpu.with_memory_space_constraint(array, pltpu.HBM) for array in fields), thickness)
    block = [kept(array) for array in block]

    def exchange(message, axis, first):
        size = blocks_x if axis == "bx" else blocks_y
        pairs = [(i, i + 1) for i in range(first, size - 1, 2)]
        axes = ("z", "core") if axis == "bx" else axis
        return lax.ppermute(message, axes, pairs + [(j, i) for i, j in pairs])

    rows_b, rows_a = (exchange(rows_b, "bx", 1), exchange(rows_a, "bx", 0))
    cols_b, cols_a = (exchange(cols_b, "by", 1), exchange(cols_a, "by", 0))
    positions = (lax.axis_index("by") * rows_y + jnp.arange(rows_y, dtype=jnp.int32)).astype(jnp.float32)
    latitude = latitude_rate(positions, blocks_y * rows_y)[None]

    new_tracers, moved_velocity, surface = pl.pallas_call(
        level_kernel,
        out_shape=[
            like(*tracers.shape), held(*velocity.shape),
            held(chips_z * blocks_y, height, 1, rows_y),
        ],
        in_specs=[VMEM] * 10,
        out_specs=[ANY, VMEM, VMEM],
        scratch_shapes=[
            pltpu.VMEM(tracers.shape, jnp.float32),
            pltpu.VMEM((2, levels, *shape), jnp.float32),
            pltpu.SemaphoreType.DMA,
        ],
    )(*block, kept(latitude), kept(rows_a), kept(rows_b), kept(cols_a), kept(cols_b))

    gathered = lax.all_to_all(surface, ("z", "by"), split_axis=0, concat_axis=0, tiled=True)
    swapped = lax.ppermute(gathered, "core", [(0, 1), (1, 0)])
    gathered, swapped = (array.reshape(-1, rows_y) for array in (gathered, swapped))

    def solve(*refs):
        solve_kernel(blocks_x, blocks_y, *refs)

    blocks = blocks_x * blocks_y
    new_velocity, pressure = pl.pallas_call(
        solve,
        out_shape=[like(*velocity.shape), like(*shape)],
        in_specs=[VMEM] * 4,
        out_specs=[VMEM] * 2,
        scratch_shapes=[pltpu.VMEM((blocks, *shape), jnp.float32)] * 9,
        compiler_params=pltpu.CompilerParams(vmem_limit_bytes=(4 + 52 * blocks // 1024) * 2**20),
    )(kept(gathered), kept(swapped), kept(moved_velocity), block[2])
    return new_tracers, new_velocity, pressure


def solution(mesh):
    size_x, size_y = (mesh.shape["bx"], mesh.shape["by"])
    chips = jax.sharding.Mesh(mesh.devices.reshape(size_x // 2, 2, size_y), ("z", "core", "by"))
    along_x = ("z", "core")
    placed = (
        P(None, None, along_x, "by"),
        P(None, None, along_x, "by"),
        P(along_x, "by"),
        P(),
        P(along_x, None),
    )
    return jax.shard_map(
        body,
        mesh=chips,
        in_specs=placed,
        out_specs=(P(None, None, along_x, "by"), P(None, None, along_x, "by"), P(along_x, "by")),
        check_vma=False,
    )
```

```python
import math

import jax
import jax.numpy as jnp
from jax import lax
from jax.experimental import pallas as pl
from jax.experimental.pallas import tpu as pltpu
from jax.sharding import PartitionSpec as P

ITERS = 3

HEAT_ALPHA = 0.5
SALINITY_BETA = 0.8
KAPPA_SPREAD = 0.15
VISCOSITY = 0.1
TIME_INCREMENT = 0.2
GRAVITY = 1.0

HELD_SIZE = 2**18

VMEM = pl.BlockSpec(memory_space=pltpu.VMEM)
ANY = pl.BlockSpec(memory_space=pl.ANY)


def lanes_of(shape):
    return lax.broadcasted_iota(jnp.int32, shape, 1)


def sublanes_of(shape):
    return lax.broadcasted_iota(jnp.int32, shape, 0)


def position_x():
    return lax.axis_index("z") * lax.axis_size("core") + lax.axis_index("core")


def pack_rims(
    tracers_in, velocity_in, wet_in, diagonal_in, thickness_in,
    rows_a, rows_b, cols_a, cols_b, tracers, velocity, wet, diagonal, weights,
    thickness, semaphores,
):
    levels, cols_x, rows_y = tracers.shape[1:]
    row_start = pl.multiple_of(lax.axis_index("by") * rows_y, rows_y)
    copies = [
        pltpu.make_async_copy(source, target, semaphores.at[number])
        for number, (source, target) in enumerate((
            (tracers_in, tracers),
            (velocity_in, velocity),
            (wet_in, wet),
            (thickness_in, thickness),
            (diagonal_in.at[:, pl.ds(row_start, rows_y)], diagonal),
        ))
    ]
    for copy in copies:
        copy.start()
    even_x, even_y = (lax.axis_index("core") == 0, lax.axis_index("by") % 2 == 0)
    lane = lanes_of((cols_x, rows_y))
    for copy in copies:
        copy.wait()
    for level in range(levels):
        weights[level : level + 1, :] = jnp.full((1, rows_y), thickness[level], jnp.float32)
    counts = wet[...].astype(jnp.float32)
    first, last = jnp.zeros_like(counts), jnp.zeros_like(counts)
    for index in range(4 * levels + 1):
        field, level = divmod(index, levels)
        if field < 4:
            tile = (tracers if field < 2 else velocity)[field % 2, level]
        else:
            tile = counts
        top, bottom = (tile[0:1, :], tile[cols_x - 1 : cols_x, :])
        rows_a[index : index + 1, :] = jnp.where(even_x, bottom, top)
        rows_b[index : index + 1, :] = jnp.where(even_x, top, bottom)
        first = jnp.where(lane == index, tile[:, 0:1], first)
        last = jnp.where(lane == index, tile[:, rows_y - 1 : rows_y], last)
    cols_a[...] = jnp.where(even_y, last, first)
    cols_b[...] = jnp.where(even_y, first, last)


def level_kernel(
    tracers, velocity, wet, diagonal, weights, latitude, rows_b, rows_a, cols_b, cols_a,
    new_tracers, moved_velocity, surface,
    next_tracers, gradients, semaphore,
):
    levels, cols_x, rows_y = tracers.shape[1:]
    shape = (cols_x, rows_y)
    lane, sublane = (lanes_of(shape), sublanes_of(shape))
    low_x, high_x = (sublane == 0, sublane == cols_x - 1)
    low_y, high_y = (lane == 0, lane == rows_y - 1)
    even_x, even_y = (lax.axis_index("core") == 0, lax.axis_index("by") % 2 == 0)
    after_cols = jnp.where(even_y, cols_a[...], cols_b[...])
    before_cols = jnp.where(even_y, cols_b[...], cols_a[...])

    def neighbours(tile, index):
        row_a, row_b = (rows_a[index : index + 1, :], rows_b[index : index + 1, :])
        after_row, before_row = (jnp.where(even_x, row_a, row_b), jnp.where(even_x, row_b, row_a))
        return (
            jnp.where(high_x, after_row, pltpu.roll(tile, cols_x - 1, 0)),
            jnp.where(low_x, before_row, pltpu.roll(tile, 1, 0)),
            jnp.where(high_y, after_cols[:, index : index + 1], pltpu.roll(tile, rows_y - 1, 1)),
            jnp.where(low_y, before_cols[:, index : index + 1], pltpu.roll(tile, 1, 1)),
        )

    counts = wet[...].astype(jnp.float32)
    around = neighbours(counts, 4 * levels)
    shared = [jnp.minimum(counts, other) for other in around]
    both_x = jnp.minimum(shared[0], shared[1])
    both_y = jnp.minimum(shared[2], shared[3])
    zero = jnp.zeros(shape, jnp.float32)

    def laplacian(tile, others, level):
        total = zero
        for other, limit in zip(others, shared):
            total = total + jnp.where(limit > level, other - tile, 0.0)
        return total

    difference_x, difference_y = (zero, zero)
    for level in range(levels):
        weight = weights[level : level + 1, :]
        heat, salt = (tracers[0, level], tracers[1, level])
        heat_around = neighbours(heat, level)
        salt_around = neighbours(salt, levels + level)
        loads = [
            jnp.where(count > level, SALINITY_BETA * s - HEAT_ALPHA * t, 0.0)
            for count, s, t in zip(around, salt_around, heat_around)
        ]
        difference_x = difference_x + weight * (loads[0] - loads[1])
        difference_y = difference_y + weight * (loads[2] - loads[3])
        gradients[0, level] = jnp.where(both_x > level, difference_x * 0.5, 0.0)
        gradients[1, level] = jnp.where(both_y > level, difference_y * 0.5, 0.0)
        diffusivity = TIME_INCREMENT * KAPPA_SPREAD
        next_tracers[0, level] = heat + diffusivity * laplacian(heat, heat_around, level)
        next_tracers[1, level] = salt + diffusivity * laplacian(salt, salt_around, level)
    leaving = pltpu.make_async_copy(next_tracers, new_tracers, semaphore)
    leaving.start()

    coriolis = jnp.broadcast_to(latitude[...], shape)
    flow_x, flow_y = (zero, zero)
    for level in range(levels):
        here = counts > level
        weight = weights[level : level + 1, :]
        zonal, merid = (velocity[0, level], velocity[1, level])
        spread_x = laplacian(zonal, neighbours(zonal, 2 * levels + level), level)
        spread_y = laplacian(merid, neighbours(merid, 3 * levels + level), level)
        zonal_rate = coriolis * merid - gradients[0, level] + VISCOSITY * spread_x
        merid_rate = -coriolis * zonal - gradients[1, level] + VISCOSITY * spread_y
        next_zonal = zonal + jnp.where(here, TIME_INCREMENT * zonal_rate, 0.0)
        next_merid = merid + jnp.where(here, TIME_INCREMENT * merid_rate, 0.0)
        moved_velocity[0, level] = next_zonal
        moved_velocity[1, level] = next_merid
        flow_x = flow_x + jnp.where(here, weight * next_zonal, 0.0)
        flow_y = flow_y + jnp.where(here, weight * next_merid, 0.0)
    inverse = jnp.where(counts > 0, 1.0, 0.0) / (4.0 + diagonal[...])
    ahead = jnp.where(high_x, 0.0, pltpu.roll(flow_x, cols_x - 1, 0))
    behind = jnp.where(low_x, 0.0, pltpu.roll(flow_x, 1, 0))
    slope = ahead - behind
    ahead = jnp.where(high_y, 0.0, pltpu.roll(flow_y, rows_y - 1, 1))
    behind = jnp.where(low_y, 0.0, pltpu.roll(flow_y, 1, 1))
    inner = (slope + (ahead - behind)) * 0.5
    edge_x = flow_x * 0.5
    edge_y = flow_y * 0.5
    first = jnp.where(lane == sublane, edge_y[:, 0:1], 0.0)
    last = jnp.where(lane == sublane + cols_x, edge_y[:, rows_y - 1 : rows_y], 0.0)
    corner = jnp.sum(first + last, axis=0, keepdims=True)

    def place(target):
        surface[target, 0:cols_x, 0, :] = inner
        surface[target, cols_x : 2 * cols_x, 0, :] = inverse
        surface[target, 2 * cols_x : 2 * cols_x + 1, 0, :] = edge_x[0:1, :]
        surface[target, 2 * cols_x + 1 : 2 * cols_x + 2, 0, :] = edge_x[cols_x - 1 : cols_x, :]
        surface[target, 2 * cols_x + 2 : 2 * cols_x + 3, 0, :] = corner

    pl.loop(0, surface.shape[0], unroll=8)(place)
    leaving.wait()


def solve_kernel(
    blocks_x, blocks_y, gathered, swapped, moved_velocity, wet,
    new_velocity, pressure,
    residual, inverses, lifted_0, lifted_1, smooth_0, smooth_1, smooth_2, image_0, direction_1,
):
    levels, cols_x, rows_y = moved_velocity.shape[1:]
    shape = (cols_x, rows_y)
    lane, sublane = (lanes_of(shape), sublanes_of(shape))
    low_x, high_x = (sublane == 0, sublane == cols_x - 1)
    low_y, high_y = (lane == 0, lane == rows_y - 1)
    zero = jnp.zeros(shape, jnp.float32)

    def each_row(step, carry):
        if blocks_x <= 8:
            for row in range(blocks_x):
                carry = step(row, carry)
            return carry
        return lax.fori_loop(0, blocks_x, step, carry)

    def guarded(load, row, column):
        if isinstance(row, int):
            return load(row * blocks_y + column) if 0 <= row < blocks_x else 0.0
        inside = jnp.logical_and(row >= 0, row < blocks_x)
        return load(jnp.clip(row, 0, blocks_x - 1) * blocks_y + column) * inside.astype(jnp.float32)

    def along_x(load, row, column):
        tile = load(row * blocks_y + column)
        other = guarded(lambda i: load(i, slice(0, 1)), row + 1, column)
        after = jnp.where(high_x, other, pltpu.roll(tile, cols_x - 1, 0))
        other = guarded(lambda i: load(i, slice(cols_x - 1, cols_x)), row - 1, column)
        before = jnp.where(low_x, other, pltpu.roll(tile, 1, 0))
        return after + before

    def along_y(tiles):
        ahead = [pltpu.roll(tile, rows_y - 1, 1) for tile in tiles] + [0.0]
        behind = [0.0] + [pltpu.roll(tile, 1, 1) for tile in tiles]
        return [
            jnp.where(high_y, ahead[c + 1], ahead[c]) + jnp.where(low_y, behind[c], behind[c + 1])
            for c in range(blocks_y)
        ]

    def lift(inverse, tile):
        first = inverse * tile
        near = jnp.where(high_x, 0.0, pltpu.roll(first, cols_x - 1, 0))
        near = near + jnp.where(low_x, 0.0, pltpu.roll(first, 1, 0))
        near = near + jnp.where(high_y, 0.0, pltpu.roll(first, rows_y - 1, 1))
        near = near + jnp.where(low_y, 0.0, pltpu.roll(first, 1, 1))
        return tile + near

    def total(values):
        return jnp.sum(values, axis=(0, 1), keepdims=True)

    height = 2 * cols_x + 3

    def start_from(by_core):
        def rows_of(row, column, first, count):
            if isinstance(row, int):
                place = (row // 2 * blocks_y + column) * height + first
                return by_core[row % 2][place : place + count, :]
            place = (row // 2 * blocks_y + column) * height + first
            found = [blocks[pl.ds(place, count), :] for blocks in by_core]
            return jnp.where(row % 2 == 0, *found)

        def edge_row(which, row, column):
            if isinstance(row, int):
                inside = 0 <= row < blocks_x
                return rows_of(row, column, 2 * cols_x + which, 1) if inside else 0.0
            inside = jnp.logical_and(row >= 0, row < blocks_x).astype(jnp.float32)
            row = jnp.clip(row, 0, blocks_x - 1)
            return rows_of(row, column, 2 * cols_x + which, 1) * inside

        def step(row, carry):
            corners = [rows_of(row, c, 2 * cols_x + 2, 1) for c in range(blocks_y)]
            filler = [jnp.zeros((1, rows_y), jnp.float32)] * (-blocks_y % 8)
            corners = jnp.transpose(jnp.concatenate(corners + filler, axis=0))
            for column in range(blocks_y):
                index = row * blocks_y + column
                forcing = rows_of(row, column, 0, cols_x)
                forcing = forcing + jnp.where(high_x, edge_row(0, row + 1, column), 0.0)
                forcing = forcing - jnp.where(low_x, edge_row(1, row - 1, column), 0.0)
                if column + 1 < blocks_y:
                    beyond = corners[0:cols_x, column + 1 : column + 2]
                    forcing = forcing + jnp.where(high_y, beyond, 0.0)
                if column > 0:
                    beyond = corners[cols_x : 2 * cols_x, column - 1 : column]
                    forcing = forcing - jnp.where(low_y, beyond, 0.0)
                inverse = rows_of(row, column, cols_x, cols_x)
                lifted = lift(inverse, forcing)
                inverses[index] = inverse
                residual[index] = forcing
                lifted_0[index] = lifted
                smooth_0[index] = inverse * lifted
            return carry

        each_row(step, 0)

    def operate(lifted, smooth, image):
        def load(index, rows=slice(None)):
            return smooth[index, rows]

        def step(row, carry):
            inner, curvature = carry
            tiles = [smooth[row * blocks_y + c] for c in range(blocks_y)]
            beside = along_y(tiles)
            for column in range(blocks_y):
                index = row * blocks_y + column
                result = lifted[index] - (along_x(load, row, column) + beside[column])
                if image is not None:
                    image[index] = result
                inner = inner + residual[index] * tiles[column]
                curvature = curvature + tiles[column] * result
            return inner, curvature

        inner, curvature = each_row(step, (zero, zero))
        return total(inner), total(curvature)

    own_core = lax.axis_index("core")
    pl.when(own_core == 0)(lambda: start_from((gathered, swapped)))
    pl.when(own_core == 1)(lambda: start_from((swapped, gathered)))
    inner_0, curvature_0 = operate(lifted_0, smooth_0, image_0)
    step_0 = inner_0 / curvature_0

    def advance_0(row, carry):
        for column in range(blocks_y):
            index = row * blocks_y + column
            left = residual[index] - step_0 * image_0[index]
            inverse = inverses[index]
            lifted = lift(inverse, left)
            residual[index] = left
            lifted_1[index] = lifted
            smooth_1[index] = inverse * lifted
        return carry

    each_row(advance_0, 0)
    image_1 = lifted_1
    inner_1, curvature_1 = operate(lifted_1, smooth_1, image_1)
    turn_1 = inner_1 / inner_0
    step_1 = inner_1 / (curvature_1 - turn_1 * inner_1 / step_0)

    def advance_1(row, carry):
        for column in range(blocks_y):
            index = row * blocks_y + column
            direction_1[index] = smooth_1[index] + turn_1 * smooth_0[index]
            left = residual[index] - step_1 * (image_1[index] + turn_1 * image_0[index])
            inverse = inverses[index]
            lifted = lift(inverse, left)
            residual[index] = left
            lifted_0[index] = lifted
            smooth_2[index] = inverse * lifted
        return carry

    each_row(advance_1, 0)
    inner_2, curvature_2 = operate(lifted_0, smooth_2, None)
    turn_2 = inner_2 / inner_1
    step_2 = inner_2 / (curvature_2 - turn_2 * inner_2 / step_1)

    def iterate(index):
        previous = direction_1[index]
        result = step_0 * smooth_0[index] + step_1 * previous
        return result + step_2 * (smooth_2[index] + turn_2 * previous)

    own_x, own_y = (position_x(), lax.axis_index("by"))

    def block(shift_x, shift_y):
        row, column = (own_x + shift_x, own_y + shift_y)
        inside = (row >= 0) & (row < blocks_x) & (column >= 0) & (column < blocks_y)
        row, column = (jnp.clip(row, 0, blocks_x - 1), jnp.clip(column, 0, blocks_y - 1))
        return jnp.where(inside, iterate(row * blocks_y + column), 0.0)

    own = iterate(own_x * blocks_y + own_y)
    pressure[...] = own
    upper = jnp.where(high_x, pltpu.roll(block(1, 0), cols_x - 1, 0), pltpu.roll(own, cols_x - 1, 0))
    lower = jnp.where(low_x, pltpu.roll(block(-1, 0), 1, 0), pltpu.roll(own, 1, 0))
    slope_x = GRAVITY * ((upper - lower) * 0.5)
    upper = jnp.where(high_y, pltpu.roll(block(0, 1), rows_y - 1, 1), pltpu.roll(own, rows_y - 1, 1))
    lower = jnp.where(low_y, pltpu.roll(block(0, -1), 1, 1), pltpu.roll(own, 1, 1))
    slope_y = GRAVITY * ((upper - lower) * 0.5)
    counts = wet[...]
    for level in range(levels):
        here = counts > level
        new_velocity[0, level] = moved_velocity[0, level] - jnp.where(here, slope_x, 0.0)
        new_velocity[1, level] = moved_velocity[1, level] - jnp.where(here, slope_y, 0.0)


def latitude_rate(positions, total_rows):
    return 1.5 * jnp.sin(math.pi * ((positions + 0.5) / total_rows - 0.5))


def body(tracers, velocity, wet_levels, thickness, diagonal):
    levels = tracers.shape[1]
    cols_x, rows_y = wet_levels.shape
    chips_z, cores, blocks_y = (lax.axis_size("z"), lax.axis_size("core"), lax.axis_size("by"))
    blocks_x = chips_z * cores
    shape = (cols_x, rows_y)
    height = 2 * cols_x + 3
    rim_rows = 4 * levels + 1

    def like(*dims):
        return jax.ShapeDtypeStruct(dims, jnp.float32)

    def held(*dims):
        return pltpu.VMEM(dims, jnp.float32) if math.prod(dims) <= HELD_SIZE else like(*dims)

    def kept(array):
        if array.size > HELD_SIZE:
            return array
        return pltpu.with_memory_space_constraint(array, pltpu.VMEM)

    fields = (tracers, velocity, wet_levels, diagonal, thickness)
    rows_a, rows_b, cols_a, cols_b, *block = pl.pallas_call(
        pack_rims,
        out_shape=[
            held(rim_rows, rows_y), held(rim_rows, rows_y), held(*shape), held(*shape),
            held(*tracers.shape), held(*velocity.shape), pltpu.VMEM(shape, wet_levels.dtype),
            held(*shape), held(levels, rows_y),
        ],
        in_specs=[ANY] * 5,
        out_specs=[VMEM] * 9,
        scratch_shapes=[pltpu.SMEM(thickness.shape, jnp.float32), pltpu.SemaphoreType.DMA((5,))],
    )(*(pltpu.with_memory_space_constraint(array, pltpu.HBM) for array in fields))
    block = [kept(array) for array in block]

    def exchange(message, axis, first):
        size = blocks_x if axis == "bx" else blocks_y
        pairs = [(i, i + 1) for i in range(first, size - 1, 2)]
        axes = ("z", "core") if axis == "bx" else axis
        return lax.ppermute(message, axes, pairs + [(j, i) for i, j in pairs])

    rows_b, rows_a = (exchange(rows_b, "bx", 1), exchange(rows_a, "bx", 0))
    cols_b, cols_a = (exchange(cols_b, "by", 1), exchange(cols_a, "by", 0))
    positions = (lax.axis_index("by") * rows_y + jnp.arange(rows_y, dtype=jnp.int32)).astype(jnp.float32)
    latitude = latitude_rate(positions, blocks_y * rows_y)[None]

    new_tracers, moved_velocity, surface = pl.pallas_call(
        level_kernel,
        out_shape=[
            like(*tracers.shape), held(*velocity.shape),
            held(chips_z * blocks_y, height, 1, rows_y),
        ],
        in_specs=[VMEM] * 10,
        out_specs=[ANY, VMEM, VMEM],
        scratch_shapes=[
            pltpu.VMEM(tracers.shape, jnp.float32),
            pltpu.VMEM((2, levels, *shape), jnp.float32),
            pltpu.SemaphoreType.DMA,
        ],
    )(*block, kept(latitude), kept(rows_b), kept(rows_a), kept(cols_b), kept(cols_a))

    gathered = lax.all_to_all(surface, ("z", "by"), split_axis=0, concat_axis=0, tiled=True)
    swapped = lax.ppermute(gathered, "core", [(0, 1), (1, 0)])
    gathered, swapped = (array.reshape(-1, rows_y) for array in (gathered, swapped))

    def solve(*refs):
        solve_kernel(blocks_x, blocks_y, *refs)

    blocks = blocks_x * blocks_y
    new_velocity, pressure = pl.pallas_call(
        solve,
        out_shape=[like(*velocity.shape), like(*shape)],
        in_specs=[VMEM] * 4,
        out_specs=[VMEM] * 2,
        scratch_shapes=[pltpu.VMEM((blocks, *shape), jnp.float32)] * 9,
        compiler_params=pltpu.CompilerParams(vmem_limit_bytes=(4 + 52 * blocks // 1024) * 2**20),
    )(kept(gathered), kept(swapped), kept(moved_velocity), block[2])
    return new_tracers, new_velocity, pressure


def solution(mesh):
    size_x, size_y = (mesh.shape["bx"], mesh.shape["by"])
    chips = jax.sharding.Mesh(mesh.devices.reshape(size_x // 2, 2, size_y), ("z", "core", "by"))
    along_x = ("z", "core")
    placed = (
        P(None, None, along_x, "by"),
        P(None, None, along_x, "by"),
        P(along_x, "by"),
        P(),
        P(along_x, None),
    )
    return jax.shard_map(
        body,
        mesh=chips,
        in_specs=placed,
        out_specs=(P(None, None, along_x, "by"), P(None, None, along_x, "by"), P(along_x, "by")),
        check_vma=False,
    )
```

```python
import math

import jax
import jax.numpy as jnp
from jax import lax
from jax.experimental import pallas as pl
from jax.experimental.pallas import tpu as pltpu
from jax.sharding import PartitionSpec as P

ITERS = 3

HEAT_ALPHA = 0.5
SALINITY_BETA = 0.8
KAPPA_SPREAD = 0.15
VISCOSITY = 0.1
TIME_INCREMENT = 0.2
GRAVITY = 1.0

HELD_SIZE = 2**18

VMEM = pl.BlockSpec(memory_space=pltpu.VMEM)
ANY = pl.BlockSpec(memory_space=pl.ANY)


def lanes_of(shape):
    return lax.broadcasted_iota(jnp.int32, shape, 1)


def sublanes_of(shape):
    return lax.broadcasted_iota(jnp.int32, shape, 0)


def position_x():
    return lax.axis_index("z") * lax.axis_size("core") + lax.axis_index("core")


def pack_rims(
    tracers_in, velocity_in, wet_in, diagonal_in, thickness_in,
    rows_a, rows_b, cols, tracers, velocity, wet, diagonal, weights,
    thickness, semaphores,
):
    levels, cols_x, rows_y = tracers.shape[1:]
    row_start = pl.multiple_of(lax.axis_index("by") * rows_y, rows_y)
    copies = [
        pltpu.make_async_copy(source, target, semaphores.at[number])
        for number, (source, target) in enumerate((
            (tracers_in, tracers),
            (velocity_in, velocity),
            (wet_in, wet),
            (thickness_in, thickness),
            (diagonal_in.at[:, pl.ds(row_start, rows_y)], diagonal),
        ))
    ]
    for copy in copies:
        copy.start()
    even_x = lax.axis_index("core") == 0
    lane = lanes_of((cols_x, rows_y))
    for copy in copies:
        copy.wait()
    for level in range(levels):
        weights[level : level + 1, :] = jnp.full((1, rows_y), thickness[level], jnp.float32)
    counts = wet[...].astype(jnp.float32)
    first, last = jnp.zeros_like(counts), jnp.zeros_like(counts)
    for index in range(4 * levels + 1):
        field, level = divmod(index, levels)
        if field < 4:
            tile = (tracers if field < 2 else velocity)[field % 2, level]
        else:
            tile = counts
        top, bottom = (tile[0:1, :], tile[cols_x - 1 : cols_x, :])
        rows_a[index : index + 1, :] = jnp.where(even_x, bottom, top)
        rows_b[index : index + 1, :] = jnp.where(even_x, top, bottom)
        first = jnp.where(lane == index, tile[:, 0:1], first)
        last = jnp.where(lane == index, tile[:, rows_y - 1 : rows_y], last)
    own_y = lax.axis_index("by")
    for target in range(cols.shape[0]):
        cols[target] = jnp.where(target > own_y, last, first)


def level_kernel(
    tracers, velocity, wet, diagonal, weights, latitude, rows_b, rows_a, cols,
    new_tracers, moved_velocity, surface,
    next_tracers, gradients, semaphore,
):
    levels, cols_x, rows_y = tracers.shape[1:]
    shape = (cols_x, rows_y)
    lane, sublane = (lanes_of(shape), sublanes_of(shape))
    low_x, high_x = (sublane == 0, sublane == cols_x - 1)
    low_y, high_y = (lane == 0, lane == rows_y - 1)
    even_x, own_y, blocks_y = (lax.axis_index("core") == 0, lax.axis_index("by"), cols.shape[0])
    after_cols = jnp.where(own_y < blocks_y - 1, cols[jnp.minimum(own_y + 1, blocks_y - 1)], 0.0)
    before_cols = jnp.where(own_y > 0, cols[jnp.maximum(own_y - 1, 0)], 0.0)

    def neighbours(tile, index):
        row_a, row_b = (rows_a[index : index + 1, :], rows_b[index : index + 1, :])
        after_row, before_row = (jnp.where(even_x, row_a, row_b), jnp.where(even_x, row_b, row_a))
        return (
            jnp.where(high_x, after_row, pltpu.roll(tile, cols_x - 1, 0)),
            jnp.where(low_x, before_row, pltpu.roll(tile, 1, 0)),
            jnp.where(high_y, after_cols[:, index : index + 1], pltpu.roll(tile, rows_y - 1, 1)),
            jnp.where(low_y, before_cols[:, index : index + 1], pltpu.roll(tile, 1, 1)),
        )

    counts = wet[...].astype(jnp.float32)
    around = neighbours(counts, 4 * levels)
    shared = [jnp.minimum(counts, other) for other in around]
    both_x = jnp.minimum(shared[0], shared[1])
    both_y = jnp.minimum(shared[2], shared[3])
    zero = jnp.zeros(shape, jnp.float32)

    def laplacian(tile, others, level):
        total = zero
        for other, limit in zip(others, shared):
            total = total + jnp.where(limit > level, other - tile, 0.0)
        return total

    difference_x, difference_y = (zero, zero)
    for level in range(levels):
        weight = weights[level : level + 1, :]
        heat, salt = (tracers[0, level], tracers[1, level])
        heat_around = neighbours(heat, level)
        salt_around = neighbours(salt, levels + level)
        loads = [
            jnp.where(count > level, SALINITY_BETA * s - HEAT_ALPHA * t, 0.0)
            for count, s, t in zip(around, salt_around, heat_around)
        ]
        difference_x = difference_x + weight * (loads[0] - loads[1])
        difference_y = difference_y + weight * (loads[2] - loads[3])
        gradients[0, level] = jnp.where(both_x > level, difference_x * 0.5, 0.0)
        gradients[1, level] = jnp.where(both_y > level, difference_y * 0.5, 0.0)
        diffusivity = TIME_INCREMENT * KAPPA_SPREAD
        next_tracers[0, level] = heat + diffusivity * laplacian(heat, heat_around, level)
        next_tracers[1, level] = salt + diffusivity * laplacian(salt, salt_around, level)
    leaving = pltpu.make_async_copy(next_tracers, new_tracers, semaphore)
    leaving.start()

    coriolis = jnp.broadcast_to(latitude[...], shape)
    flow_x, flow_y = (zero, zero)
    for level in range(levels):
        here = counts > level
        weight = weights[level : level + 1, :]
        zonal, merid = (velocity[0, level], velocity[1, level])
        spread_x = laplacian(zonal, neighbours(zonal, 2 * levels + level), level)
        spread_y = laplacian(merid, neighbours(merid, 3 * levels + level), level)
        zonal_rate = coriolis * merid - gradients[0, level] + VISCOSITY * spread_x
        merid_rate = -coriolis * zonal - gradients[1, level] + VISCOSITY * spread_y
        next_zonal = zonal + jnp.where(here, TIME_INCREMENT * zonal_rate, 0.0)
        next_merid = merid + jnp.where(here, TIME_INCREMENT * merid_rate, 0.0)
        moved_velocity[0, level] = next_zonal
        moved_velocity[1, level] = next_merid
        flow_x = flow_x + jnp.where(here, weight * next_zonal, 0.0)
        flow_y = flow_y + jnp.where(here, weight * next_merid, 0.0)
    inverse = jnp.where(counts > 0, 1.0, 0.0) / (4.0 + diagonal[...])
    ahead = jnp.where(high_x, 0.0, pltpu.roll(flow_x, cols_x - 1, 0))
    behind = jnp.where(low_x, 0.0, pltpu.roll(flow_x, 1, 0))
    slope = ahead - behind
    ahead = jnp.where(high_y, 0.0, pltpu.roll(flow_y, rows_y - 1, 1))
    behind = jnp.where(low_y, 0.0, pltpu.roll(flow_y, 1, 1))
    inner = (slope + (ahead - behind)) * 0.5
    edge_x = flow_x * 0.5
    edge_y = flow_y * 0.5
    first = jnp.where(lane == sublane, edge_y[:, 0:1], 0.0)
    last = jnp.where(lane == sublane + cols_x, edge_y[:, rows_y - 1 : rows_y], 0.0)
    corner = jnp.sum(first + last, axis=0, keepdims=True)

    def place(target):
        surface[target, 0:cols_x, 0, :] = inner
        surface[target, cols_x : 2 * cols_x, 0, :] = inverse
        surface[target, 2 * cols_x : 2 * cols_x + 1, 0, :] = edge_x[0:1, :]
        surface[target, 2 * cols_x + 1 : 2 * cols_x + 2, 0, :] = edge_x[cols_x - 1 : cols_x, :]
        surface[target, 2 * cols_x + 2 : 2 * cols_x + 3, 0, :] = corner

    pl.loop(0, surface.shape[0], unroll=8)(place)
    leaving.wait()


def solve_kernel(
    blocks_x, blocks_y, gathered, moved_velocity, wet,
    new_velocity, pressure,
    residual, inverses, lifted_0, lifted_1, smooth_0, smooth_1, smooth_2, image_0, direction_1,
):
    levels, cols_x, rows_y = moved_velocity.shape[1:]
    shape = (cols_x, rows_y)
    lane, sublane = (lanes_of(shape), sublanes_of(shape))
    low_x, high_x = (sublane == 0, sublane == cols_x - 1)
    low_y, high_y = (lane == 0, lane == rows_y - 1)
    zero = jnp.zeros(shape, jnp.float32)

    def each_row(step, carry):
        if blocks_x <= 8:
            for row in range(blocks_x):
                carry = step(row, carry)
            return carry
        return lax.fori_loop(0, blocks_x, step, carry)

    def guarded(load, row, column):
        if isinstance(row, int):
            return load(row * blocks_y + column) if 0 <= row < blocks_x else 0.0
        inside = jnp.logical_and(row >= 0, row < blocks_x)
        return load(jnp.clip(row, 0, blocks_x - 1) * blocks_y + column) * inside.astype(jnp.float32)

    def along_x(load, row, column):
        tile = load(row * blocks_y + column)
        other = guarded(lambda i: load(i, slice(0, 1)), row + 1, column)
        after = jnp.where(high_x, other, pltpu.roll(tile, cols_x - 1, 0))
        other = guarded(lambda i: load(i, slice(cols_x - 1, cols_x)), row - 1, column)
        before = jnp.where(low_x, other, pltpu.roll(tile, 1, 0))
        return after + before

    def along_y(tiles):
        ahead = [pltpu.roll(tile, rows_y - 1, 1) for tile in tiles] + [0.0]
        behind = [0.0] + [pltpu.roll(tile, 1, 1) for tile in tiles]
        return [
            jnp.where(high_y, ahead[c + 1], ahead[c]) + jnp.where(low_y, behind[c], behind[c + 1])
            for c in range(blocks_y)
        ]

    def lift(inverse, tile):
        first = inverse * tile
        near = jnp.where(high_x, 0.0, pltpu.roll(first, cols_x - 1, 0))
        near = near + jnp.where(low_x, 0.0, pltpu.roll(first, 1, 0))
        near = near + jnp.where(high_y, 0.0, pltpu.roll(first, rows_y - 1, 1))
        near = near + jnp.where(low_y, 0.0, pltpu.roll(first, 1, 1))
        return tile + near

    def total(values):
        return jnp.sum(values, axis=(0, 1), keepdims=True)

    height = 2 * cols_x + 3

    def start_all():
        def rows_of(row, column, first, count):
            place = (column * blocks_x + row) * height + first
            return gathered[pl.ds(place, count), :]

        def edge_row(which, row, column):
            if isinstance(row, int):
                inside = 0 <= row < blocks_x
                return rows_of(row, column, 2 * cols_x + which, 1) if inside else 0.0
            inside = jnp.logical_and(row >= 0, row < blocks_x).astype(jnp.float32)
            row = jnp.clip(row, 0, blocks_x - 1)
            return rows_of(row, column, 2 * cols_x + which, 1) * inside

        def step(row, carry):
            corners = [rows_of(row, c, 2 * cols_x + 2, 1) for c in range(blocks_y)]
            filler = [jnp.zeros((1, rows_y), jnp.float32)] * (-blocks_y % 8)
            corners = jnp.transpose(jnp.concatenate(corners + filler, axis=0))
            for column in range(blocks_y):
                index = row * blocks_y + column
                forcing = rows_of(row, column, 0, cols_x)
                forcing = forcing + jnp.where(high_x, edge_row(0, row + 1, column), 0.0)
                forcing = forcing - jnp.where(low_x, edge_row(1, row - 1, column), 0.0)
                if column + 1 < blocks_y:
                    beyond = corners[0:cols_x, column + 1 : column + 2]
                    forcing = forcing + jnp.where(high_y, beyond, 0.0)
                if column > 0:
                    beyond = corners[cols_x : 2 * cols_x, column - 1 : column]
                    forcing = forcing - jnp.where(low_y, beyond, 0.0)
                inverse = rows_of(row, column, cols_x, cols_x)
                lifted = lift(inverse, forcing)
                inverses[index] = inverse
                residual[index] = forcing
                lifted_0[index] = lifted
                smooth_0[index] = inverse * lifted
            return carry

        each_row(step, 0)

    def operate(lifted, smooth, image):
        def load(index, rows=slice(None)):
            return smooth[index, rows]

        def step(row, carry):
            inner, curvature = carry
            tiles = [smooth[row * blocks_y + c] for c in range(blocks_y)]
            beside = along_y(tiles)
            for column in range(blocks_y):
                index = row * blocks_y + column
                result = lifted[index] - (along_x(load, row, column) + beside[column])
                if image is not None:
                    image[index] = result
                inner = inner + residual[index] * tiles[column]
                curvature = curvature + tiles[column] * result
            return inner, curvature

        inner, curvature = each_row(step, (zero, zero))
        return total(inner), total(curvature)

    start_all()
    inner_0, curvature_0 = operate(lifted_0, smooth_0, image_0)
    step_0 = inner_0 / curvature_0

    def advance_0(row, carry):
        for column in range(blocks_y):
            index = row * blocks_y + column
            left = residual[index] - step_0 * image_0[index]
            inverse = inverses[index]
            lifted = lift(inverse, left)
            residual[index] = left
            lifted_1[index] = lifted
            smooth_1[index] = inverse * lifted
        return carry

    each_row(advance_0, 0)
    image_1 = lifted_1
    inner_1, curvature_1 = operate(lifted_1, smooth_1, image_1)
    turn_1 = inner_1 / inner_0
    step_1 = inner_1 / (curvature_1 - turn_1 * inner_1 / step_0)

    def advance_1(row, carry):
        for column in range(blocks_y):
            index = row * blocks_y + column
            direction_1[index] = smooth_1[index] + turn_1 * smooth_0[index]
            left = residual[index] - step_1 * (image_1[index] + turn_1 * image_0[index])
            inverse = inverses[index]
            lifted = lift(inverse, left)
            residual[index] = left
            lifted_0[index] = lifted
            smooth_2[index] = inverse * lifted
        return carry

    each_row(advance_1, 0)
    inner_2, curvature_2 = operate(lifted_0, smooth_2, None)
    turn_2 = inner_2 / inner_1
    step_2 = inner_2 / (curvature_2 - turn_2 * inner_2 / step_1)

    def iterate(index):
        previous = direction_1[index]
        result = step_0 * smooth_0[index] + step_1 * previous
        return result + step_2 * (smooth_2[index] + turn_2 * previous)

    own_x, own_y = (position_x(), lax.axis_index("by"))

    def block(shift_x, shift_y):
        row, column = (own_x + shift_x, own_y + shift_y)
        inside = (row >= 0) & (row < blocks_x) & (column >= 0) & (column < blocks_y)
        row, column = (jnp.clip(row, 0, blocks_x - 1), jnp.clip(column, 0, blocks_y - 1))
        return jnp.where(inside, iterate(row * blocks_y + column), 0.0)

    own = iterate(own_x * blocks_y + own_y)
    pressure[...] = own
    upper = jnp.where(high_x, pltpu.roll(block(1, 0), cols_x - 1, 0), pltpu.roll(own, cols_x - 1, 0))
    lower = jnp.where(low_x, pltpu.roll(block(-1, 0), 1, 0), pltpu.roll(own, 1, 0))
    slope_x = GRAVITY * ((upper - lower) * 0.5)
    upper = jnp.where(high_y, pltpu.roll(block(0, 1), rows_y - 1, 1), pltpu.roll(own, rows_y - 1, 1))
    lower = jnp.where(low_y, pltpu.roll(block(0, -1), 1, 1), pltpu.roll(own, 1, 1))
    slope_y = GRAVITY * ((upper - lower) * 0.5)
    counts = wet[...]
    for level in range(levels):
        here = counts > level
        new_velocity[0, level] = moved_velocity[0, level] - jnp.where(here, slope_x, 0.0)
        new_velocity[1, level] = moved_velocity[1, level] - jnp.where(here, slope_y, 0.0)


def latitude_rate(positions, total_rows):
    return 1.5 * jnp.sin(math.pi * ((positions + 0.5) / total_rows - 0.5))


def body(tracers, velocity, wet_levels, thickness, diagonal):
    levels = tracers.shape[1]
    cols_x, rows_y = wet_levels.shape
    chips_z, cores, blocks_y = (lax.axis_size("z"), lax.axis_size("core"), lax.axis_size("by"))
    blocks_x = chips_z * cores
    shape = (cols_x, rows_y)
    height = 2 * cols_x + 3
    rim_rows = 4 * levels + 1

    def like(*dims):
        return jax.ShapeDtypeStruct(dims, jnp.float32)

    def held(*dims):
        return pltpu.VMEM(dims, jnp.float32) if math.prod(dims) <= HELD_SIZE else like(*dims)

    def kept(array):
        if array.size > HELD_SIZE:
            return array
        return pltpu.with_memory_space_constraint(array, pltpu.VMEM)

    fields = (tracers, velocity, wet_levels, diagonal, thickness)
    rows_a, rows_b, cols, *block = pl.pallas_call(
        pack_rims,
        out_shape=[
            held(rim_rows, rows_y), held(rim_rows, rows_y), held(blocks_y, *shape),
            held(*tracers.shape), held(*velocity.shape), pltpu.VMEM(shape, wet_levels.dtype),
            held(*shape), held(levels, rows_y),
        ],
        in_specs=[ANY] * 5,
        out_specs=[VMEM] * 8,
        scratch_shapes=[pltpu.SMEM(thickness.shape, jnp.float32), pltpu.SemaphoreType.DMA((5,))],
    )(*(pltpu.with_memory_space_constraint(array, pltpu.HBM) for array in fields))
    block = [kept(array) for array in block]

    def exchange(message, first):
        pairs = [(i, i + 1) for i in range(first, blocks_x - 1, 2)]
        return lax.ppermute(message, ("z", "core"), pairs + [(j, i) for i, j in pairs])

    cols = lax.all_to_all(cols, "by", split_axis=0, concat_axis=0, tiled=True)
    rows_b, rows_a = (exchange(rows_b, 1), exchange(rows_a, 0))
    positions = (lax.axis_index("by") * rows_y + jnp.arange(rows_y, dtype=jnp.int32)).astype(jnp.float32)
    latitude = latitude_rate(positions, blocks_y * rows_y)[None]

    new_tracers, moved_velocity, surface = pl.pallas_call(
        level_kernel,
        out_shape=[
            like(*tracers.shape), held(*velocity.shape),
            held(blocks_x, height, 1, rows_y),
        ],
        in_specs=[VMEM] * 9,
        out_specs=[ANY, VMEM, VMEM],
        scratch_shapes=[
            pltpu.VMEM(tracers.shape, jnp.float32),
            pltpu.VMEM((2, levels, *shape), jnp.float32),
            pltpu.SemaphoreType.DMA,
        ],
    )(*block, kept(latitude), kept(rows_b), kept(rows_a), kept(cols))

    gathered = lax.all_to_all(surface, ("z", "core"), split_axis=0, concat_axis=0, tiled=True)
    gathered = lax.all_gather(gathered, "by", axis=0, tiled=True).reshape(-1, rows_y)

    def solve(*refs):
        solve_kernel(blocks_x, blocks_y, *refs)

    blocks = blocks_x * blocks_y
    new_velocity, pressure = pl.pallas_call(
        solve,
        out_shape=[like(*velocity.shape), like(*shape)],
        in_specs=[VMEM] * 3,
        out_specs=[VMEM] * 2,
        scratch_shapes=[pltpu.VMEM((blocks, *shape), jnp.float32)] * 9,
        compiler_params=pltpu.CompilerParams(vmem_limit_bytes=(4 + 52 * blocks // 1024) * 2**20),
    )(kept(gathered), kept(moved_velocity), block[2])
    return new_tracers, new_velocity, pressure


def solution(mesh):
    size_x, size_y = (mesh.shape["bx"], mesh.shape["by"])
    chips = jax.sharding.Mesh(mesh.devices.reshape(size_x // 2, 2, size_y), ("z", "core", "by"))
    along_x = ("z", "core")
    placed = (
        P(None, None, along_x, "by"),
        P(None, None, along_x, "by"),
        P(along_x, "by"),
        P(),
        P(along_x, None),
    )
    return jax.shard_map(
        body,
        mesh=chips,
        in_specs=placed,
        out_specs=(P(None, None, along_x, "by"), P(None, None, along_x, "by"), P(along_x, "by")),
        check_vma=False,
    )
```

```python
import math

import jax
import jax.numpy as jnp
from jax import lax
from jax.experimental import pallas as pl
from jax.experimental.pallas import tpu as pltpu
from jax.sharding import PartitionSpec as P

ITERS = 3

HEAT_ALPHA = 0.5
SALINITY_BETA = 0.8
KAPPA_SPREAD = 0.15
VISCOSITY = 0.1
TIME_INCREMENT = 0.2
GRAVITY = 1.0

HELD_SIZE = 2**18

VMEM = pl.BlockSpec(memory_space=pltpu.VMEM)
ANY = pl.BlockSpec(memory_space=pl.ANY)


def lanes_of(shape):
    return lax.broadcasted_iota(jnp.int32, shape, 1)


def sublanes_of(shape):
    return lax.broadcasted_iota(jnp.int32, shape, 0)


def position_x():
    return lax.axis_index("z") * lax.axis_size("core") + lax.axis_index("core")


def pack_rims(
    tracers_in, velocity_in, wet_in, diagonal_in, thickness_in,
    rows_a, rows_b, early, tracers, velocity, wet, weights,
    diagonal, thickness, semaphores,
):
    levels, cols_x, rows_y = tracers.shape[1:]
    row_start = pl.multiple_of(lax.axis_index("by") * rows_y, rows_y)
    copies = [
        pltpu.make_async_copy(source, target, semaphores.at[number])
        for number, (source, target) in enumerate((
            (tracers_in, tracers),
            (velocity_in, velocity),
            (wet_in, wet),
            (thickness_in, thickness),
            (diagonal_in.at[:, pl.ds(row_start, rows_y)], diagonal),
        ))
    ]
    for copy in copies:
        copy.start()
    even_x = lax.axis_index("core") == 0
    lane = lanes_of((cols_x, rows_y))
    for copy in copies:
        copy.wait()
    for level in range(levels):
        weights[level : level + 1, :] = jnp.full((1, rows_y), thickness[level], jnp.float32)
    counts = wet[...].astype(jnp.float32)
    first, last = jnp.zeros_like(counts), jnp.zeros_like(counts)
    for index in range(4 * levels + 1):
        field, level = divmod(index, levels)
        if field < 4:
            tile = (tracers if field < 2 else velocity)[field % 2, level]
        else:
            tile = counts
        top, bottom = (tile[0:1, :], tile[cols_x - 1 : cols_x, :])
        rows_a[index : index + 1, :] = jnp.where(even_x, bottom, top)
        rows_b[index : index + 1, :] = jnp.where(even_x, top, bottom)
        first = jnp.where(lane == index, tile[:, 0:1], first)
        last = jnp.where(lane == index, tile[:, rows_y - 1 : rows_y], last)
    inverse = jnp.where(counts > 0, 1.0, 0.0) / (4.0 + diagonal[...])
    blocks_y = lax.axis_size("by")
    own_y = lax.axis_index("by")
    sides = [jnp.where(column > own_y, last, first) for column in range(blocks_y)]

    def place(row):
        for column, side in enumerate(sides):
            early[row * blocks_y + column, 0:cols_x] = inverse
            early[row * blocks_y + column, cols_x : 2 * cols_x] = side

    pl.loop(0, early.shape[0] // blocks_y, unroll=8)(place)


def level_kernel(
    tracers, velocity, wet, weights, latitude, rows_b, rows_a, early,
    new_tracers, moved_velocity, surface,
    next_tracers, gradients, semaphore,
):
    levels, cols_x, rows_y = tracers.shape[1:]
    shape = (cols_x, rows_y)
    lane, sublane = (lanes_of(shape), sublanes_of(shape))
    low_x, high_x = (sublane == 0, sublane == cols_x - 1)
    low_y, high_y = (lane == 0, lane == rows_y - 1)
    even_x = lax.axis_index("core") == 0
    own_y, blocks_y = (lax.axis_index("by"), lax.axis_size("by"))
    own = position_x() * blocks_y + own_y
    after = jnp.minimum(own + 1, early.shape[0] - 1)
    before = jnp.maximum(own - 1, 0)
    after_cols = jnp.where(own_y < blocks_y - 1, early[after, cols_x : 2 * cols_x], 0.0)
    before_cols = jnp.where(own_y > 0, early[before, cols_x : 2 * cols_x], 0.0)

    def neighbours(tile, index):
        row_a, row_b = (rows_a[index : index + 1, :], rows_b[index : index + 1, :])
        after_row, before_row = (jnp.where(even_x, row_a, row_b), jnp.where(even_x, row_b, row_a))
        return (
            jnp.where(high_x, after_row, pltpu.roll(tile, cols_x - 1, 0)),
            jnp.where(low_x, before_row, pltpu.roll(tile, 1, 0)),
            jnp.where(high_y, after_cols[:, index : index + 1], pltpu.roll(tile, rows_y - 1, 1)),
            jnp.where(low_y, before_cols[:, index : index + 1], pltpu.roll(tile, 1, 1)),
        )

    counts = wet[...].astype(jnp.float32)
    around = neighbours(counts, 4 * levels)
    shared = [jnp.minimum(counts, other) for other in around]
    both_x = jnp.minimum(shared[0], shared[1])
    both_y = jnp.minimum(shared[2], shared[3])
    zero = jnp.zeros(shape, jnp.float32)

    def laplacian(tile, others, level):
        total = zero
        for other, limit in zip(others, shared):
            total = total + jnp.where(limit > level, other - tile, 0.0)
        return total

    difference_x, difference_y = (zero, zero)
    for level in range(levels):
        weight = weights[level : level + 1, :]
        heat, salt = (tracers[0, level], tracers[1, level])
        heat_around = neighbours(heat, level)
        salt_around = neighbours(salt, levels + level)
        loads = [
            jnp.where(count > level, SALINITY_BETA * s - HEAT_ALPHA * t, 0.0)
            for count, s, t in zip(around, salt_around, heat_around)
        ]
        difference_x = difference_x + weight * (loads[0] - loads[1])
        difference_y = difference_y + weight * (loads[2] - loads[3])
        gradients[0, level] = jnp.where(both_x > level, difference_x * 0.5, 0.0)
        gradients[1, level] = jnp.where(both_y > level, difference_y * 0.5, 0.0)
        diffusivity = TIME_INCREMENT * KAPPA_SPREAD
        next_tracers[0, level] = heat + diffusivity * laplacian(heat, heat_around, level)
        next_tracers[1, level] = salt + diffusivity * laplacian(salt, salt_around, level)
    leaving = pltpu.make_async_copy(next_tracers, new_tracers, semaphore)
    leaving.start()

    coriolis = jnp.broadcast_to(latitude[...], shape)
    flow_x, flow_y = (zero, zero)
    for level in range(levels):
        here = counts > level
        weight = weights[level : level + 1, :]
        zonal, merid = (velocity[0, level], velocity[1, level])
        spread_x = laplacian(zonal, neighbours(zonal, 2 * levels + level), level)
        spread_y = laplacian(merid, neighbours(merid, 3 * levels + level), level)
        zonal_rate = coriolis * merid - gradients[0, level] + VISCOSITY * spread_x
        merid_rate = -coriolis * zonal - gradients[1, level] + VISCOSITY * spread_y
        next_zonal = zonal + jnp.where(here, TIME_INCREMENT * zonal_rate, 0.0)
        next_merid = merid + jnp.where(here, TIME_INCREMENT * merid_rate, 0.0)
        moved_velocity[0, level] = next_zonal
        moved_velocity[1, level] = next_merid
        flow_x = flow_x + jnp.where(here, weight * next_zonal, 0.0)
        flow_y = flow_y + jnp.where(here, weight * next_merid, 0.0)
    ahead = jnp.where(high_x, 0.0, pltpu.roll(flow_x, cols_x - 1, 0))
    behind = jnp.where(low_x, 0.0, pltpu.roll(flow_x, 1, 0))
    slope = ahead - behind
    ahead = jnp.where(high_y, 0.0, pltpu.roll(flow_y, rows_y - 1, 1))
    behind = jnp.where(low_y, 0.0, pltpu.roll(flow_y, 1, 1))
    inner = (slope + (ahead - behind)) * 0.5
    edge_x = flow_x * 0.5
    edge_y = flow_y * 0.5
    first = jnp.where(lane == sublane, edge_y[:, 0:1], 0.0)
    last = jnp.where(lane == sublane + cols_x, edge_y[:, rows_y - 1 : rows_y], 0.0)
    corner = jnp.sum(first + last, axis=0, keepdims=True)

    def place(target):
        surface[target, 0:cols_x, 0, :] = inner
        surface[target, cols_x : cols_x + 1, 0, :] = edge_x[0:1, :]
        surface[target, cols_x + 1 : cols_x + 2, 0, :] = edge_x[cols_x - 1 : cols_x, :]
        surface[target, cols_x + 2 : cols_x + 3, 0, :] = corner

    pl.loop(0, surface.shape[0], unroll=8)(place)
    leaving.wait()


def solve_kernel(
    blocks_x, blocks_y, gathered, early, moved_velocity, wet,
    new_velocity, pressure,
    residual, lifted_0, lifted_1, smooth_0, smooth_1, smooth_2, image_0, direction_1,
):
    levels, cols_x, rows_y = moved_velocity.shape[1:]
    shape = (cols_x, rows_y)
    lane, sublane = (lanes_of(shape), sublanes_of(shape))
    low_x, high_x = (sublane == 0, sublane == cols_x - 1)
    low_y, high_y = (lane == 0, lane == rows_y - 1)
    zero = jnp.zeros(shape, jnp.float32)

    def each_row(step, carry):
        if blocks_x <= 8:
            for row in range(blocks_x):
                carry = step(row, carry)
            return carry
        return lax.fori_loop(0, blocks_x, step, carry)

    def guarded(load, row, column):
        if isinstance(row, int):
            return load(row * blocks_y + column) if 0 <= row < blocks_x else 0.0
        inside = jnp.logical_and(row >= 0, row < blocks_x)
        return load(jnp.clip(row, 0, blocks_x - 1) * blocks_y + column) * inside.astype(jnp.float32)

    def along_x(load, row, column):
        tile = load(row * blocks_y + column)
        other = guarded(lambda i: load(i, slice(0, 1)), row + 1, column)
        after = jnp.where(high_x, other, pltpu.roll(tile, cols_x - 1, 0))
        other = guarded(lambda i: load(i, slice(cols_x - 1, cols_x)), row - 1, column)
        before = jnp.where(low_x, other, pltpu.roll(tile, 1, 0))
        return after + before

    def along_y(tiles):
        ahead = [pltpu.roll(tile, rows_y - 1, 1) for tile in tiles] + [0.0]
        behind = [0.0] + [pltpu.roll(tile, 1, 1) for tile in tiles]
        return [
            jnp.where(high_y, ahead[c + 1], ahead[c]) + jnp.where(low_y, behind[c], behind[c + 1])
            for c in range(blocks_y)
        ]

    def lift(inverse, tile):
        first = inverse * tile
        near = jnp.where(high_x, 0.0, pltpu.roll(first, cols_x - 1, 0))
        near = near + jnp.where(low_x, 0.0, pltpu.roll(first, 1, 0))
        near = near + jnp.where(high_y, 0.0, pltpu.roll(first, rows_y - 1, 1))
        near = near + jnp.where(low_y, 0.0, pltpu.roll(first, 1, 1))
        return tile + near

    def total(values):
        return jnp.sum(values, axis=(0, 1), keepdims=True)

    height = cols_x + 3

    def start_all():
        def rows_of(row, column, first, count):
            place = (row * blocks_y + column) * height + first
            return gathered[pl.ds(place, count), :]

        def edge_row(which, row, column):
            if isinstance(row, int):
                inside = 0 <= row < blocks_x
                return rows_of(row, column, cols_x + which, 1) if inside else 0.0
            inside = jnp.logical_and(row >= 0, row < blocks_x).astype(jnp.float32)
            row = jnp.clip(row, 0, blocks_x - 1)
            return rows_of(row, column, cols_x + which, 1) * inside

        def step(row, carry):
            corners = [rows_of(row, c, cols_x + 2, 1) for c in range(blocks_y)]
            filler = [jnp.zeros((1, rows_y), jnp.float32)] * (-blocks_y % 8)
            corners = jnp.transpose(jnp.concatenate(corners + filler, axis=0))
            for column in range(blocks_y):
                index = row * blocks_y + column
                forcing = rows_of(row, column, 0, cols_x)
                forcing = forcing + jnp.where(high_x, edge_row(0, row + 1, column), 0.0)
                forcing = forcing - jnp.where(low_x, edge_row(1, row - 1, column), 0.0)
                if column + 1 < blocks_y:
                    beyond = corners[0:cols_x, column + 1 : column + 2]
                    forcing = forcing + jnp.where(high_y, beyond, 0.0)
                if column > 0:
                    beyond = corners[cols_x : 2 * cols_x, column - 1 : column]
                    forcing = forcing - jnp.where(low_y, beyond, 0.0)
                inverse = early[index, 0:cols_x]
                lifted = lift(inverse, forcing)
                residual[index] = forcing
                lifted_0[index] = lifted
                smooth_0[index] = inverse * lifted
            return carry

        each_row(step, 0)

    def operate(lifted, smooth, image):
        def load(index, rows=slice(None)):
            return smooth[index, rows]

        def step(row, carry):
            inner, curvature = carry
            tiles = [smooth[row * blocks_y + c] for c in range(blocks_y)]
            beside = along_y(tiles)
            for column in range(blocks_y):
                index = row * blocks_y + column
                result = lifted[index] - (along_x(load, row, column) + beside[column])
                if image is not None:
                    image[index] = result
                inner = inner + residual[index] * tiles[column]
                curvature = curvature + tiles[column] * result
            return inner, curvature

        inner, curvature = each_row(step, (zero, zero))
        return total(inner), total(curvature)

    start_all()
    inner_0, curvature_0 = operate(lifted_0, smooth_0, image_0)
    step_0 = inner_0 / curvature_0

    def advance_0(row, carry):
        for column in range(blocks_y):
            index = row * blocks_y + column
            left = residual[index] - step_0 * image_0[index]
            inverse = early[index, 0:cols_x]
            lifted = lift(inverse, left)
            residual[index] = left
            lifted_1[index] = lifted
            smooth_1[index] = inverse * lifted
        return carry

    each_row(advance_0, 0)
    image_1 = lifted_1
    inner_1, curvature_1 = operate(lifted_1, smooth_1, image_1)
    turn_1 = inner_1 / inner_0
    step_1 = inner_1 / (curvature_1 - turn_1 * inner_1 / step_0)

    def advance_1(row, carry):
        for column in range(blocks_y):
            index = row * blocks_y + column
            direction_1[index] = smooth_1[index] + turn_1 * smooth_0[index]
            left = residual[index] - step_1 * (image_1[index] + turn_1 * image_0[index])
            inverse = early[index, 0:cols_x]
            lifted = lift(inverse, left)
            residual[index] = left
            lifted_0[index] = lifted
            smooth_2[index] = inverse * lifted
        return carry

    each_row(advance_1, 0)
    inner_2, curvature_2 = operate(lifted_0, smooth_2, None)
    turn_2 = inner_2 / inner_1
    step_2 = inner_2 / (curvature_2 - turn_2 * inner_2 / step_1)

    def iterate(index):
        previous = direction_1[index]
        result = step_0 * smooth_0[index] + step_1 * previous
        return result + step_2 * (smooth_2[index] + turn_2 * previous)

    own_x, own_y = (position_x(), lax.axis_index("by"))

    def block(shift_x, shift_y):
        row, column = (own_x + shift_x, own_y + shift_y)
        inside = (row >= 0) & (row < blocks_x) & (column >= 0) & (column < blocks_y)
        row, column = (jnp.clip(row, 0, blocks_x - 1), jnp.clip(column, 0, blocks_y - 1))
        return jnp.where(inside, iterate(row * blocks_y + column), 0.0)

    own = iterate(own_x * blocks_y + own_y)
    pressure[...] = own
    upper = jnp.where(high_x, pltpu.roll(block(1, 0), cols_x - 1, 0), pltpu.roll(own, cols_x - 1, 0))
    lower = jnp.where(low_x, pltpu.roll(block(-1, 0), 1, 0), pltpu.roll(own, 1, 0))
    slope_x = GRAVITY * ((upper - lower) * 0.5)
    upper = jnp.where(high_y, pltpu.roll(block(0, 1), rows_y - 1, 1), pltpu.roll(own, rows_y - 1, 1))
    lower = jnp.where(low_y, pltpu.roll(block(0, -1), 1, 1), pltpu.roll(own, 1, 1))
    slope_y = GRAVITY * ((upper - lower) * 0.5)
    counts = wet[...]
    for level in range(levels):
        here = counts > level
        new_velocity[0, level] = moved_velocity[0, level] - jnp.where(here, slope_x, 0.0)
        new_velocity[1, level] = moved_velocity[1, level] - jnp.where(here, slope_y, 0.0)


def latitude_rate(positions, total_rows):
    return 1.5 * jnp.sin(math.pi * ((positions + 0.5) / total_rows - 0.5))


def body(tracers, velocity, wet_levels, thickness, diagonal):
    levels = tracers.shape[1]
    cols_x, rows_y = wet_levels.shape
    chips_z, cores, blocks_y = (lax.axis_size("z"), lax.axis_size("core"), lax.axis_size("by"))
    blocks_x = chips_z * cores
    shape = (cols_x, rows_y)
    height = cols_x + 3
    blocks = blocks_x * blocks_y
    rim_rows = 4 * levels + 1

    def like(*dims):
        return jax.ShapeDtypeStruct(dims, jnp.float32)

    def held(*dims):
        return pltpu.VMEM(dims, jnp.float32) if math.prod(dims) <= HELD_SIZE else like(*dims)

    def kept(array):
        if array.size > HELD_SIZE:
            return array
        return pltpu.with_memory_space_constraint(array, pltpu.VMEM)

    fields = (tracers, velocity, wet_levels, diagonal, thickness)
    rows_a, rows_b, early, *block = pl.pallas_call(
        pack_rims,
        out_shape=[
            held(rim_rows, rows_y), held(rim_rows, rows_y), held(blocks, 2 * cols_x, rows_y),
            held(*tracers.shape), held(*velocity.shape), pltpu.VMEM(shape, wet_levels.dtype),
            held(levels, rows_y),
        ],
        in_specs=[ANY] * 5,
        out_specs=[VMEM] * 7,
        scratch_shapes=[pltpu.VMEM(shape, jnp.float32), pltpu.SMEM(thickness.shape, jnp.float32), pltpu.SemaphoreType.DMA((5,))],
    )(*(pltpu.with_memory_space_constraint(array, pltpu.HBM) for array in fields))
    block = [kept(array) for array in block]

    def exchange(message, first):
        pairs = [(i, i + 1) for i in range(first, blocks_x - 1, 2)]
        return lax.ppermute(message, ("z", "core"), pairs + [(j, i) for i, j in pairs])

    everywhere = ("z", "core", "by")
    early = lax.all_to_all(early, everywhere, split_axis=0, concat_axis=0, tiled=True)
    rows_b, rows_a = (exchange(rows_b, 1), exchange(rows_a, 0))
    positions = (lax.axis_index("by") * rows_y + jnp.arange(rows_y, dtype=jnp.int32)).astype(jnp.float32)
    latitude = latitude_rate(positions, blocks_y * rows_y)[None]

    new_tracers, moved_velocity, surface = pl.pallas_call(
        level_kernel,
        out_shape=[
            like(*tracers.shape), held(*velocity.shape),
            held(blocks, height, 1, rows_y),
        ],
        in_specs=[VMEM] * 8,
        out_specs=[ANY, VMEM, VMEM],
        scratch_shapes=[
            pltpu.VMEM(tracers.shape, jnp.float32),
            pltpu.VMEM((2, levels, *shape), jnp.float32),
            pltpu.SemaphoreType.DMA,
        ],
    )(*block, kept(latitude), kept(rows_b), kept(rows_a), kept(early))

    gathered = lax.all_to_all(surface, everywhere, split_axis=0, concat_axis=0, tiled=True)
    gathered = gathered.reshape(-1, rows_y)

    def solve(*refs):
        solve_kernel(blocks_x, blocks_y, *refs)

    new_velocity, pressure = pl.pallas_call(
        solve,
        out_shape=[like(*velocity.shape), like(*shape)],
        in_specs=[VMEM] * 4,
        out_specs=[VMEM] * 2,
        scratch_shapes=[pltpu.VMEM((blocks, *shape), jnp.float32)] * 8,
        compiler_params=pltpu.CompilerParams(vmem_limit_bytes=(4 + 52 * blocks // 1024) * 2**20),
    )(kept(gathered), kept(early), kept(moved_velocity), block[2])
    return new_tracers, new_velocity, pressure


def solution(mesh):
    size_x, size_y = (mesh.shape["bx"], mesh.shape["by"])
    chips = jax.sharding.Mesh(mesh.devices.reshape(size_x // 2, 2, size_y), ("z", "core", "by"))
    along_x = ("z", "core")
    placed = (
        P(None, None, along_x, "by"),
        P(None, None, along_x, "by"),
        P(along_x, "by"),
        P(),
        P(along_x, None),
    )
    return jax.shard_map(
        body,
        mesh=chips,
        in_specs=placed,
        out_specs=(P(None, None, along_x, "by"), P(None, None, along_x, "by"), P(along_x, "by")),
        check_vma=False,
    )
```

```python
import math

import jax
import jax.numpy as jnp
from jax import lax
from jax.experimental import pallas as pl
from jax.experimental.pallas import tpu as pltpu
from jax.sharding import PartitionSpec as P

ITERS = 3

HEAT_ALPHA = 0.5
SALINITY_BETA = 0.8
KAPPA_SPREAD = 0.15
VISCOSITY = 0.1
TIME_INCREMENT = 0.2
GRAVITY = 1.0

HELD_SIZE = 2**18

VMEM = pl.BlockSpec(memory_space=pltpu.VMEM)
ANY = pl.BlockSpec(memory_space=pl.ANY)


def lanes_of(shape):
    return lax.broadcasted_iota(jnp.int32, shape, 1)


def sublanes_of(shape):
    return lax.broadcasted_iota(jnp.int32, shape, 0)


def position_x():
    return lax.axis_index("z") * lax.axis_size("core") + lax.axis_index("core")


def pack_rims(
    tracers_in, velocity_in, wet_in, diagonal_in, thickness_in,
    rows_a, rows_b, cols_a, cols_b, tracers, velocity, wet, diagonal, weights,
    thickness, semaphores,
):
    levels, cols_x, rows_y = tracers.shape[1:]
    row_start = pl.multiple_of(lax.axis_index("by") * rows_y, rows_y)
    copies = [
        pltpu.make_async_copy(source, target, semaphores.at[number])
        for number, (source, target) in enumerate((
            (tracers_in, tracers),
            (velocity_in, velocity),
            (wet_in, wet),
            (thickness_in, thickness),
            (diagonal_in.at[:, pl.ds(row_start, rows_y)], diagonal),
        ))
    ]
    for copy in copies:
        copy.start()
    even_x, even_y = (lax.axis_index("core") == 0, lax.axis_index("by") % 2 == 0)
    lane = lanes_of((cols_x, rows_y))
    for copy in copies:
        copy.wait()
    for level in range(levels):
        weights[level : level + 1, :] = jnp.full((1, rows_y), thickness[level], jnp.float32)
    counts = wet[...].astype(jnp.float32)
    first, last = jnp.zeros_like(counts), jnp.zeros_like(counts)
    for index in range(4 * levels + 1):
        field, level = divmod(index, levels)
        if field < 4:
            tile = (tracers if field < 2 else velocity)[field % 2, level]
        else:
            tile = counts
        top, bottom = (tile[0:1, :], tile[cols_x - 1 : cols_x, :])
        rows_a[index : index + 1, :] = jnp.where(even_x, bottom, top)
        rows_b[index : index + 1, :] = jnp.where(even_x, top, bottom)
        first = jnp.where(lane == index, tile[:, 0:1], first)
        last = jnp.where(lane == index, tile[:, rows_y - 1 : rows_y], last)
    cols_a[...] = jnp.where(even_y, last, first)
    cols_b[...] = jnp.where(even_y, first, last)


def level_kernel(
    tracers, velocity, wet, diagonal, weights, latitude, rows_b, rows_a, cols_b, cols_a,
    new_tracers, moved_velocity, surface,
    next_tracers, gradients, semaphore,
):
    levels, cols_x, rows_y = tracers.shape[1:]
    shape = (cols_x, rows_y)
    lane, sublane = (lanes_of(shape), sublanes_of(shape))
    low_x, high_x = (sublane == 0, sublane == cols_x - 1)
    low_y, high_y = (lane == 0, lane == rows_y - 1)
    even_x, even_y = (lax.axis_index("core") == 0, lax.axis_index("by") % 2 == 0)
    after_cols = jnp.where(even_y, cols_a[...], cols_b[...])
    before_cols = jnp.where(even_y, cols_b[...], cols_a[...])

    def neighbours(tile, index):
        row_a, row_b = (rows_a[index : index + 1, :], rows_b[index : index + 1, :])
        after_row, before_row = (jnp.where(even_x, row_a, row_b), jnp.where(even_x, row_b, row_a))
        return (
            jnp.where(high_x, after_row, pltpu.roll(tile, cols_x - 1, 0)),
            jnp.where(low_x, before_row, pltpu.roll(tile, 1, 0)),
            jnp.where(high_y, after_cols[:, index : index + 1], pltpu.roll(tile, rows_y - 1, 1)),
            jnp.where(low_y, before_cols[:, index : index + 1], pltpu.roll(tile, 1, 1)),
        )

    counts = wet[...].astype(jnp.float32)
    around = neighbours(counts, 4 * levels)
    shared = [jnp.minimum(counts, other) for other in around]
    both_x = jnp.minimum(shared[0], shared[1])
    both_y = jnp.minimum(shared[2], shared[3])
    zero = jnp.zeros(shape, jnp.float32)

    def laplacian(tile, others, level):
        total = zero
        for other, limit in zip(others, shared):
            total = total + jnp.where(limit > level, other - tile, 0.0)
        return total

    difference_x, difference_y = (zero, zero)
    for level in range(levels):
        weight = weights[level : level + 1, :]
        heat, salt = (tracers[0, level], tracers[1, level])
        heat_around = neighbours(heat, level)
        salt_around = neighbours(salt, levels + level)
        loads = [
            jnp.where(count > level, SALINITY_BETA * s - HEAT_ALPHA * t, 0.0)
            for count, s, t in zip(around, salt_around, heat_around)
        ]
        difference_x = difference_x + weight * (loads[0] - loads[1])
        difference_y = difference_y + weight * (loads[2] - loads[3])
        gradients[0, level] = jnp.where(both_x > level, difference_x * 0.5, 0.0)
        gradients[1, level] = jnp.where(both_y > level, difference_y * 0.5, 0.0)
        diffusivity = TIME_INCREMENT * KAPPA_SPREAD
        next_tracers[0, level] = heat + diffusivity * laplacian(heat, heat_around, level)
        next_tracers[1, level] = salt + diffusivity * laplacian(salt, salt_around, level)
    leaving = pltpu.make_async_copy(next_tracers, new_tracers, semaphore)
    leaving.start()

    coriolis = jnp.broadcast_to(latitude[...], shape)
    flow_x, flow_y = (zero, zero)
    for level in range(levels):
        here = counts > level
        weight = weights[level : level + 1, :]
        zonal, merid = (velocity[0, level], velocity[1, level])
        spread_x = laplacian(zonal, neighbours(zonal, 2 * levels + level), level)
        spread_y = laplacian(merid, neighbours(merid, 3 * levels + level), level)
        zonal_rate = coriolis * merid - gradients[0, level] + VISCOSITY * spread_x
        merid_rate = -coriolis * zonal - gradients[1, level] + VISCOSITY * spread_y
        next_zonal = zonal + jnp.where(here, TIME_INCREMENT * zonal_rate, 0.0)
        next_merid = merid + jnp.where(here, TIME_INCREMENT * merid_rate, 0.0)
        moved_velocity[0, level] = next_zonal
        moved_velocity[1, level] = next_merid
        flow_x = flow_x + jnp.where(here, weight * next_zonal, 0.0)
        flow_y = flow_y + jnp.where(here, weight * next_merid, 0.0)
    inverse = jnp.where(counts > 0, 1.0, 0.0) / (4.0 + diagonal[...])
    ahead = jnp.where(high_x, 0.0, pltpu.roll(flow_x, cols_x - 1, 0))
    behind = jnp.where(low_x, 0.0, pltpu.roll(flow_x, 1, 0))
    slope = ahead - behind
    ahead = jnp.where(high_y, 0.0, pltpu.roll(flow_y, rows_y - 1, 1))
    behind = jnp.where(low_y, 0.0, pltpu.roll(flow_y, 1, 1))
    inner = (slope + (ahead - behind)) * 0.5
    edge_x = flow_x * 0.5
    edge_y = flow_y * 0.5
    first = jnp.where(lane == sublane, edge_y[:, 0:1], 0.0)
    last = jnp.where(lane == sublane + cols_x, edge_y[:, rows_y - 1 : rows_y], 0.0)
    corner = jnp.sum(first + last, axis=0, keepdims=True)

    def place(target):
        surface[target, 0:cols_x, 0, :] = inner
        surface[target, cols_x : 2 * cols_x, 0, :] = inverse
        surface[target, 2 * cols_x : 2 * cols_x + 1, 0, :] = edge_x[0:1, :]
        surface[target, 2 * cols_x + 1 : 2 * cols_x + 2, 0, :] = edge_x[cols_x - 1 : cols_x, :]
        surface[target, 2 * cols_x + 2 : 2 * cols_x + 3, 0, :] = corner

    pl.loop(0, surface.shape[0], unroll=8)(place)
    leaving.wait()


def solve_kernel(
    blocks_x, blocks_y, gathered, moved_velocity, wet,
    new_velocity, pressure,
    residual, inverses, lifted_0, lifted_1, smooth_0, smooth_1, smooth_2, image_0, direction_1,
):
    levels, cols_x, rows_y = moved_velocity.shape[1:]
    shape = (cols_x, rows_y)
    lane, sublane = (lanes_of(shape), sublanes_of(shape))
    low_x, high_x = (sublane == 0, sublane == cols_x - 1)
    low_y, high_y = (lane == 0, lane == rows_y - 1)
    zero = jnp.zeros(shape, jnp.float32)

    def each_row(step, carry):
        if blocks_x <= 8:
            for row in range(blocks_x):
                carry = step(row, carry)
            return carry
        return lax.fori_loop(0, blocks_x, step, carry)

    def guarded(load, row, column):
        if isinstance(row, int):
            return load(row * blocks_y + column) if 0 <= row < blocks_x else 0.0
        inside = jnp.logical_and(row >= 0, row < blocks_x)
        return load(jnp.clip(row, 0, blocks_x - 1) * blocks_y + column) * inside.astype(jnp.float32)

    def along_x(load, row, column):
        tile = load(row * blocks_y + column)
        other = guarded(lambda i: load(i, slice(0, 1)), row + 1, column)
        after = jnp.where(high_x, other, pltpu.roll(tile, cols_x - 1, 0))
        other = guarded(lambda i: load(i, slice(cols_x - 1, cols_x)), row - 1, column)
        before = jnp.where(low_x, other, pltpu.roll(tile, 1, 0))
        return after + before

    def along_y(tiles):
        ahead = [pltpu.roll(tile, rows_y - 1, 1) for tile in tiles] + [0.0]
        behind = [0.0] + [pltpu.roll(tile, 1, 1) for tile in tiles]
        return [
            jnp.where(high_y, ahead[c + 1], ahead[c]) + jnp.where(low_y, behind[c], behind[c + 1])
            for c in range(blocks_y)
        ]

    def lift(inverse, tile):
        first = inverse * tile
        near = jnp.where(high_x, 0.0, pltpu.roll(first, cols_x - 1, 0))
        near = near + jnp.where(low_x, 0.0, pltpu.roll(first, 1, 0))
        near = near + jnp.where(high_y, 0.0, pltpu.roll(first, rows_y - 1, 1))
        near = near + jnp.where(low_y, 0.0, pltpu.roll(first, 1, 1))
        return tile + near

    def total(values):
        return jnp.sum(values, axis=(0, 1), keepdims=True)

    height = 2 * cols_x + 3

    def start_all():
        def rows_of(row, column, first, count):
            place = (row * blocks_y + column) * height + first
            return gathered[pl.ds(place, count), :]

        def edge_row(which, row, column):
            if isinstance(row, int):
                inside = 0 <= row < blocks_x
                return rows_of(row, column, 2 * cols_x + which, 1) if inside else 0.0
            inside = jnp.logical_and(row >= 0, row < blocks_x).astype(jnp.float32)
            row = jnp.clip(row, 0, blocks_x - 1)
            return rows_of(row, column, 2 * cols_x + which, 1) * inside

        def step(row, carry):
            corners = [rows_of(row, c, 2 * cols_x + 2, 1) for c in range(blocks_y)]
            filler = [jnp.zeros((1, rows_y), jnp.float32)] * (-blocks_y % 8)
            corners = jnp.transpose(jnp.concatenate(corners + filler, axis=0))
            for column in range(blocks_y):
                index = row * blocks_y + column
                forcing = rows_of(row, column, 0, cols_x)
                forcing = forcing + jnp.where(high_x, edge_row(0, row + 1, column), 0.0)
                forcing = forcing - jnp.where(low_x, edge_row(1, row - 1, column), 0.0)
                if column + 1 < blocks_y:
                    beyond = corners[0:cols_x, column + 1 : column + 2]
                    forcing = forcing + jnp.where(high_y, beyond, 0.0)
                if column > 0:
                    beyond = corners[cols_x : 2 * cols_x, column - 1 : column]
                    forcing = forcing - jnp.where(low_y, beyond, 0.0)
                inverse = rows_of(row, column, cols_x, cols_x)
                lifted = lift(inverse, forcing)
                inverses[index] = inverse
                residual[index] = forcing
                lifted_0[index] = lifted
                smooth_0[index] = inverse * lifted
            return carry

        each_row(step, 0)

    def operate(lifted, smooth, image):
        def load(index, rows=slice(None)):
            return smooth[index, rows]

        def step(row, carry):
            inner, curvature = carry
            tiles = [smooth[row * blocks_y + c] for c in range(blocks_y)]
            beside = along_y(tiles)
            for column in range(blocks_y):
                index = row * blocks_y + column
                result = lifted[index] - (along_x(load, row, column) + beside[column])
                if image is not None:
                    image[index] = result
                inner = inner + residual[index] * tiles[column]
                curvature = curvature + tiles[column] * result
            return inner, curvature

        inner, curvature = each_row(step, (zero, zero))
        return total(inner), total(curvature)

    start_all()
    inner_0, curvature_0 = operate(lifted_0, smooth_0, image_0)
    step_0 = inner_0 / curvature_0

    def advance_0(row, carry):
        for column in range(blocks_y):
            index = row * blocks_y + column
            left = residual[index] - step_0 * image_0[index]
            inverse = inverses[index]
            lifted = lift(inverse, left)
            residual[index] = left
            lifted_1[index] = lifted
            smooth_1[index] = inverse * lifted
        return carry

    each_row(advance_0, 0)
    image_1 = lifted_1
    inner_1, curvature_1 = operate(lifted_1, smooth_1, image_1)
    turn_1 = inner_1 / inner_0
    step_1 = inner_1 / (curvature_1 - turn_1 * inner_1 / step_0)

    def advance_1(row, carry):
        for column in range(blocks_y):
            index = row * blocks_y + column
            direction_1[index] = smooth_1[index] + turn_1 * smooth_0[index]
            left = residual[index] - step_1 * (image_1[index] + turn_1 * image_0[index])
            inverse = inverses[index]
            lifted = lift(inverse, left)
            residual[index] = left
            lifted_0[index] = lifted
            smooth_2[index] = inverse * lifted
        return carry

    each_row(advance_1, 0)
    inner_2, curvature_2 = operate(lifted_0, smooth_2, None)
    turn_2 = inner_2 / inner_1
    step_2 = inner_2 / (curvature_2 - turn_2 * inner_2 / step_1)

    def iterate(index):
        previous = direction_1[index]
        result = step_0 * smooth_0[index] + step_1 * previous
        return result + step_2 * (smooth_2[index] + turn_2 * previous)

    own_x, own_y = (position_x(), lax.axis_index("by"))

    def block(shift_x, shift_y):
        row, column = (own_x + shift_x, own_y + shift_y)
        inside = (row >= 0) & (row < blocks_x) & (column >= 0) & (column < blocks_y)
        row, column = (jnp.clip(row, 0, blocks_x - 1), jnp.clip(column, 0, blocks_y - 1))
        return jnp.where(inside, iterate(row * blocks_y + column), 0.0)

    own = iterate(own_x * blocks_y + own_y)
    pressure[...] = own
    upper = jnp.where(high_x, pltpu.roll(block(1, 0), cols_x - 1, 0), pltpu.roll(own, cols_x - 1, 0))
    lower = jnp.where(low_x, pltpu.roll(block(-1, 0), 1, 0), pltpu.roll(own, 1, 0))
    slope_x = GRAVITY * ((upper - lower) * 0.5)
    upper = jnp.where(high_y, pltpu.roll(block(0, 1), rows_y - 1, 1), pltpu.roll(own, rows_y - 1, 1))
    lower = jnp.where(low_y, pltpu.roll(block(0, -1), 1, 1), pltpu.roll(own, 1, 1))
    slope_y = GRAVITY * ((upper - lower) * 0.5)
    counts = wet[...]
    for level in range(levels):
        here = counts > level
        new_velocity[0, level] = moved_velocity[0, level] - jnp.where(here, slope_x, 0.0)
        new_velocity[1, level] = moved_velocity[1, level] - jnp.where(here, slope_y, 0.0)


def latitude_rate(positions, total_rows):
    return 1.5 * jnp.sin(math.pi * ((positions + 0.5) / total_rows - 0.5))


def body(tracers, velocity, wet_levels, thickness, diagonal):
    levels = tracers.shape[1]
    cols_x, rows_y = wet_levels.shape
    chips_z, cores, blocks_y = (lax.axis_size("z"), lax.axis_size("core"), lax.axis_size("by"))
    blocks_x = chips_z * cores
    shape = (cols_x, rows_y)
    height = 2 * cols_x + 3
    blocks = blocks_x * blocks_y
    rim_rows = 4 * levels + 1

    def like(*dims):
        return jax.ShapeDtypeStruct(dims, jnp.float32)

    def held(*dims):
        return pltpu.VMEM(dims, jnp.float32) if math.prod(dims) <= HELD_SIZE else like(*dims)

    def kept(array):
        if array.size > HELD_SIZE:
            return array
        return pltpu.with_memory_space_constraint(array, pltpu.VMEM)

    fields = (tracers, velocity, wet_levels, diagonal, thickness)
    rows_a, rows_b, cols_a, cols_b, *block = pl.pallas_call(
        pack_rims,
        out_shape=[
            held(rim_rows, rows_y), held(rim_rows, rows_y), held(*shape), held(*shape),
            held(*tracers.shape), held(*velocity.shape), pltpu.VMEM(shape, wet_levels.dtype),
            held(*shape), held(levels, rows_y),
        ],
        in_specs=[ANY] * 5,
        out_specs=[VMEM] * 9,
        scratch_shapes=[pltpu.SMEM(thickness.shape, jnp.float32), pltpu.SemaphoreType.DMA((5,))],
    )(*(pltpu.with_memory_space_constraint(array, pltpu.HBM) for array in fields))
    block = [kept(array) for array in block]

    def exchange(message, axis, first):
        size = blocks_x if axis == "bx" else blocks_y
        pairs = [(i, i + 1) for i in range(first, size - 1, 2)]
        axes = ("z", "core") if axis == "bx" else axis
        return lax.ppermute(message, axes, pairs + [(j, i) for i, j in pairs])

    rows_b, rows_a = (exchange(rows_b, "bx", 1), exchange(rows_a, "bx", 0))
    cols_b, cols_a = (exchange(cols_b, "by", 1), exchange(cols_a, "by", 0))
    positions = (lax.axis_index("by") * rows_y + jnp.arange(rows_y, dtype=jnp.int32)).astype(jnp.float32)
    latitude = latitude_rate(positions, blocks_y * rows_y)[None]

    new_tracers, moved_velocity, surface = pl.pallas_call(
        level_kernel,
        out_shape=[
            like(*tracers.shape), held(*velocity.shape),
            held(blocks, height, 1, rows_y),
        ],
        in_specs=[VMEM] * 10,
        out_specs=[ANY, VMEM, VMEM],
        scratch_shapes=[
            pltpu.VMEM(tracers.shape, jnp.float32),
            pltpu.VMEM((2, levels, *shape), jnp.float32),
            pltpu.SemaphoreType.DMA,
        ],
    )(*block, kept(latitude), kept(rows_b), kept(rows_a), kept(cols_b), kept(cols_a))

    gathered = lax.all_to_all(surface, ("z", "core", "by"), split_axis=0, concat_axis=0, tiled=True)
    gathered = gathered.reshape(-1, rows_y)

    def solve(*refs):
        solve_kernel(blocks_x, blocks_y, *refs)

    new_velocity, pressure = pl.pallas_call(
        solve,
        out_shape=[like(*velocity.shape), like(*shape)],
        in_specs=[VMEM] * 3,
        out_specs=[VMEM] * 2,
        scratch_shapes=[pltpu.VMEM((blocks, *shape), jnp.float32)] * 9,
        compiler_params=pltpu.CompilerParams(vmem_limit_bytes=(4 + 52 * blocks // 1024) * 2**20),
    )(kept(gathered), kept(moved_velocity), block[2])
    return new_tracers, new_velocity, pressure


def solution(mesh):
    size_x, size_y = (mesh.shape["bx"], mesh.shape["by"])
    chips = jax.sharding.Mesh(mesh.devices.reshape(size_x // 2, 2, size_y), ("z", "core", "by"))
    along_x = ("z", "core")
    placed = (
        P(None, None, along_x, "by"),
        P(None, None, along_x, "by"),
        P(along_x, "by"),
        P(),
        P(along_x, None),
    )
    return jax.shard_map(
        body,
        mesh=chips,
        in_specs=placed,
        out_specs=(P(None, None, along_x, "by"), P(None, None, along_x, "by"), P(along_x, "by")),
        check_vma=False,
    )
```

```python
import math

import jax
import jax.numpy as jnp
from jax import lax
from jax.experimental import pallas as pl
from jax.experimental.pallas import tpu as pltpu
from jax.sharding import PartitionSpec as P

ITERS = 3

HEAT_ALPHA = 0.5
SALINITY_BETA = 0.8
KAPPA_SPREAD = 0.15
VISCOSITY = 0.1
TIME_INCREMENT = 0.2
GRAVITY = 1.0

HELD_SIZE = 2**18

VMEM = pl.BlockSpec(memory_space=pltpu.VMEM)
ANY = pl.BlockSpec(memory_space=pl.ANY)


def lanes_of(shape):
    return lax.broadcasted_iota(jnp.int32, shape, 1)


def sublanes_of(shape):
    return lax.broadcasted_iota(jnp.int32, shape, 0)


def position_x():
    return lax.axis_index("z") * lax.axis_size("core") + lax.axis_index("core")


def pack_rims(
    tracers_in, velocity_in, wet_in, diagonal_in, thickness_in,
    rows_a, rows_b, cols_a, cols_b, tracers, velocity, wet, diagonal, weights,
    thickness, semaphores,
):
    levels, cols_x, rows_y = tracers.shape[1:]
    row_start = pl.multiple_of(lax.axis_index("by") * rows_y, rows_y)
    copies = [
        pltpu.make_async_copy(source, target, semaphores.at[number])
        for number, (source, target) in enumerate((
            (tracers_in, tracers),
            (velocity_in, velocity),
            (wet_in, wet),
            (thickness_in, thickness),
            (diagonal_in.at[:, pl.ds(row_start, rows_y)], diagonal),
        ))
    ]
    for copy in copies:
        copy.start()
    even_x, even_y = (lax.axis_index("core") == 0, lax.axis_index("by") % 2 == 0)
    lane = lanes_of((cols_x, rows_y))
    for copy in copies:
        copy.wait()
    for level in range(levels):
        weights[level : level + 1, :] = jnp.full((1, rows_y), thickness[level], jnp.float32)
    counts = wet[...].astype(jnp.float32)
    first, last = jnp.zeros_like(counts), jnp.zeros_like(counts)
    for index in range(4 * levels + 1):
        field, level = divmod(index, levels)
        if field < 4:
            tile = (tracers if field < 2 else velocity)[field % 2, level]
        else:
            tile = counts
        top, bottom = (tile[0:1, :], tile[cols_x - 1 : cols_x, :])
        rows_a[index : index + 1, :] = jnp.where(even_x, bottom, top)
        rows_b[index : index + 1, :] = jnp.where(even_x, top, bottom)
        first = jnp.where(lane == index, tile[:, 0:1], first)
        last = jnp.where(lane == index, tile[:, rows_y - 1 : rows_y], last)
    cols_a[...] = jnp.where(even_y, last, first)
    cols_b[...] = jnp.where(even_y, first, last)


def edges_of(shape):
    sublane, lane = (sublanes_of(shape), lanes_of(shape))
    return sublane == 0, sublane == shape[0] - 1, lane == 0, lane == shape[1] - 1


def neighbours_of(tile, after_row, before_row, after_col, before_col):
    low_x, high_x, low_y, high_y = edges_of(tile.shape)
    cols_x, rows_y = tile.shape
    return (
        jnp.where(high_x, after_row, pltpu.roll(tile, cols_x - 1, 0)),
        jnp.where(low_x, before_row, pltpu.roll(tile, 1, 0)),
        jnp.where(high_y, after_col, pltpu.roll(tile, rows_y - 1, 1)),
        jnp.where(low_y, before_col, pltpu.roll(tile, 1, 1)),
    )


def laplacian(tile, others, shared, level):
    total = jnp.zeros_like(tile)
    for other, limit in zip(others, shared):
        total = total + jnp.where(limit > level, other - tile, 0.0)
    return total


def side_columns(cols_b, cols_a):
    even_y = lax.axis_index("by") % 2 == 0
    a, b = (cols_a[...], cols_b[...])
    return jnp.where(even_y, a, b), jnp.where(even_y, b, a)


def level_kernel(
    tracers, velocity, wet, weights, latitude, cols_b, cols_a, rows_a,
    moved_velocity, flows, inner,
):
    levels, cols_x, rows_y = tracers.shape[1:]
    shape = (cols_x, rows_y)
    even_x = lax.axis_index("core") == 0
    after_cols, before_cols = side_columns(cols_b, cols_a)

    def neighbours(tile, index):
        row = rows_a[index : index + 1, :]
        after_row, before_row = (jnp.where(even_x, row, 0.0), jnp.where(even_x, 0.0, row))
        sides = (after_cols[:, index : index + 1], before_cols[:, index : index + 1])
        return neighbours_of(tile, after_row, before_row, *sides)

    counts = wet[...].astype(jnp.float32)
    around = neighbours(counts, 4 * levels)
    shared = [jnp.minimum(counts, other) for other in around]
    both_x = jnp.minimum(shared[0], shared[1])
    both_y = jnp.minimum(shared[2], shared[3])
    zero = jnp.zeros(shape, jnp.float32)
    coriolis = jnp.broadcast_to(latitude[...], shape)
    difference_x, difference_y, flow_x, flow_y = (zero, zero, zero, zero)
    for level in range(levels):
        here = counts > level
        weight = weights[level : level + 1, :]
        heat_around = neighbours(tracers[0, level], level)
        salt_around = neighbours(tracers[1, level], levels + level)
        loads = [
            jnp.where(count > level, SALINITY_BETA * s - HEAT_ALPHA * t, 0.0)
            for count, s, t in zip(around, salt_around, heat_around)
        ]
        difference_x = difference_x + weight * (loads[0] - loads[1])
        difference_y = difference_y + weight * (loads[2] - loads[3])
        inner[level : level + 1, :] = jnp.where(
            even_x, difference_x[0:1, :], difference_x[cols_x - 1 : cols_x, :]
        )
        gradient_x = jnp.where(both_x > level, difference_x * 0.5, 0.0)
        gradient_y = jnp.where(both_y > level, difference_y * 0.5, 0.0)
        zonal, merid = (velocity[0, level], velocity[1, level])
        spread_x = laplacian(zonal, neighbours(zonal, 2 * levels + level), shared, level)
        spread_y = laplacian(merid, neighbours(merid, 3 * levels + level), shared, level)
        zonal_rate = coriolis * merid - gradient_x + VISCOSITY * spread_x
        merid_rate = -coriolis * zonal - gradient_y + VISCOSITY * spread_y
        next_zonal = zonal + jnp.where(here, TIME_INCREMENT * zonal_rate, 0.0)
        next_merid = merid + jnp.where(here, TIME_INCREMENT * merid_rate, 0.0)
        moved_velocity[0, level] = next_zonal
        moved_velocity[1, level] = next_merid
        flow_x = flow_x + jnp.where(here, weight * next_zonal, 0.0)
        flow_y = flow_y + jnp.where(here, weight * next_merid, 0.0)
    flows[0] = flow_x
    flows[1] = flow_y


def edge_kernel(
    own, across, inner, weights, wet, diagonal, flows,
    surface, change,
):
    levels = weights.shape[0]
    cols_x, rows_y = shape = wet.shape
    low_x, high_x, low_y, high_y = edges_of(shape)
    lane, sublane = (lanes_of(shape), sublanes_of(shape))
    even_x = lax.axis_index("core") == 0
    sign = jnp.where(even_x, -1.0, 1.0)
    counts = wet[...].astype(jnp.float32)
    within = jnp.where(even_x, counts[1:2, :], counts[cols_x - 2 : cols_x - 1, :])
    count = across[4 * levels : 4 * levels + 1, :]
    shared = jnp.minimum(count, own[4 * levels : 4 * levels + 1, :])
    both = jnp.minimum(shared, within)
    pressure = jnp.zeros((1, rows_y), jnp.float32)
    added_x, added_y = (pressure, pressure)
    for level in range(levels):
        heat, salt, zonal, merid = (
            across[field * levels + level : field * levels + level + 1, :] for field in range(4)
        )
        own_zonal, own_merid = (
            own[field * levels + level : field * levels + level + 1, :] for field in (2, 3)
        )
        weight = weights[level : level + 1, :]
        load = jnp.where(count > level, SALINITY_BETA * salt - HEAT_ALPHA * heat, 0.0)
        pressure = pressure + weight * load
        slope = (inner[level : level + 1, :] + sign * pressure) * 0.5
        spread_x = jnp.where(shared > level, zonal - own_zonal, 0.0)
        spread_y = jnp.where(shared > level, merid - own_merid, 0.0)
        rate = VISCOSITY * spread_x - jnp.where(both > level, slope, 0.0)
        change_x = TIME_INCREMENT * rate
        change_y = (TIME_INCREMENT * VISCOSITY) * spread_y
        change[0, level : level + 1, :] = change_x
        change[1, level : level + 1, :] = change_y
        added_x = added_x + weight * change_x
        added_y = added_y + weight * change_y
    edge = sublane == jnp.where(even_x, 0, cols_x - 1)
    flow_x = flows[0] + jnp.where(edge, added_x, 0.0)
    flow_y = flows[1] + jnp.where(edge, added_y, 0.0)
    inverse = jnp.where(counts > 0, 1.0, 0.0) / (4.0 + diagonal[...])
    ahead = jnp.where(high_x, 0.0, pltpu.roll(flow_x, cols_x - 1, 0))
    behind = jnp.where(low_x, 0.0, pltpu.roll(flow_x, 1, 0))
    slope = ahead - behind
    ahead = jnp.where(high_y, 0.0, pltpu.roll(flow_y, rows_y - 1, 1))
    behind = jnp.where(low_y, 0.0, pltpu.roll(flow_y, 1, 1))
    divergence = (slope + (ahead - behind)) * 0.5
    edge_x = flow_x * 0.5
    edge_y = flow_y * 0.5
    first = jnp.where(lane == sublane, edge_y[:, 0:1], 0.0)
    last = jnp.where(lane == sublane + cols_x, edge_y[:, rows_y - 1 : rows_y], 0.0)
    corner = jnp.sum(first + last, axis=0, keepdims=True)

    def place(target):
        surface[target, 0:cols_x, 0, :] = divergence
        surface[target, cols_x : 2 * cols_x, 0, :] = inverse
        surface[target, 2 * cols_x : 2 * cols_x + 1, 0, :] = edge_x[0:1, :]
        surface[target, 2 * cols_x + 1 : 2 * cols_x + 2, 0, :] = edge_x[cols_x - 1 : cols_x, :]
        surface[target, 2 * cols_x + 2 : 2 * cols_x + 3, 0, :] = corner

    pl.loop(0, surface.shape[0], unroll=8)(place)


def tracer_kernel(
    tracers, wet, moved, change, cols_b, cols_a, rows_b, rows_a, after_gather,
    new_tracers, moved_velocity,
):
    del after_gather
    levels, cols_x, rows_y = tracers.shape[1:]
    even_x = lax.axis_index("core") == 0
    after_cols, before_cols = side_columns(cols_b, cols_a)

    def neighbours(tile, index):
        row_a, row_b = (rows_a[index : index + 1, :], rows_b[index : index + 1, :])
        rows = (jnp.where(even_x, row_a, row_b), jnp.where(even_x, row_b, row_a))
        sides = (after_cols[:, index : index + 1], before_cols[:, index : index + 1])
        return neighbours_of(tile, *rows, *sides)

    counts = wet[...].astype(jnp.float32)
    shared = [jnp.minimum(counts, other) for other in neighbours(counts, 4 * levels)]
    diffusivity = TIME_INCREMENT * KAPPA_SPREAD
    sublane = sublanes_of((cols_x, rows_y))
    edge = sublane == jnp.where(even_x, 0, cols_x - 1)
    for level in range(levels):
        for part in range(2):
            tile = tracers[part, level]
            spread = laplacian(tile, neighbours(tile, part * levels + level), shared, level)
            new_tracers[part, level] = tile + diffusivity * spread
            added = jnp.where(edge, change[part, level : level + 1, :], 0.0)
            moved_velocity[part, level] = moved[part, level] + added


def solve_kernel(
    blocks_x, blocks_y, gathered, swapped, moved_velocity, wet,
    new_velocity, pressure,
    forcing, edges, residual, inverses, lifted_0, lifted_1, smooth_0, smooth_1, smooth_2, image_0, direction_1,
):
    levels, cols_x, rows_y = moved_velocity.shape[1:]
    shape = (cols_x, rows_y)
    lane, sublane = (lanes_of(shape), sublanes_of(shape))
    low_x, high_x = (sublane == 0, sublane == cols_x - 1)
    low_y, high_y = (lane == 0, lane == rows_y - 1)
    zero = jnp.zeros(shape, jnp.float32)

    def each(count, step, carry):
        if blocks_x <= 8:
            for number in range(count):
                carry = step(number, carry)
            return carry
        return lax.fori_loop(0, count, step, carry)

    def each_row(step, carry):
        return each(blocks_x, step, carry)

    def guarded(load, row, column):
        if isinstance(row, int):
            return load(row * blocks_y + column) if 0 <= row < blocks_x else 0.0
        inside = jnp.logical_and(row >= 0, row < blocks_x)
        return load(jnp.clip(row, 0, blocks_x - 1) * blocks_y + column) * inside.astype(jnp.float32)

    def along_x(load, row, column):
        tile = load(row * blocks_y + column)
        other = guarded(lambda i: load(i, slice(0, 1)), row + 1, column)
        after = jnp.where(high_x, other, pltpu.roll(tile, cols_x - 1, 0))
        other = guarded(lambda i: load(i, slice(cols_x - 1, cols_x)), row - 1, column)
        before = jnp.where(low_x, other, pltpu.roll(tile, 1, 0))
        return after + before

    def along_y(tiles):
        ahead = [pltpu.roll(tile, rows_y - 1, 1) for tile in tiles] + [0.0]
        behind = [0.0] + [pltpu.roll(tile, 1, 1) for tile in tiles]
        return [
            jnp.where(high_y, ahead[c + 1], ahead[c]) + jnp.where(low_y, behind[c], behind[c + 1])
            for c in range(blocks_y)
        ]

    def lift(inverse, tile):
        first = inverse * tile
        near = jnp.where(high_x, 0.0, pltpu.roll(first, cols_x - 1, 0))
        near = near + jnp.where(low_x, 0.0, pltpu.roll(first, 1, 0))
        near = near + jnp.where(high_y, 0.0, pltpu.roll(first, rows_y - 1, 1))
        near = near + jnp.where(low_y, 0.0, pltpu.roll(first, 1, 1))
        return tile + near

    def total(values):
        return jnp.sum(values, axis=(0, 1), keepdims=True)

    height = 2 * cols_x + 3

    own_core = lax.axis_index("core")

    def unpack(chip, carry):
        for column in range(blocks_y):
            place = (chip * blocks_y + column) * height
            for blocks, core in ((gathered, own_core), (swapped, 1 - own_core)):
                index = (2 * chip + core) * blocks_y + column
                forcing[index] = blocks[pl.ds(place, cols_x), :]
                inverses[index] = blocks[pl.ds(place + cols_x, cols_x), :]
                edges[index, 0:3] = blocks[pl.ds(place + 2 * cols_x, 3), :]
        return carry

    each(blocks_x // 2, unpack, 0)

    def edge_row(which, row, column):
        return guarded(lambda i: edges[i, which : which + 1], row, column)

    def begin(row, carry):
        corners = [edges[row * blocks_y + c, 2:3] for c in range(blocks_y)]
        filler = [jnp.zeros((1, rows_y), jnp.float32)] * (-blocks_y % 8)
        corners = jnp.transpose(jnp.concatenate(corners + filler, axis=0))
        for column in range(blocks_y):
            index = row * blocks_y + column
            whole = forcing[index]
            whole = whole + jnp.where(high_x, edge_row(0, row + 1, column), 0.0)
            whole = whole - jnp.where(low_x, edge_row(1, row - 1, column), 0.0)
            if column + 1 < blocks_y:
                whole = whole + jnp.where(high_y, corners[0:cols_x, column + 1 : column + 2], 0.0)
            if column > 0:
                beyond = corners[cols_x : 2 * cols_x, column - 1 : column]
                whole = whole - jnp.where(low_y, beyond, 0.0)
            inverse = inverses[index]
            lifted = lift(inverse, whole)
            residual[index] = whole
            lifted_0[index] = lifted
            smooth_0[index] = inverse * lifted
        return carry

    def operate(lifted, smooth, image):
        def load(index, rows=slice(None)):
            return smooth[index, rows]

        def step(row, carry):
            inner, curvature = carry
            tiles = [smooth[row * blocks_y + c] for c in range(blocks_y)]
            beside = along_y(tiles)
            for column in range(blocks_y):
                index = row * blocks_y + column
                result = lifted[index] - (along_x(load, row, column) + beside[column])
                if image is not None:
                    image[index] = result
                inner = inner + residual[index] * tiles[column]
                curvature = curvature + tiles[column] * result
            return inner, curvature

        inner, curvature = each_row(step, (zero, zero))
        return total(inner), total(curvature)

    each_row(begin, 0)
    inner_0, curvature_0 = operate(lifted_0, smooth_0, image_0)
    step_0 = inner_0 / curvature_0

    def advance_0(row, carry):
        for column in range(blocks_y):
            index = row * blocks_y + column
            left = residual[index] - step_0 * image_0[index]
            inverse = inverses[index]
            lifted = lift(inverse, left)
            residual[index] = left
            lifted_1[index] = lifted
            smooth_1[index] = inverse * lifted
        return carry

    each_row(advance_0, 0)
    image_1 = lifted_1
    inner_1, curvature_1 = operate(lifted_1, smooth_1, image_1)
    turn_1 = inner_1 / inner_0
    step_1 = inner_1 / (curvature_1 - turn_1 * inner_1 / step_0)

    def advance_1(row, carry):
        for column in range(blocks_y):
            index = row * blocks_y + column
            direction_1[index] = smooth_1[index] + turn_1 * smooth_0[index]
            left = residual[index] - step_1 * (image_1[index] + turn_1 * image_0[index])
            inverse = inverses[index]
            lifted = lift(inverse, left)
            residual[index] = left
            lifted_0[index] = lifted
            smooth_2[index] = inverse * lifted
        return carry

    each_row(advance_1, 0)
    inner_2, curvature_2 = operate(lifted_0, smooth_2, None)
    turn_2 = inner_2 / inner_1
    step_2 = inner_2 / (curvature_2 - turn_2 * inner_2 / step_1)

    def iterate(index):
        previous = direction_1[index]
        result = step_0 * smooth_0[index] + step_1 * previous
        return result + step_2 * (smooth_2[index] + turn_2 * previous)

    own_x, own_y = (position_x(), lax.axis_index("by"))

    def block(shift_x, shift_y):
        row, column = (own_x + shift_x, own_y + shift_y)
        inside = (row >= 0) & (row < blocks_x) & (column >= 0) & (column < blocks_y)
        row, column = (jnp.clip(row, 0, blocks_x - 1), jnp.clip(column, 0, blocks_y - 1))
        return jnp.where(inside, iterate(row * blocks_y + column), 0.0)

    own = iterate(own_x * blocks_y + own_y)
    pressure[...] = own
    upper = jnp.where(high_x, pltpu.roll(block(1, 0), cols_x - 1, 0), pltpu.roll(own, cols_x - 1, 0))
    lower = jnp.where(low_x, pltpu.roll(block(-1, 0), 1, 0), pltpu.roll(own, 1, 0))
    slope_x = GRAVITY * ((upper - lower) * 0.5)
    upper = jnp.where(high_y, pltpu.roll(block(0, 1), rows_y - 1, 1), pltpu.roll(own, rows_y - 1, 1))
    lower = jnp.where(low_y, pltpu.roll(block(0, -1), 1, 1), pltpu.roll(own, 1, 1))
    slope_y = GRAVITY * ((upper - lower) * 0.5)
    counts = wet[...]
    for level in range(levels):
        here = counts > level
        new_velocity[0, level] = moved_velocity[0, level] - jnp.where(here, slope_x, 0.0)
        new_velocity[1, level] = moved_velocity[1, level] - jnp.where(here, slope_y, 0.0)


def latitude_rate(positions, total_rows):
    return 1.5 * jnp.sin(math.pi * ((positions + 0.5) / total_rows - 0.5))


def body(tracers, velocity, wet_levels, thickness, diagonal):
    levels = tracers.shape[1]
    cols_x, rows_y = wet_levels.shape
    chips_z, cores, blocks_y = (lax.axis_size("z"), lax.axis_size("core"), lax.axis_size("by"))
    blocks_x = chips_z * cores
    shape = (cols_x, rows_y)
    height = 2 * cols_x + 3
    rim_rows = 4 * levels + 1

    def like(*dims):
        return jax.ShapeDtypeStruct(dims, jnp.float32)

    def held(*dims):
        return pltpu.VMEM(dims, jnp.float32) if math.prod(dims) <= HELD_SIZE else like(*dims)

    def kept(array):
        if array.size > HELD_SIZE:
            return array
        return pltpu.with_memory_space_constraint(array, pltpu.VMEM)

    fields = (tracers, velocity, wet_levels, diagonal, thickness)
    rows_a, rows_b, cols_a, cols_b, *block = pl.pallas_call(
        pack_rims,
        out_shape=[
            held(rim_rows, rows_y), held(rim_rows, rows_y), held(*shape), held(*shape),
            held(*tracers.shape), held(*velocity.shape), pltpu.VMEM(shape, wet_levels.dtype),
            held(*shape), held(levels, rows_y),
        ],
        in_specs=[ANY] * 5,
        out_specs=[VMEM] * 9,
        scratch_shapes=[pltpu.SMEM(thickness.shape, jnp.float32), pltpu.SemaphoreType.DMA((5,))],
    )(*(pltpu.with_memory_space_constraint(array, pltpu.HBM) for array in fields))
    block = [kept(array) for array in block]

    def exchange(message, axis, first):
        size = blocks_x if axis == "bx" else blocks_y
        pairs = [(i, i + 1) for i in range(first, size - 1, 2)]
        axes = ("z", "core") if axis == "bx" else axis
        return lax.ppermute(message, axes, pairs + [(j, i) for i, j in pairs])

    sent = rows_b
    rows_b, rows_a = (exchange(rows_b, "bx", 1), exchange(rows_a, "bx", 0))
    cols_b, cols_a = (exchange(cols_b, "by", 1), exchange(cols_a, "by", 0))
    positions = (lax.axis_index("by") * rows_y + jnp.arange(rows_y, dtype=jnp.int32)).astype(jnp.float32)
    latitude = latitude_rate(positions, blocks_y * rows_y)[None]

    tracers, velocity, wet, diagonal, weights = block
    sent = kept(sent)
    rows_a, rows_b, cols_a, cols_b = (kept(array) for array in (rows_a, rows_b, cols_a, cols_b))
    moved, flows, inner = pl.pallas_call(
        level_kernel,
        out_shape=[held(*velocity.shape), held(2, *shape), held(levels, rows_y)],
        in_specs=[VMEM] * 8,
        out_specs=[VMEM] * 3,
    )(tracers, velocity, wet, weights, kept(latitude), cols_b, cols_a, rows_a)
    surface, change = pl.pallas_call(
        edge_kernel,
        out_shape=[held(chips_z * blocks_y, height, 1, rows_y), held(2, levels, rows_y)],
        in_specs=[VMEM] * 7,
        out_specs=[VMEM] * 2,
    )(sent, rows_b, kept(inner), weights, wet, diagonal, kept(flows))

    gathered = lax.all_to_all(surface, ("z", "by"), split_axis=0, concat_axis=0, tiled=True)
    swapped = lax.ppermute(gathered, "core", [(0, 1), (1, 0)])
    new_tracers, moved_velocity = pl.pallas_call(
        tracer_kernel,
        out_shape=[like(*tracers.shape), held(*velocity.shape)],
        in_specs=[VMEM] * 8 + [ANY],
        out_specs=[VMEM] * 2,
    )(tracers, wet, kept(moved), kept(change), cols_b, cols_a, rows_b, rows_a, gathered)
    gathered, swapped = (array.reshape(-1, rows_y) for array in (gathered, swapped))

    def solve(*refs):
        solve_kernel(blocks_x, blocks_y, *refs)

    blocks = blocks_x * blocks_y
    new_velocity, pressure = pl.pallas_call(
        solve,
        out_shape=[like(*velocity.shape), like(*shape)],
        in_specs=[VMEM] * 4,
        out_specs=[VMEM] * 2,
        scratch_shapes=[pltpu.VMEM((blocks, *shape), jnp.float32)] * 11,
        compiler_params=pltpu.CompilerParams(vmem_limit_bytes=(4 + 52 * blocks // 1024) * 2**20),
    )(kept(gathered), kept(swapped), kept(moved_velocity), wet)
    return new_tracers, new_velocity, pressure


def solution(mesh):
    size_x, size_y = (mesh.shape["bx"], mesh.shape["by"])
    chips = jax.sharding.Mesh(mesh.devices.reshape(size_x // 2, 2, size_y), ("z", "core", "by"))
    along_x = ("z", "core")
    placed = (
        P(None, None, along_x, "by"),
        P(None, None, along_x, "by"),
        P(along_x, "by"),
        P(),
        P(along_x, None),
    )
    return jax.shard_map(
        body,
        mesh=chips,
        in_specs=placed,
        out_specs=(P(None, None, along_x, "by"), P(None, None, along_x, "by"), P(along_x, "by")),
        check_vma=False,
    )
```

```python
import math

import jax
import jax.numpy as jnp
from jax import lax
from jax.experimental import pallas as pl
from jax.experimental.pallas import tpu as pltpu
from jax.sharding import PartitionSpec as P

ITERS = 3

HEAT_ALPHA = 0.5
SALINITY_BETA = 0.8
KAPPA_SPREAD = 0.15
VISCOSITY = 0.1
TIME_INCREMENT = 0.2
GRAVITY = 1.0

HELD_SIZE = 2**18

VMEM = pl.BlockSpec(memory_space=pltpu.VMEM)
ANY = pl.BlockSpec(memory_space=pl.ANY)


def lanes_of(shape):
    return lax.broadcasted_iota(jnp.int32, shape, 1)


def sublanes_of(shape):
    return lax.broadcasted_iota(jnp.int32, shape, 0)


def position_x():
    return lax.axis_index("z") * lax.axis_size("core") + lax.axis_index("core")


def pack_rims(
    tracers_in, velocity_in, wet_in, diagonal_in, thickness_in,
    rows_a, rows_b, cols_a, cols_b, tracers, velocity, wet, diagonal, weights,
    thickness, semaphores,
):
    levels, cols_x, rows_y = tracers.shape[1:]
    row_start = pl.multiple_of(lax.axis_index("by") * rows_y, rows_y)
    copies = [
        pltpu.make_async_copy(source, target, semaphores.at[number])
        for number, (source, target) in enumerate((
            (tracers_in, tracers),
            (velocity_in, velocity),
            (wet_in, wet),
            (thickness_in, thickness),
            (diagonal_in.at[:, pl.ds(row_start, rows_y)], diagonal),
        ))
    ]
    for copy in copies:
        copy.start()
    even_x, even_y = (lax.axis_index("core") == 0, lax.axis_index("by") % 2 == 0)
    lane = lanes_of((cols_x, rows_y))
    for copy in copies:
        copy.wait()
    for level in range(levels):
        weights[level : level + 1, :] = jnp.full((1, rows_y), thickness[level], jnp.float32)
    counts = wet[...].astype(jnp.float32)
    first, last = jnp.zeros_like(counts), jnp.zeros_like(counts)
    for index in range(4 * levels + 1):
        field, level = divmod(index, levels)
        if field < 4:
            tile = (tracers if field < 2 else velocity)[field % 2, level]
        else:
            tile = counts
        top, bottom = (tile[0:1, :], tile[cols_x - 1 : cols_x, :])
        rows_a[index : index + 1, :] = jnp.where(even_x, bottom, top)
        rows_b[index : index + 1, :] = jnp.where(even_x, top, bottom)
        first = jnp.where(lane == index, tile[:, 0:1], first)
        last = jnp.where(lane == index, tile[:, rows_y - 1 : rows_y], last)
    cols_a[...] = jnp.where(even_y, last, first)
    cols_b[...] = jnp.where(even_y, first, last)


def edges_of(shape):
    sublane, lane = (sublanes_of(shape), lanes_of(shape))
    return sublane == 0, sublane == shape[0] - 1, lane == 0, lane == shape[1] - 1


def neighbours_of(tile, after_row, before_row, after_col, before_col):
    low_x, high_x, low_y, high_y = edges_of(tile.shape)
    cols_x, rows_y = tile.shape
    return (
        jnp.where(high_x, after_row, pltpu.roll(tile, cols_x - 1, 0)),
        jnp.where(low_x, before_row, pltpu.roll(tile, 1, 0)),
        jnp.where(high_y, after_col, pltpu.roll(tile, rows_y - 1, 1)),
        jnp.where(low_y, before_col, pltpu.roll(tile, 1, 1)),
    )


def laplacian(tile, others, shared, level):
    total = jnp.zeros_like(tile)
    for other, limit in zip(others, shared):
        total = total + jnp.where(limit > level, other - tile, 0.0)
    return total


def side_columns(cols_b, cols_a):
    even_y = lax.axis_index("by") % 2 == 0
    a, b = (cols_a[...], cols_b[...])
    return jnp.where(even_y, a, b), jnp.where(even_y, b, a)


def level_kernel(
    tracers, velocity, wet, weights, latitude, cols_b, cols_a, rows_a,
    moved_velocity, flows, inner,
):
    levels, cols_x, rows_y = tracers.shape[1:]
    shape = (cols_x, rows_y)
    even_x = lax.axis_index("core") == 0
    after_cols, before_cols = side_columns(cols_b, cols_a)

    def neighbours(tile, index):
        row = rows_a[index : index + 1, :]
        after_row, before_row = (jnp.where(even_x, row, 0.0), jnp.where(even_x, 0.0, row))
        sides = (after_cols[:, index : index + 1], before_cols[:, index : index + 1])
        return neighbours_of(tile, after_row, before_row, *sides)

    counts = wet[...].astype(jnp.float32)
    around = neighbours(counts, 4 * levels)
    shared = [jnp.minimum(counts, other) for other in around]
    both_x = jnp.minimum(shared[0], shared[1])
    both_y = jnp.minimum(shared[2], shared[3])
    zero = jnp.zeros(shape, jnp.float32)
    coriolis = jnp.broadcast_to(latitude[...], shape)
    difference_x, difference_y, flow_x, flow_y = (zero, zero, zero, zero)
    for level in range(levels):
        here = counts > level
        weight = weights[level : level + 1, :]
        heat_around = neighbours(tracers[0, level], level)
        salt_around = neighbours(tracers[1, level], levels + level)
        loads = [
            jnp.where(count > level, SALINITY_BETA * s - HEAT_ALPHA * t, 0.0)
            for count, s, t in zip(around, salt_around, heat_around)
        ]
        difference_x = difference_x + weight * (loads[0] - loads[1])
        difference_y = difference_y + weight * (loads[2] - loads[3])
        inner[level : level + 1, :] = jnp.where(
            even_x, difference_x[0:1, :], difference_x[cols_x - 1 : cols_x, :]
        )
        gradient_x = jnp.where(both_x > level, difference_x * 0.5, 0.0)
        gradient_y = jnp.where(both_y > level, difference_y * 0.5, 0.0)
        zonal, merid = (velocity[0, level], velocity[1, level])
        spread_x = laplacian(zonal, neighbours(zonal, 2 * levels + level), shared, level)
        spread_y = laplacian(merid, neighbours(merid, 3 * levels + level), shared, level)
        zonal_rate = coriolis * merid - gradient_x + VISCOSITY * spread_x
        merid_rate = -coriolis * zonal - gradient_y + VISCOSITY * spread_y
        next_zonal = zonal + jnp.where(here, TIME_INCREMENT * zonal_rate, 0.0)
        next_merid = merid + jnp.where(here, TIME_INCREMENT * merid_rate, 0.0)
        moved_velocity[0, level] = next_zonal
        moved_velocity[1, level] = next_merid
        flow_x = flow_x + jnp.where(here, weight * next_zonal, 0.0)
        flow_y = flow_y + jnp.where(here, weight * next_merid, 0.0)
    flows[0] = flow_x
    flows[1] = flow_y


def edge_kernel(
    own, across, inner, weights, wet, diagonal, flows,
    surface, change,
):
    levels = weights.shape[0]
    cols_x, rows_y = shape = wet.shape
    low_x, high_x, low_y, high_y = edges_of(shape)
    lane, sublane = (lanes_of(shape), sublanes_of(shape))
    even_x = lax.axis_index("core") == 0
    sign = jnp.where(even_x, -1.0, 1.0)
    counts = wet[...].astype(jnp.float32)
    within = jnp.where(even_x, counts[1:2, :], counts[cols_x - 2 : cols_x - 1, :])
    count = across[4 * levels : 4 * levels + 1, :]
    shared = jnp.minimum(count, own[4 * levels : 4 * levels + 1, :])
    both = jnp.minimum(shared, within)
    pressure = jnp.zeros((1, rows_y), jnp.float32)
    added_x, added_y = (pressure, pressure)
    for level in range(levels):
        heat, salt, zonal, merid = (
            across[field * levels + level : field * levels + level + 1, :] for field in range(4)
        )
        own_zonal, own_merid = (
            own[field * levels + level : field * levels + level + 1, :] for field in (2, 3)
        )
        weight = weights[level : level + 1, :]
        load = jnp.where(count > level, SALINITY_BETA * salt - HEAT_ALPHA * heat, 0.0)
        pressure = pressure + weight * load
        slope = (inner[level : level + 1, :] + sign * pressure) * 0.5
        spread_x = jnp.where(shared > level, zonal - own_zonal, 0.0)
        spread_y = jnp.where(shared > level, merid - own_merid, 0.0)
        rate = VISCOSITY * spread_x - jnp.where(both > level, slope, 0.0)
        change_x = TIME_INCREMENT * rate
        change_y = (TIME_INCREMENT * VISCOSITY) * spread_y
        change[0, level : level + 1, :] = change_x
        change[1, level : level + 1, :] = change_y
        added_x = added_x + weight * change_x
        added_y = added_y + weight * change_y
    edge = sublane == jnp.where(even_x, 0, cols_x - 1)
    flow_x = flows[0] + jnp.where(edge, added_x, 0.0)
    flow_y = flows[1] + jnp.where(edge, added_y, 0.0)
    inverse = jnp.where(counts > 0, 1.0, 0.0) / (4.0 + diagonal[...])
    ahead = jnp.where(high_x, 0.0, pltpu.roll(flow_x, cols_x - 1, 0))
    behind = jnp.where(low_x, 0.0, pltpu.roll(flow_x, 1, 0))
    slope = ahead - behind
    ahead = jnp.where(high_y, 0.0, pltpu.roll(flow_y, rows_y - 1, 1))
    behind = jnp.where(low_y, 0.0, pltpu.roll(flow_y, 1, 1))
    divergence = (slope + (ahead - behind)) * 0.5
    edge_x = flow_x * 0.5
    edge_y = flow_y * 0.5
    first = jnp.where(lane == sublane, edge_y[:, 0:1], 0.0)
    last = jnp.where(lane == sublane + cols_x, edge_y[:, rows_y - 1 : rows_y], 0.0)
    corner = jnp.sum(first + last, axis=0, keepdims=True)

    def place(target):
        surface[target, 0:cols_x, 0, :] = divergence
        surface[target, cols_x : 2 * cols_x, 0, :] = inverse
        surface[target, 2 * cols_x : 2 * cols_x + 1, 0, :] = edge_x[0:1, :]
        surface[target, 2 * cols_x + 1 : 2 * cols_x + 2, 0, :] = edge_x[cols_x - 1 : cols_x, :]
        surface[target, 2 * cols_x + 2 : 2 * cols_x + 3, 0, :] = corner

    pl.loop(0, surface.shape[0], unroll=8)(place)


def tracer_kernel(
    tracers, wet, moved, change, cols_b, cols_a, rows_b, rows_a, after_gather,
    new_tracers, moved_velocity,
):
    del after_gather
    levels, cols_x, rows_y = tracers.shape[1:]
    even_x = lax.axis_index("core") == 0
    after_cols, before_cols = side_columns(cols_b, cols_a)

    def neighbours(tile, index):
        row_a, row_b = (rows_a[index : index + 1, :], rows_b[index : index + 1, :])
        rows = (jnp.where(even_x, row_a, row_b), jnp.where(even_x, row_b, row_a))
        sides = (after_cols[:, index : index + 1], before_cols[:, index : index + 1])
        return neighbours_of(tile, *rows, *sides)

    counts = wet[...].astype(jnp.float32)
    shared = [jnp.minimum(counts, other) for other in neighbours(counts, 4 * levels)]
    diffusivity = TIME_INCREMENT * KAPPA_SPREAD
    sublane = sublanes_of((cols_x, rows_y))
    edge = sublane == jnp.where(even_x, 0, cols_x - 1)
    for level in range(levels):
        for part in range(2):
            tile = tracers[part, level]
            spread = laplacian(tile, neighbours(tile, part * levels + level), shared, level)
            new_tracers[part, level] = tile + diffusivity * spread
            added = jnp.where(edge, change[part, level : level + 1, :], 0.0)
            moved_velocity[part, level] = moved[part, level] + added


def solve_kernel(
    blocks_x, blocks_y, gathered, swapped, moved_velocity, wet,
    new_velocity, pressure,
    forcing, edges, residual, inverses, lifted_0, lifted_1, smooth_0, smooth_1, smooth_2, image_0, direction_1,
):
    levels, cols_x, rows_y = moved_velocity.shape[1:]
    shape = (cols_x, rows_y)
    lane, sublane = (lanes_of(shape), sublanes_of(shape))
    low_x, high_x = (sublane == 0, sublane == cols_x - 1)
    low_y, high_y = (lane == 0, lane == rows_y - 1)
    zero = jnp.zeros(shape, jnp.float32)

    def each(count, step, carry):
        if blocks_x <= 8:
            for number in range(count):
                carry = step(number, carry)
            return carry
        return lax.fori_loop(0, count, step, carry)

    def each_row(step, carry):
        return each(blocks_x, step, carry)

    def guarded(load, row, column):
        if isinstance(row, int):
            return load(row * blocks_y + column) if 0 <= row < blocks_x else 0.0
        inside = jnp.logical_and(row >= 0, row < blocks_x)
        return load(jnp.clip(row, 0, blocks_x - 1) * blocks_y + column) * inside.astype(jnp.float32)

    def along_x(load, row, column):
        tile = load(row * blocks_y + column)
        other = guarded(lambda i: load(i, slice(0, 1)), row + 1, column)
        after = jnp.where(high_x, other, pltpu.roll(tile, cols_x - 1, 0))
        other = guarded(lambda i: load(i, slice(cols_x - 1, cols_x)), row - 1, column)
        before = jnp.where(low_x, other, pltpu.roll(tile, 1, 0))
        return after + before

    def along_y(tiles):
        ahead = [pltpu.roll(tile, rows_y - 1, 1) for tile in tiles] + [0.0]
        behind = [0.0] + [pltpu.roll(tile, 1, 1) for tile in tiles]
        return [
            jnp.where(high_y, ahead[c + 1], ahead[c]) + jnp.where(low_y, behind[c], behind[c + 1])
            for c in range(blocks_y)
        ]

    def lift(inverse, tile):
        first = inverse * tile
        near = jnp.where(high_x, 0.0, pltpu.roll(first, cols_x - 1, 0))
        near = near + jnp.where(low_x, 0.0, pltpu.roll(first, 1, 0))
        near = near + jnp.where(high_y, 0.0, pltpu.roll(first, rows_y - 1, 1))
        near = near + jnp.where(low_y, 0.0, pltpu.roll(first, 1, 1))
        return tile + near

    def total(values):
        return jnp.sum(values, axis=(0, 1), keepdims=True)

    height = 2 * cols_x + 3

    own_core = lax.axis_index("core")

    def unpack(chip, carry):
        for column in range(blocks_y):
            place = (chip * blocks_y + column) * height
            for blocks, core in ((gathered, own_core), (swapped, 1 - own_core)):
                index = (2 * chip + core) * blocks_y + column
                forcing[index] = blocks[pl.ds(place, cols_x), :]
                inverses[index] = blocks[pl.ds(place + cols_x, cols_x), :]
                edges[index, 0:3] = blocks[pl.ds(place + 2 * cols_x, 3), :]
        return carry

    each(blocks_x // 2, unpack, 0)

    def edge_row(which, row, column):
        return guarded(lambda i: edges[i, which : which + 1], row, column)

    def begin(row, carry):
        corners = [edges[row * blocks_y + c, 2:3] for c in range(blocks_y)]
        filler = [jnp.zeros((1, rows_y), jnp.float32)] * (-blocks_y % 8)
        corners = jnp.transpose(jnp.concatenate(corners + filler, axis=0))
        for column in range(blocks_y):
            index = row * blocks_y + column
            whole = forcing[index]
            whole = whole + jnp.where(high_x, edge_row(0, row + 1, column), 0.0)
            whole = whole - jnp.where(low_x, edge_row(1, row - 1, column), 0.0)
            if column + 1 < blocks_y:
                whole = whole + jnp.where(high_y, corners[0:cols_x, column + 1 : column + 2], 0.0)
            if column > 0:
                beyond = corners[cols_x : 2 * cols_x, column - 1 : column]
                whole = whole - jnp.where(low_y, beyond, 0.0)
            inverse = inverses[index]
            lifted = lift(inverse, whole)
            residual[index] = whole
            lifted_0[index] = lifted
            smooth_0[index] = inverse * lifted
        return carry

    def operate(lifted, smooth, image):
        def load(index, rows=slice(None)):
            return smooth[index, rows]

        def step(row, carry):
            inner, curvature = carry
            tiles = [smooth[row * blocks_y + c] for c in range(blocks_y)]
            beside = along_y(tiles)
            for column in range(blocks_y):
                index = row * blocks_y + column
                result = lifted[index] - (along_x(load, row, column) + beside[column])
                if image is not None:
                    image[index] = result
                inner = inner + residual[index] * tiles[column]
                curvature = curvature + tiles[column] * result
            return inner, curvature

        inner, curvature = each_row(step, (zero, zero))
        return total(inner), total(curvature)

    each_row(begin, 0)
    inner_0, curvature_0 = operate(lifted_0, smooth_0, image_0)
    step_0 = inner_0 / curvature_0

    def advance_0(row, carry):
        for column in range(blocks_y):
            index = row * blocks_y + column
            left = residual[index] - step_0 * image_0[index]
            inverse = inverses[index]
            lifted = lift(inverse, left)
            residual[index] = left
            lifted_1[index] = lifted
            smooth_1[index] = inverse * lifted
        return carry

    each_row(advance_0, 0)
    image_1 = lifted_1
    inner_1, curvature_1 = operate(lifted_1, smooth_1, image_1)
    turn_1 = inner_1 / inner_0
    step_1 = inner_1 / (curvature_1 - turn_1 * inner_1 / step_0)

    def advance_1(row, carry):
        for column in range(blocks_y):
            index = row * blocks_y + column
            direction_1[index] = smooth_1[index] + turn_1 * smooth_0[index]
            left = residual[index] - step_1 * (image_1[index] + turn_1 * image_0[index])
            inverse = inverses[index]
            lifted = lift(inverse, left)
            residual[index] = left
            lifted_0[index] = lifted
            smooth_2[index] = inverse * lifted
        return carry

    each_row(advance_1, 0)
    inner_2, curvature_2 = operate(lifted_0, smooth_2, None)
    turn_2 = inner_2 / inner_1
    step_2 = inner_2 / (curvature_2 - turn_2 * inner_2 / step_1)

    def iterate(index):
        previous = direction_1[index]
        result = step_0 * smooth_0[index] + step_1 * previous
        return result + step_2 * (smooth_2[index] + turn_2 * previous)

    own_x, own_y = (position_x(), lax.axis_index("by"))

    def block(shift_x, shift_y):
        row, column = (own_x + shift_x, own_y + shift_y)
        inside = (row >= 0) & (row < blocks_x) & (column >= 0) & (column < blocks_y)
        row, column = (jnp.clip(row, 0, blocks_x - 1), jnp.clip(column, 0, blocks_y - 1))
        return jnp.where(inside, iterate(row * blocks_y + column), 0.0)

    own = iterate(own_x * blocks_y + own_y)
    pressure[...] = own
    upper = jnp.where(high_x, pltpu.roll(block(1, 0), cols_x - 1, 0), pltpu.roll(own, cols_x - 1, 0))
    lower = jnp.where(low_x, pltpu.roll(block(-1, 0), 1, 0), pltpu.roll(own, 1, 0))
    slope_x = GRAVITY * ((upper - lower) * 0.5)
    upper = jnp.where(high_y, pltpu.roll(block(0, 1), rows_y - 1, 1), pltpu.roll(own, rows_y - 1, 1))
    lower = jnp.where(low_y, pltpu.roll(block(0, -1), 1, 1), pltpu.roll(own, 1, 1))
    slope_y = GRAVITY * ((upper - lower) * 0.5)
    counts = wet[...]
    for level in range(levels):
        here = counts > level
        new_velocity[0, level] = moved_velocity[0, level] - jnp.where(here, slope_x, 0.0)
        new_velocity[1, level] = moved_velocity[1, level] - jnp.where(here, slope_y, 0.0)


def latitude_rate(positions, total_rows):
    return 1.5 * jnp.sin(math.pi * ((positions + 0.5) / total_rows - 0.5))


def body(tracers, velocity, wet_levels, thickness, diagonal):
    levels = tracers.shape[1]
    cols_x, rows_y = wet_levels.shape
    chips_z, cores, blocks_y = (lax.axis_size("z"), lax.axis_size("core"), lax.axis_size("by"))
    blocks_x = chips_z * cores
    shape = (cols_x, rows_y)
    height = 2 * cols_x + 3
    rim_rows = 4 * levels + 1

    def like(*dims):
        return jax.ShapeDtypeStruct(dims, jnp.float32)

    def held(*dims):
        return pltpu.VMEM(dims, jnp.float32) if math.prod(dims) <= HELD_SIZE else like(*dims)

    def kept(array):
        if array.size > HELD_SIZE:
            return array
        return pltpu.with_memory_space_constraint(array, pltpu.VMEM)

    fields = (tracers, velocity, wet_levels, diagonal, thickness)
    rows_a, rows_b, cols_a, cols_b, *block = pl.pallas_call(
        pack_rims,
        out_shape=[
            held(rim_rows, rows_y), held(rim_rows, rows_y), held(*shape), held(*shape),
            held(*tracers.shape), held(*velocity.shape), pltpu.VMEM(shape, wet_levels.dtype),
            held(*shape), held(levels, rows_y),
        ],
        in_specs=[ANY] * 5,
        out_specs=[VMEM] * 9,
        scratch_shapes=[pltpu.SMEM(thickness.shape, jnp.float32), pltpu.SemaphoreType.DMA((5,))],
    )(*(pltpu.with_memory_space_constraint(array, pltpu.HBM) for array in fields))
    block = [kept(array) for array in block]

    def exchange(message, axis, first):
        size = blocks_x if axis == "bx" else blocks_y
        pairs = [(i, i + 1) for i in range(first, size - 1, 2)]
        axes = ("z", "core") if axis == "bx" else axis
        return lax.ppermute(message, axes, pairs + [(j, i) for i, j in pairs])

    sent = rows_b
    rows_b, rows_a = (exchange(rows_b, "bx", 1), exchange(rows_a, "bx", 0))
    cols_b, cols_a = (exchange(cols_b, "by", 1), exchange(cols_a, "by", 0))
    positions = (lax.axis_index("by") * rows_y + jnp.arange(rows_y, dtype=jnp.int32)).astype(jnp.float32)
    latitude = latitude_rate(positions, blocks_y * rows_y)[None]

    tracers, velocity, wet, diagonal, weights = block
    sent = kept(sent)
    rows_a, rows_b, cols_a, cols_b = (kept(array) for array in (rows_a, rows_b, cols_a, cols_b))
    moved, flows, inner = pl.pallas_call(
        level_kernel,
        out_shape=[held(*velocity.shape), held(2, *shape), held(levels, rows_y)],
        in_specs=[VMEM] * 8,
        out_specs=[VMEM] * 3,
    )(tracers, velocity, wet, weights, kept(latitude), cols_b, cols_a, rows_a)
    surface, change = pl.pallas_call(
        edge_kernel,
        out_shape=[held(chips_z * blocks_y, height, 1, rows_y), held(2, levels, rows_y)],
        in_specs=[VMEM] * 7,
        out_specs=[VMEM] * 2,
    )(sent, rows_b, kept(inner), weights, wet, diagonal, kept(flows))

    gathered = lax.all_to_all(surface, ("z", "by"), split_axis=0, concat_axis=0, tiled=True)
    swapped = lax.ppermute(gathered, "core", [(0, 1), (1, 0)])
    new_tracers, moved_velocity = pl.pallas_call(
        tracer_kernel,
        out_shape=[like(*tracers.shape), held(*velocity.shape)],
        in_specs=[VMEM] * 9,
        out_specs=[VMEM] * 2,
    )(tracers, wet, kept(moved), kept(change), cols_b, cols_a, rows_b, rows_a, kept(gathered))
    gathered, swapped = (array.reshape(-1, rows_y) for array in (gathered, swapped))

    def solve(*refs):
        solve_kernel(blocks_x, blocks_y, *refs)

    blocks = blocks_x * blocks_y
    new_velocity, pressure = pl.pallas_call(
        solve,
        out_shape=[like(*velocity.shape), like(*shape)],
        in_specs=[VMEM] * 4,
        out_specs=[VMEM] * 2,
        scratch_shapes=[pltpu.VMEM((blocks, *shape), jnp.float32)] * 11,
        compiler_params=pltpu.CompilerParams(vmem_limit_bytes=(4 + 52 * blocks // 1024) * 2**20),
    )(kept(gathered), kept(swapped), kept(moved_velocity), wet)
    return new_tracers, new_velocity, pressure


def solution(mesh):
    size_x, size_y = (mesh.shape["bx"], mesh.shape["by"])
    chips = jax.sharding.Mesh(mesh.devices.reshape(size_x // 2, 2, size_y), ("z", "core", "by"))
    along_x = ("z", "core")
    placed = (
        P(None, None, along_x, "by"),
        P(None, None, along_x, "by"),
        P(along_x, "by"),
        P(),
        P(along_x, None),
    )
    return jax.shard_map(
        body,
        mesh=chips,
        in_specs=placed,
        out_specs=(P(None, None, along_x, "by"), P(None, None, along_x, "by"), P(along_x, "by")),
        check_vma=False,
    )
```

```python
import math

import jax
import jax.numpy as jnp
from jax import lax
from jax.experimental import pallas as pl
from jax.experimental.pallas import tpu as pltpu
from jax.sharding import PartitionSpec as P

ITERS = 3

HEAT_ALPHA = 0.5
SALINITY_BETA = 0.8
KAPPA_SPREAD = 0.15
VISCOSITY = 0.1
TIME_INCREMENT = 0.2
GRAVITY = 1.0

HELD_SIZE = 2**18

VMEM = pl.BlockSpec(memory_space=pltpu.VMEM)
ANY = pl.BlockSpec(memory_space=pl.ANY)


def lanes_of(shape):
    return lax.broadcasted_iota(jnp.int32, shape, 1)


def sublanes_of(shape):
    return lax.broadcasted_iota(jnp.int32, shape, 0)


def position_x():
    return lax.axis_index("z") * lax.axis_size("core") + lax.axis_index("core")


def pack_rims(
    tracers_in, velocity_in, wet_in, diagonal_in, thickness_in,
    rows_a, rows_b, cols_a, cols_b, tracers, velocity, wet, diagonal, weights,
    thickness, semaphores,
):
    levels, cols_x, rows_y = tracers.shape[1:]
    row_start = pl.multiple_of(lax.axis_index("by") * rows_y, rows_y)
    copies = [
        pltpu.make_async_copy(source, target, semaphores.at[number])
        for number, (source, target) in enumerate((
            (tracers_in, tracers),
            (velocity_in, velocity),
            (wet_in, wet),
            (thickness_in, thickness),
            (diagonal_in.at[:, pl.ds(row_start, rows_y)], diagonal),
        ))
    ]
    for copy in copies:
        copy.start()
    even_x, even_y = (lax.axis_index("core") == 0, lax.axis_index("by") % 2 == 0)
    lane = lanes_of((cols_x, rows_y))
    for copy in copies:
        copy.wait()
    for level in range(levels):
        weights[level : level + 1, :] = jnp.full((1, rows_y), thickness[level], jnp.float32)
    counts = wet[...].astype(jnp.float32)
    first, last = jnp.zeros_like(counts), jnp.zeros_like(counts)
    for index in range(4 * levels + 1):
        field, level = divmod(index, levels)
        if field < 4:
            tile = (tracers if field < 2 else velocity)[field % 2, level]
        else:
            tile = counts
        top, bottom = (tile[0:1, :], tile[cols_x - 1 : cols_x, :])
        rows_a[index : index + 1, :] = jnp.where(even_x, bottom, top)
        rows_b[index : index + 1, :] = jnp.where(even_x, top, bottom)
        first = jnp.where(lane == index, tile[:, 0:1], first)
        last = jnp.where(lane == index, tile[:, rows_y - 1 : rows_y], last)
    cols_a[...] = jnp.where(even_y, last, first)
    cols_b[...] = jnp.where(even_y, first, last)


def edges_of(shape):
    sublane, lane = (sublanes_of(shape), lanes_of(shape))
    return sublane == 0, sublane == shape[0] - 1, lane == 0, lane == shape[1] - 1


def neighbours_of(tile, after_row, before_row, after_col, before_col):
    low_x, high_x, low_y, high_y = edges_of(tile.shape)
    cols_x, rows_y = tile.shape
    return (
        jnp.where(high_x, after_row, pltpu.roll(tile, cols_x - 1, 0)),
        jnp.where(low_x, before_row, pltpu.roll(tile, 1, 0)),
        jnp.where(high_y, after_col, pltpu.roll(tile, rows_y - 1, 1)),
        jnp.where(low_y, before_col, pltpu.roll(tile, 1, 1)),
    )


def laplacian(tile, others, shared, level):
    total = jnp.zeros_like(tile)
    for other, limit in zip(others, shared):
        total = total + jnp.where(limit > level, other - tile, 0.0)
    return total


def side_columns(cols_b, cols_a):
    even_y = lax.axis_index("by") % 2 == 0
    a, b = (cols_a[...], cols_b[...])
    return jnp.where(even_y, a, b), jnp.where(even_y, b, a)


def level_kernel(
    tracers, velocity, wet, weights, latitude, cols_b, cols_a,
    moved_velocity, flows, inner_b, inner_a,
):
    levels, cols_x, rows_y = tracers.shape[1:]
    shape = (cols_x, rows_y)
    even_x = lax.axis_index("core") == 0
    after_cols, before_cols = side_columns(cols_b, cols_a)

    def neighbours(tile, index):
        sides = (after_cols[:, index : index + 1], before_cols[:, index : index + 1])
        return neighbours_of(tile, 0.0, 0.0, *sides)

    counts = wet[...].astype(jnp.float32)
    around = neighbours(counts, 4 * levels)
    shared = [jnp.minimum(counts, other) for other in around]
    both_x = jnp.minimum(shared[0], shared[1])
    both_y = jnp.minimum(shared[2], shared[3])
    zero = jnp.zeros(shape, jnp.float32)
    coriolis = jnp.broadcast_to(latitude[...], shape)
    difference_x, difference_y, flow_x, flow_y = (zero, zero, zero, zero)
    for level in range(levels):
        here = counts > level
        weight = weights[level : level + 1, :]
        heat_around = neighbours(tracers[0, level], level)
        salt_around = neighbours(tracers[1, level], levels + level)
        loads = [
            jnp.where(count > level, SALINITY_BETA * s - HEAT_ALPHA * t, 0.0)
            for count, s, t in zip(around, salt_around, heat_around)
        ]
        difference_x = difference_x + weight * (loads[0] - loads[1])
        difference_y = difference_y + weight * (loads[2] - loads[3])
        low, high = (difference_x[0:1, :], difference_x[cols_x - 1 : cols_x, :])
        inner_b[level : level + 1, :] = jnp.where(even_x, low, high)
        inner_a[level : level + 1, :] = jnp.where(even_x, high, low)
        gradient_x = jnp.where(both_x > level, difference_x * 0.5, 0.0)
        gradient_y = jnp.where(both_y > level, difference_y * 0.5, 0.0)
        zonal, merid = (velocity[0, level], velocity[1, level])
        spread_x = laplacian(zonal, neighbours(zonal, 2 * levels + level), shared, level)
        spread_y = laplacian(merid, neighbours(merid, 3 * levels + level), shared, level)
        zonal_rate = coriolis * merid - gradient_x + VISCOSITY * spread_x
        merid_rate = -coriolis * zonal - gradient_y + VISCOSITY * spread_y
        next_zonal = zonal + jnp.where(here, TIME_INCREMENT * zonal_rate, 0.0)
        next_merid = merid + jnp.where(here, TIME_INCREMENT * merid_rate, 0.0)
        moved_velocity[0, level] = next_zonal
        moved_velocity[1, level] = next_merid
        flow_x = flow_x + jnp.where(here, weight * next_zonal, 0.0)
        flow_y = flow_y + jnp.where(here, weight * next_merid, 0.0)
    flows[0] = flow_x
    flows[1] = flow_y


def edge_change(own, across, inner, within, weights, sign, change):
    levels, rows_y = weights.shape
    count = across[4 * levels : 4 * levels + 1, :]
    shared = jnp.minimum(count, own[4 * levels : 4 * levels + 1, :])
    both = jnp.minimum(shared, within)
    pressure = jnp.zeros((1, rows_y), jnp.float32)
    added_x, added_y = (pressure, pressure)
    for level in range(levels):
        heat, salt, zonal, merid = (
            across[field * levels + level : field * levels + level + 1, :] for field in range(4)
        )
        own_zonal, own_merid = (
            own[field * levels + level : field * levels + level + 1, :] for field in (2, 3)
        )
        weight = weights[level : level + 1, :]
        load = jnp.where(count > level, SALINITY_BETA * salt - HEAT_ALPHA * heat, 0.0)
        pressure = pressure + weight * load
        slope = (inner[level : level + 1, :] + sign * pressure) * 0.5
        spread_x = jnp.where(shared > level, zonal - own_zonal, 0.0)
        spread_y = jnp.where(shared > level, merid - own_merid, 0.0)
        rate = VISCOSITY * spread_x - jnp.where(both > level, slope, 0.0)
        change_x = TIME_INCREMENT * rate
        change_y = (TIME_INCREMENT * VISCOSITY) * spread_y
        change[0, level : level + 1, :] = change_x
        change[1, level : level + 1, :] = change_y
        added_x = added_x + weight * change_x
        added_y = added_y + weight * change_y
    return added_x, added_y


def edge_masks(shape):
    even_x = lax.axis_index("core") == 0
    sublane = sublanes_of(shape)
    last = shape[0] - 1
    return sublane == jnp.where(even_x, 0, last), sublane == jnp.where(even_x, last, 0)


def edge_kernel(
    own_b, across_b, inner_b, own_a, across_a, inner_a, weights, wet, diagonal, flows,
    surface, change_b, change_a,
):
    cols_x, rows_y = shape = wet.shape
    low_x, high_x, low_y, high_y = edges_of(shape)
    lane, sublane = (lanes_of(shape), sublanes_of(shape))
    even_x = lax.axis_index("core") == 0
    sign = jnp.where(even_x, -1.0, 1.0)
    counts = wet[...].astype(jnp.float32)
    second, last_but_one = (counts[1:2, :], counts[cols_x - 2 : cols_x - 1, :])
    within_b = jnp.where(even_x, second, last_but_one)
    within_a = jnp.where(even_x, last_but_one, second)
    added_b = edge_change(own_b, across_b, inner_b, within_b, weights, sign, change_b)
    added_a = edge_change(own_a, across_a, inner_a, within_a, weights, -sign, change_a)
    edge_b, edge_a = edge_masks(shape)
    flow_x, flow_y = (
        flows[part] + jnp.where(edge_b, added_b[part], 0.0) + jnp.where(edge_a, added_a[part], 0.0)
        for part in range(2)
    )
    inverse = jnp.where(counts > 0, 1.0, 0.0) / (4.0 + diagonal[...])
    ahead = jnp.where(high_x, 0.0, pltpu.roll(flow_x, cols_x - 1, 0))
    behind = jnp.where(low_x, 0.0, pltpu.roll(flow_x, 1, 0))
    slope = ahead - behind
    ahead = jnp.where(high_y, 0.0, pltpu.roll(flow_y, rows_y - 1, 1))
    behind = jnp.where(low_y, 0.0, pltpu.roll(flow_y, 1, 1))
    divergence = (slope + (ahead - behind)) * 0.5
    edge_x = flow_x * 0.5
    edge_y = flow_y * 0.5
    first = jnp.where(lane == sublane, edge_y[:, 0:1], 0.0)
    last = jnp.where(lane == sublane + cols_x, edge_y[:, rows_y - 1 : rows_y], 0.0)
    corner = jnp.sum(first + last, axis=0, keepdims=True)

    def place(target):
        surface[target, 0:cols_x, 0, :] = divergence
        surface[target, cols_x : 2 * cols_x, 0, :] = inverse
        surface[target, 2 * cols_x : 2 * cols_x + 1, 0, :] = edge_x[0:1, :]
        surface[target, 2 * cols_x + 1 : 2 * cols_x + 2, 0, :] = edge_x[cols_x - 1 : cols_x, :]
        surface[target, 2 * cols_x + 2 : 2 * cols_x + 3, 0, :] = corner

    pl.loop(0, surface.shape[0], unroll=8)(place)


def tracer_kernel(
    tracers, wet, moved, change_b, change_a, cols_b, cols_a, rows_b, rows_a, after_gather,
    new_tracers, moved_velocity,
):
    del after_gather
    levels, cols_x, rows_y = tracers.shape[1:]
    even_x = lax.axis_index("core") == 0
    after_cols, before_cols = side_columns(cols_b, cols_a)

    def neighbours(tile, index):
        row_a, row_b = (rows_a[index : index + 1, :], rows_b[index : index + 1, :])
        rows = (jnp.where(even_x, row_a, row_b), jnp.where(even_x, row_b, row_a))
        sides = (after_cols[:, index : index + 1], before_cols[:, index : index + 1])
        return neighbours_of(tile, *rows, *sides)

    counts = wet[...].astype(jnp.float32)
    shared = [jnp.minimum(counts, other) for other in neighbours(counts, 4 * levels)]
    diffusivity = TIME_INCREMENT * KAPPA_SPREAD
    edge_b, edge_a = edge_masks((cols_x, rows_y))
    for level in range(levels):
        for part in range(2):
            tile = tracers[part, level]
            spread = laplacian(tile, neighbours(tile, part * levels + level), shared, level)
            new_tracers[part, level] = tile + diffusivity * spread
            added = jnp.where(edge_b, change_b[part, level : level + 1, :], 0.0)
            added = added + jnp.where(edge_a, change_a[part, level : level + 1, :], 0.0)
            moved_velocity[part, level] = moved[part, level] + added


def solve_kernel(
    blocks_x, blocks_y, gathered, swapped, moved_velocity, wet,
    new_velocity, pressure,
    forcing, edges, residual, inverses, lifted_0, lifted_1, smooth_0, smooth_1, smooth_2, image_0, direction_1,
):
    levels, cols_x, rows_y = moved_velocity.shape[1:]
    shape = (cols_x, rows_y)
    lane, sublane = (lanes_of(shape), sublanes_of(shape))
    low_x, high_x = (sublane == 0, sublane == cols_x - 1)
    low_y, high_y = (lane == 0, lane == rows_y - 1)
    zero = jnp.zeros(shape, jnp.float32)

    def each(count, step, carry):
        if blocks_x <= 8:
            for number in range(count):
                carry = step(number, carry)
            return carry
        return lax.fori_loop(0, count, step, carry)

    def each_row(step, carry):
        return each(blocks_x, step, carry)

    def guarded(load, row, column):
        if isinstance(row, int):
            return load(row * blocks_y + column) if 0 <= row < blocks_x else 0.0
        inside = jnp.logical_and(row >= 0, row < blocks_x)
        return load(jnp.clip(row, 0, blocks_x - 1) * blocks_y + column) * inside.astype(jnp.float32)

    def along_x(load, row, column):
        tile = load(row * blocks_y + column)
        other = guarded(lambda i: load(i, slice(0, 1)), row + 1, column)
        after = jnp.where(high_x, other, pltpu.roll(tile, cols_x - 1, 0))
        other = guarded(lambda i: load(i, slice(cols_x - 1, cols_x)), row - 1, column)
        before = jnp.where(low_x, other, pltpu.roll(tile, 1, 0))
        return after + before

    def along_y(tiles):
        ahead = [pltpu.roll(tile, rows_y - 1, 1) for tile in tiles] + [0.0]
        behind = [0.0] + [pltpu.roll(tile, 1, 1) for tile in tiles]
        return [
            jnp.where(high_y, ahead[c + 1], ahead[c]) + jnp.where(low_y, behind[c], behind[c + 1])
            for c in range(blocks_y)
        ]

    def lift(inverse, tile):
        first = inverse * tile
        near = jnp.where(high_x, 0.0, pltpu.roll(first, cols_x - 1, 0))
        near = near + jnp.where(low_x, 0.0, pltpu.roll(first, 1, 0))
        near = near + jnp.where(high_y, 0.0, pltpu.roll(first, rows_y - 1, 1))
        near = near + jnp.where(low_y, 0.0, pltpu.roll(first, 1, 1))
        return tile + near

    def total(values):
        return jnp.sum(values, axis=(0, 1), keepdims=True)

    height = 2 * cols_x + 3

    own_core = lax.axis_index("core")

    def unpack(chip, carry):
        for column in range(blocks_y):
            place = (chip * blocks_y + column) * height
            for blocks, core in ((gathered, own_core), (swapped, 1 - own_core)):
                index = (2 * chip + core) * blocks_y + column
                forcing[index] = blocks[pl.ds(place, cols_x), :]
                inverses[index] = blocks[pl.ds(place + cols_x, cols_x), :]
                edges[index, 0:3] = blocks[pl.ds(place + 2 * cols_x, 3), :]
        return carry

    each(blocks_x // 2, unpack, 0)

    def edge_row(which, row, column):
        return guarded(lambda i: edges[i, which : which + 1], row, column)

    def begin(row, carry):
        corners = [edges[row * blocks_y + c, 2:3] for c in range(blocks_y)]
        filler = [jnp.zeros((1, rows_y), jnp.float32)] * (-blocks_y % 8)
        corners = jnp.transpose(jnp.concatenate(corners + filler, axis=0))
        for column in range(blocks_y):
            index = row * blocks_y + column
            whole = forcing[index]
            whole = whole + jnp.where(high_x, edge_row(0, row + 1, column), 0.0)
            whole = whole - jnp.where(low_x, edge_row(1, row - 1, column), 0.0)
            if column + 1 < blocks_y:
                whole = whole + jnp.where(high_y, corners[0:cols_x, column + 1 : column + 2], 0.0)
            if column > 0:
                beyond = corners[cols_x : 2 * cols_x, column - 1 : column]
                whole = whole - jnp.where(low_y, beyond, 0.0)
            inverse = inverses[index]
            lifted = lift(inverse, whole)
            residual[index] = whole
            lifted_0[index] = lifted
            smooth_0[index] = inverse * lifted
        return carry

    def operate(lifted, smooth, image):
        def load(index, rows=slice(None)):
            return smooth[index, rows]

        def step(row, carry):
            inner, curvature = carry
            tiles = [smooth[row * blocks_y + c] for c in range(blocks_y)]
            beside = along_y(tiles)
            for column in range(blocks_y):
                index = row * blocks_y + column
                result = lifted[index] - (along_x(load, row, column) + beside[column])
                if image is not None:
                    image[index] = result
                inner = inner + residual[index] * tiles[column]
                curvature = curvature + tiles[column] * result
            return inner, curvature

        inner, curvature = each_row(step, (zero, zero))
        return total(inner), total(curvature)

    each_row(begin, 0)
    inner_0, curvature_0 = operate(lifted_0, smooth_0, image_0)
    step_0 = inner_0 / curvature_0

    def advance_0(row, carry):
        for column in range(blocks_y):
            index = row * blocks_y + column
            left = residual[index] - step_0 * image_0[index]
            inverse = inverses[index]
            lifted = lift(inverse, left)
            residual[index] = left
            lifted_1[index] = lifted
            smooth_1[index] = inverse * lifted
        return carry

    each_row(advance_0, 0)
    image_1 = lifted_1
    inner_1, curvature_1 = operate(lifted_1, smooth_1, image_1)
    turn_1 = inner_1 / inner_0
    step_1 = inner_1 / (curvature_1 - turn_1 * inner_1 / step_0)

    def advance_1(row, carry):
        for column in range(blocks_y):
            index = row * blocks_y + column
            direction_1[index] = smooth_1[index] + turn_1 * smooth_0[index]
            left = residual[index] - step_1 * (image_1[index] + turn_1 * image_0[index])
            inverse = inverses[index]
            lifted = lift(inverse, left)
            residual[index] = left
            lifted_0[index] = lifted
            smooth_2[index] = inverse * lifted
        return carry

    each_row(advance_1, 0)
    inner_2, curvature_2 = operate(lifted_0, smooth_2, None)
    turn_2 = inner_2 / inner_1
    step_2 = inner_2 / (curvature_2 - turn_2 * inner_2 / step_1)

    def iterate(index):
        previous = direction_1[index]
        result = step_0 * smooth_0[index] + step_1 * previous
        return result + step_2 * (smooth_2[index] + turn_2 * previous)

    own_x, own_y = (position_x(), lax.axis_index("by"))

    def block(shift_x, shift_y):
        row, column = (own_x + shift_x, own_y + shift_y)
        inside = (row >= 0) & (row < blocks_x) & (column >= 0) & (column < blocks_y)
        row, column = (jnp.clip(row, 0, blocks_x - 1), jnp.clip(column, 0, blocks_y - 1))
        return jnp.where(inside, iterate(row * blocks_y + column), 0.0)

    own = iterate(own_x * blocks_y + own_y)
    pressure[...] = own
    upper = jnp.where(high_x, pltpu.roll(block(1, 0), cols_x - 1, 0), pltpu.roll(own, cols_x - 1, 0))
    lower = jnp.where(low_x, pltpu.roll(block(-1, 0), 1, 0), pltpu.roll(own, 1, 0))
    slope_x = GRAVITY * ((upper - lower) * 0.5)
    upper = jnp.where(high_y, pltpu.roll(block(0, 1), rows_y - 1, 1), pltpu.roll(own, rows_y - 1, 1))
    lower = jnp.where(low_y, pltpu.roll(block(0, -1), 1, 1), pltpu.roll(own, 1, 1))
    slope_y = GRAVITY * ((upper - lower) * 0.5)
    counts = wet[...]
    for level in range(levels):
        here = counts > level
        new_velocity[0, level] = moved_velocity[0, level] - jnp.where(here, slope_x, 0.0)
        new_velocity[1, level] = moved_velocity[1, level] - jnp.where(here, slope_y, 0.0)


def latitude_rate(positions, total_rows):
    return 1.5 * jnp.sin(math.pi * ((positions + 0.5) / total_rows - 0.5))


def body(tracers, velocity, wet_levels, thickness, diagonal):
    levels = tracers.shape[1]
    cols_x, rows_y = wet_levels.shape
    chips_z, cores, blocks_y = (lax.axis_size("z"), lax.axis_size("core"), lax.axis_size("by"))
    blocks_x = chips_z * cores
    shape = (cols_x, rows_y)
    height = 2 * cols_x + 3
    rim_rows = 4 * levels + 1

    def like(*dims):
        return jax.ShapeDtypeStruct(dims, jnp.float32)

    def held(*dims):
        return pltpu.VMEM(dims, jnp.float32) if math.prod(dims) <= HELD_SIZE else like(*dims)

    def kept(array):
        if array.size > HELD_SIZE:
            return array
        return pltpu.with_memory_space_constraint(array, pltpu.VMEM)

    fields = (tracers, velocity, wet_levels, diagonal, thickness)
    rows_a, rows_b, cols_a, cols_b, *block = pl.pallas_call(
        pack_rims,
        out_shape=[
            held(rim_rows, rows_y), held(rim_rows, rows_y), held(*shape), held(*shape),
            held(*tracers.shape), held(*velocity.shape), pltpu.VMEM(shape, wet_levels.dtype),
            held(*shape), held(levels, rows_y),
        ],
        in_specs=[ANY] * 5,
        out_specs=[VMEM] * 9,
        scratch_shapes=[pltpu.SMEM(thickness.shape, jnp.float32), pltpu.SemaphoreType.DMA((5,))],
    )(*(pltpu.with_memory_space_constraint(array, pltpu.HBM) for array in fields))
    block = [kept(array) for array in block]

    def exchange(message, axis, first):
        size = blocks_x if axis == "bx" else blocks_y
        pairs = [(i, i + 1) for i in range(first, size - 1, 2)]
        axes = ("z", "core") if axis == "bx" else axis
        return lax.ppermute(message, axes, pairs + [(j, i) for i, j in pairs])

    sent_b, sent_a = (rows_b, rows_a)
    rows_b, rows_a = (exchange(rows_b, "bx", 1), exchange(rows_a, "bx", 0))
    cols_b, cols_a = (exchange(cols_b, "by", 1), exchange(cols_a, "by", 0))
    positions = (lax.axis_index("by") * rows_y + jnp.arange(rows_y, dtype=jnp.int32)).astype(jnp.float32)
    latitude = latitude_rate(positions, blocks_y * rows_y)[None]

    tracers, velocity, wet, diagonal, weights = block
    sent_b, sent_a = (kept(sent_b), kept(sent_a))
    rows_a, rows_b, cols_a, cols_b = (kept(array) for array in (rows_a, rows_b, cols_a, cols_b))
    moved, flows, inner_b, inner_a = pl.pallas_call(
        level_kernel,
        out_shape=[held(*velocity.shape), held(2, *shape)] + [held(levels, rows_y)] * 2,
        in_specs=[VMEM] * 7,
        out_specs=[VMEM] * 4,
    )(tracers, velocity, wet, weights, kept(latitude), cols_b, cols_a)
    inner_b, inner_a, flows = (kept(inner_b), kept(inner_a), kept(flows))
    surface, change_b, change_a = pl.pallas_call(
        edge_kernel,
        out_shape=[held(chips_z * blocks_y, height, 1, rows_y)] + [held(2, levels, rows_y)] * 2,
        in_specs=[VMEM] * 10,
        out_specs=[VMEM] * 3,
    )(sent_b, rows_b, inner_b, sent_a, rows_a, inner_a, weights, wet, diagonal, flows)

    gathered = lax.all_to_all(surface, ("z", "by"), split_axis=0, concat_axis=0, tiled=True)
    swapped = lax.ppermute(gathered, "core", [(0, 1), (1, 0)])
    new_tracers, moved_velocity = pl.pallas_call(
        tracer_kernel,
        out_shape=[like(*tracers.shape), held(*velocity.shape)],
        in_specs=[VMEM] * 10,
        out_specs=[VMEM] * 2,
    )(
        tracers, wet, kept(moved), kept(change_b), kept(change_a),
        cols_b, cols_a, rows_b, rows_a, kept(gathered),
    )
    gathered, swapped = (array.reshape(-1, rows_y) for array in (gathered, swapped))

    def solve(*refs):
        solve_kernel(blocks_x, blocks_y, *refs)

    blocks = blocks_x * blocks_y
    new_velocity, pressure = pl.pallas_call(
        solve,
        out_shape=[like(*velocity.shape), like(*shape)],
        in_specs=[VMEM] * 4,
        out_specs=[VMEM] * 2,
        scratch_shapes=[pltpu.VMEM((blocks, *shape), jnp.float32)] * 11,
        compiler_params=pltpu.CompilerParams(vmem_limit_bytes=(4 + 52 * blocks // 1024) * 2**20),
    )(kept(gathered), kept(swapped), kept(moved_velocity), wet)
    return new_tracers, new_velocity, pressure


def solution(mesh):
    size_x, size_y = (mesh.shape["bx"], mesh.shape["by"])
    chips = jax.sharding.Mesh(mesh.devices.reshape(size_x // 2, 2, size_y), ("z", "core", "by"))
    along_x = ("z", "core")
    placed = (
        P(None, None, along_x, "by"),
        P(None, None, along_x, "by"),
        P(along_x, "by"),
        P(),
        P(along_x, None),
    )
    return jax.shard_map(
        body,
        mesh=chips,
        in_specs=placed,
        out_specs=(P(None, None, along_x, "by"), P(None, None, along_x, "by"), P(along_x, "by")),
        check_vma=False,
    )
```

```python
import math

import jax
import jax.numpy as jnp
from jax import lax
from jax.experimental import pallas as pl
from jax.experimental.pallas import tpu as pltpu
from jax.sharding import PartitionSpec as P

ITERS = 3

HEAT_ALPHA = 0.5
SALINITY_BETA = 0.8
KAPPA_SPREAD = 0.15
VISCOSITY = 0.1
TIME_INCREMENT = 0.2
GRAVITY = 1.0

HELD_SIZE = 2**18

VMEM = pl.BlockSpec(memory_space=pltpu.VMEM)
ANY = pl.BlockSpec(memory_space=pl.ANY)


def lanes_of(shape):
    return lax.broadcasted_iota(jnp.int32, shape, 1)


def sublanes_of(shape):
    return lax.broadcasted_iota(jnp.int32, shape, 0)


def position_x():
    return lax.axis_index("z") * lax.axis_size("core") + lax.axis_index("core")


def pack_rims(
    tracers_in, velocity_in, wet_in, diagonal_in, thickness_in,
    rows_a, rows_b, cols_a, cols_b, tracers, velocity, wet, diagonal, weights,
    thickness, semaphores,
):
    levels, cols_x, rows_y = tracers.shape[1:]
    row_start = pl.multiple_of(lax.axis_index("by") * rows_y, rows_y)
    copies = [
        pltpu.make_async_copy(source, target, semaphores.at[number])
        for number, (source, target) in enumerate((
            (tracers_in, tracers),
            (velocity_in, velocity),
            (wet_in, wet),
            (thickness_in, thickness),
            (diagonal_in.at[:, pl.ds(row_start, rows_y)], diagonal),
        ))
    ]
    for copy in copies:
        copy.start()
    even_x, even_y = (lax.axis_index("core") == 0, lax.axis_index("by") % 2 == 0)
    lane = lanes_of((cols_x, rows_y))
    for copy in copies:
        copy.wait()
    for level in range(levels):
        weights[level : level + 1, :] = jnp.full((1, rows_y), thickness[level], jnp.float32)
    counts = wet[...].astype(jnp.float32)
    first, last = jnp.zeros_like(counts), jnp.zeros_like(counts)
    for index in range(4 * levels + 1):
        field, level = divmod(index, levels)
        if field < 4:
            tile = (tracers if field < 2 else velocity)[field % 2, level]
        else:
            tile = counts
        top, bottom = (tile[0:1, :], tile[cols_x - 1 : cols_x, :])
        rows_a[index : index + 1, :] = jnp.where(even_x, bottom, top)
        rows_b[index : index + 1, :] = jnp.where(even_x, top, bottom)
        first = jnp.where(lane == index, tile[:, 0:1], first)
        last = jnp.where(lane == index, tile[:, rows_y - 1 : rows_y], last)
    cols_a[...] = jnp.where(even_y, last, first)
    cols_b[...] = jnp.where(even_y, first, last)


def edges_of(shape):
    sublane, lane = (sublanes_of(shape), lanes_of(shape))
    return sublane == 0, sublane == shape[0] - 1, lane == 0, lane == shape[1] - 1


def neighbours_of(tile, after_row, before_row, after_col, before_col):
    low_x, high_x, low_y, high_y = edges_of(tile.shape)
    cols_x, rows_y = tile.shape
    return (
        jnp.where(high_x, after_row, pltpu.roll(tile, cols_x - 1, 0)),
        jnp.where(low_x, before_row, pltpu.roll(tile, 1, 0)),
        jnp.where(high_y, after_col, pltpu.roll(tile, rows_y - 1, 1)),
        jnp.where(low_y, before_col, pltpu.roll(tile, 1, 1)),
    )


def laplacian(tile, others, shared, level):
    total = jnp.zeros_like(tile)
    for other, limit in zip(others, shared):
        total = total + jnp.where(limit > level, other - tile, 0.0)
    return total


def side_columns(cols_b, cols_a):
    even_y = lax.axis_index("by") % 2 == 0
    a, b = (cols_a[...], cols_b[...])
    return jnp.where(even_y, a, b), jnp.where(even_y, b, a)


def level_kernel(
    tracers, velocity, wet, weights, latitude, cols_b, cols_a,
    moved_velocity, flows, inner_b, inner_a,
):
    levels, cols_x, rows_y = tracers.shape[1:]
    shape = (cols_x, rows_y)
    even_x = lax.axis_index("core") == 0
    after_cols, before_cols = side_columns(cols_b, cols_a)

    def neighbours(tile, index):
        sides = (after_cols[:, index : index + 1], before_cols[:, index : index + 1])
        return neighbours_of(tile, 0.0, 0.0, *sides)

    counts = wet[...].astype(jnp.float32)
    around = neighbours(counts, 4 * levels)
    shared = [jnp.minimum(counts, other) for other in around]
    both_x = jnp.minimum(shared[0], shared[1])
    both_y = jnp.minimum(shared[2], shared[3])
    zero = jnp.zeros(shape, jnp.float32)
    coriolis = jnp.broadcast_to(latitude[...], shape)
    difference_x, difference_y, flow_x, flow_y = (zero, zero, zero, zero)
    for level in range(levels):
        here = counts > level
        weight = weights[level : level + 1, :]
        heat_around = neighbours(tracers[0, level], level)
        salt_around = neighbours(tracers[1, level], levels + level)
        loads = [
            jnp.where(count > level, SALINITY_BETA * s - HEAT_ALPHA * t, 0.0)
            for count, s, t in zip(around, salt_around, heat_around)
        ]
        difference_x = difference_x + weight * (loads[0] - loads[1])
        difference_y = difference_y + weight * (loads[2] - loads[3])
        low, high = (difference_x[0:1, :], difference_x[cols_x - 1 : cols_x, :])
        inner_b[level : level + 1, :] = jnp.where(even_x, low, high)
        inner_a[level : level + 1, :] = jnp.where(even_x, high, low)
        gradient_x = jnp.where(both_x > level, difference_x * 0.5, 0.0)
        gradient_y = jnp.where(both_y > level, difference_y * 0.5, 0.0)
        zonal, merid = (velocity[0, level], velocity[1, level])
        spread_x = laplacian(zonal, neighbours(zonal, 2 * levels + level), shared, level)
        spread_y = laplacian(merid, neighbours(merid, 3 * levels + level), shared, level)
        zonal_rate = coriolis * merid - gradient_x + VISCOSITY * spread_x
        merid_rate = -coriolis * zonal - gradient_y + VISCOSITY * spread_y
        next_zonal = zonal + jnp.where(here, TIME_INCREMENT * zonal_rate, 0.0)
        next_merid = merid + jnp.where(here, TIME_INCREMENT * merid_rate, 0.0)
        moved_velocity[0, level] = next_zonal
        moved_velocity[1, level] = next_merid
        flow_x = flow_x + jnp.where(here, weight * next_zonal, 0.0)
        flow_y = flow_y + jnp.where(here, weight * next_merid, 0.0)
    flows[0] = flow_x
    flows[1] = flow_y


def edge_change(own, across, inner, within, weights, sign, change):
    levels, rows_y = weights.shape
    count = across[4 * levels : 4 * levels + 1, :]
    shared = jnp.minimum(count, own[4 * levels : 4 * levels + 1, :])
    both = jnp.minimum(shared, within)
    pressure = jnp.zeros((1, rows_y), jnp.float32)
    added_x, added_y = (pressure, pressure)
    for level in range(levels):
        heat, salt, zonal, merid = (
            across[field * levels + level : field * levels + level + 1, :] for field in range(4)
        )
        own_zonal, own_merid = (
            own[field * levels + level : field * levels + level + 1, :] for field in (2, 3)
        )
        weight = weights[level : level + 1, :]
        load = jnp.where(count > level, SALINITY_BETA * salt - HEAT_ALPHA * heat, 0.0)
        pressure = pressure + weight * load
        slope = (inner[level : level + 1, :] + sign * pressure) * 0.5
        spread_x = jnp.where(shared > level, zonal - own_zonal, 0.0)
        spread_y = jnp.where(shared > level, merid - own_merid, 0.0)
        rate = VISCOSITY * spread_x - jnp.where(both > level, slope, 0.0)
        change_x = TIME_INCREMENT * rate
        change_y = (TIME_INCREMENT * VISCOSITY) * spread_y
        change[0, level : level + 1, :] = change_x
        change[1, level : level + 1, :] = change_y
        added_x = added_x + weight * change_x
        added_y = added_y + weight * change_y
    return added_x, added_y


def edge_masks(shape):
    even_x = lax.axis_index("core") == 0
    sublane = sublanes_of(shape)
    last = shape[0] - 1
    return sublane == jnp.where(even_x, 0, last), sublane == jnp.where(even_x, last, 0)


def edge_kernel(
    own_b, across_b, inner_b, own_a, across_a, inner_a, weights, wet, diagonal, flows,
    surface, change_b, change_a,
):
    cols_x, rows_y = shape = wet.shape
    low_x, high_x, low_y, high_y = edges_of(shape)
    lane, sublane = (lanes_of(shape), sublanes_of(shape))
    even_x = lax.axis_index("core") == 0
    sign = jnp.where(even_x, -1.0, 1.0)
    counts = wet[...].astype(jnp.float32)
    second, last_but_one = (counts[1:2, :], counts[cols_x - 2 : cols_x - 1, :])
    within_b = jnp.where(even_x, second, last_but_one)
    within_a = jnp.where(even_x, last_but_one, second)
    added_b = edge_change(own_b, across_b, inner_b, within_b, weights, sign, change_b)
    added_a = edge_change(own_a, across_a, inner_a, within_a, weights, -sign, change_a)
    edge_b, edge_a = edge_masks(shape)
    flow_x, flow_y = (
        flows[part] + jnp.where(edge_b, added_b[part], 0.0) + jnp.where(edge_a, added_a[part], 0.0)
        for part in range(2)
    )
    inverse = jnp.where(counts > 0, 1.0, 0.0) / (4.0 + diagonal[...])
    ahead = jnp.where(high_x, 0.0, pltpu.roll(flow_x, cols_x - 1, 0))
    behind = jnp.where(low_x, 0.0, pltpu.roll(flow_x, 1, 0))
    slope = ahead - behind
    ahead = jnp.where(high_y, 0.0, pltpu.roll(flow_y, rows_y - 1, 1))
    behind = jnp.where(low_y, 0.0, pltpu.roll(flow_y, 1, 1))
    divergence = (slope + (ahead - behind)) * 0.5
    edge_x = flow_x * 0.5
    edge_y = flow_y * 0.5
    first = jnp.where(lane == sublane, edge_y[:, 0:1], 0.0)
    last = jnp.where(lane == sublane + cols_x, edge_y[:, rows_y - 1 : rows_y], 0.0)
    corner = jnp.sum(first + last, axis=0, keepdims=True)

    def place(target):
        surface[target, 0:cols_x, 0, :] = divergence
        surface[target, cols_x : 2 * cols_x, 0, :] = inverse
        surface[target, 2 * cols_x : 2 * cols_x + 1, 0, :] = edge_x[0:1, :]
        surface[target, 2 * cols_x + 1 : 2 * cols_x + 2, 0, :] = edge_x[cols_x - 1 : cols_x, :]
        surface[target, 2 * cols_x + 2 : 2 * cols_x + 3, 0, :] = corner

    pl.loop(0, surface.shape[0], unroll=8)(place)


def tracer_kernel(
    tracers, wet, moved, change_b, change_a, cols_b, cols_a, rows_b, rows_a, after_gather,
    new_tracers, moved_velocity,
):
    del after_gather
    levels, cols_x, rows_y = tracers.shape[1:]
    even_x = lax.axis_index("core") == 0
    after_cols, before_cols = side_columns(cols_b, cols_a)

    def neighbours(tile, index):
        row_a, row_b = (rows_a[index : index + 1, :], rows_b[index : index + 1, :])
        rows = (jnp.where(even_x, row_a, row_b), jnp.where(even_x, row_b, row_a))
        sides = (after_cols[:, index : index + 1], before_cols[:, index : index + 1])
        return neighbours_of(tile, *rows, *sides)

    counts = wet[...].astype(jnp.float32)
    shared = [jnp.minimum(counts, other) for other in neighbours(counts, 4 * levels)]
    diffusivity = TIME_INCREMENT * KAPPA_SPREAD
    edge_b, edge_a = edge_masks((cols_x, rows_y))
    for level in range(levels):
        for part in range(2):
            tile = tracers[part, level]
            spread = laplacian(tile, neighbours(tile, part * levels + level), shared, level)
            new_tracers[part, level] = tile + diffusivity * spread
            added = jnp.where(edge_b, change_b[part, level : level + 1, :], 0.0)
            added = added + jnp.where(edge_a, change_a[part, level : level + 1, :], 0.0)
            moved_velocity[part, level] = moved[part, level] + added


def solve_kernel(
    blocks_x, blocks_y, gathered, swapped, moved_velocity, wet,
    new_velocity, pressure,
    forcing, edges, residual, inverses, lifted_0, lifted_1, smooth_0, smooth_1, smooth_2, image_0, direction_1,
):
    levels, cols_x, rows_y = moved_velocity.shape[1:]
    shape = (cols_x, rows_y)
    lane, sublane = (lanes_of(shape), sublanes_of(shape))
    low_x, high_x = (sublane == 0, sublane == cols_x - 1)
    low_y, high_y = (lane == 0, lane == rows_y - 1)
    zero = jnp.zeros(shape, jnp.float32)

    def each(count, step, carry):
        if blocks_x <= 8:
            for number in range(count):
                carry = step(number, carry)
            return carry
        return lax.fori_loop(0, count, step, carry)

    def each_row(step, carry):
        return each(blocks_x, step, carry)

    def guarded(load, row, column):
        if isinstance(row, int):
            return load(row * blocks_y + column) if 0 <= row < blocks_x else 0.0
        inside = jnp.logical_and(row >= 0, row < blocks_x)
        return load(jnp.clip(row, 0, blocks_x - 1) * blocks_y + column) * inside.astype(jnp.float32)

    def along_x(load, row, column):
        tile = load(row * blocks_y + column)
        other = guarded(lambda i: load(i, slice(0, 1)), row + 1, column)
        after = jnp.where(high_x, other, pltpu.roll(tile, cols_x - 1, 0))
        other = guarded(lambda i: load(i, slice(cols_x - 1, cols_x)), row - 1, column)
        before = jnp.where(low_x, other, pltpu.roll(tile, 1, 0))
        return after + before

    def along_y(tiles):
        ahead = [pltpu.roll(tile, rows_y - 1, 1) for tile in tiles] + [0.0]
        behind = [0.0] + [pltpu.roll(tile, 1, 1) for tile in tiles]
        return [
            jnp.where(high_y, ahead[c + 1], ahead[c]) + jnp.where(low_y, behind[c], behind[c + 1])
            for c in range(blocks_y)
        ]

    def lift(inverse, tile):
        first = inverse * tile
        near = jnp.where(high_x, 0.0, pltpu.roll(first, cols_x - 1, 0))
        near = near + jnp.where(low_x, 0.0, pltpu.roll(first, 1, 0))
        near = near + jnp.where(high_y, 0.0, pltpu.roll(first, rows_y - 1, 1))
        near = near + jnp.where(low_y, 0.0, pltpu.roll(first, 1, 1))
        return tile + near

    def total(values):
        return jnp.sum(values, axis=(0, 1), keepdims=True)

    height = 2 * cols_x + 3

    own_core = lax.axis_index("core")

    def unpack(chip, carry):
        for column in range(blocks_y):
            place = (column * (blocks_x // 2) + chip) * height
            for blocks, core in ((gathered, own_core), (swapped, 1 - own_core)):
                index = (2 * chip + core) * blocks_y + column
                forcing[index] = blocks[pl.ds(place, cols_x), :]
                inverses[index] = blocks[pl.ds(place + cols_x, cols_x), :]
                edges[index, 0:3] = blocks[pl.ds(place + 2 * cols_x, 3), :]
        return carry

    each(blocks_x // 2, unpack, 0)

    def edge_row(which, row, column):
        return guarded(lambda i: edges[i, which : which + 1], row, column)

    def columns_of(first, count):
        corners = [edges[first + number, 2:3] for number in range(count)]
        filler = [jnp.zeros((1, rows_y), jnp.float32)] * (-count % 8)
        return jnp.transpose(jnp.concatenate(corners + filler, axis=0))[0 : 2 * cols_x]

    turned = columns_of(0, blocks_x * blocks_y) if blocks_x <= 8 else None

    def begin(row, carry):
        if turned is None:
            corners = columns_of(row * blocks_y, blocks_y)
        else:
            corners = turned[:, row * blocks_y : (row + 1) * blocks_y]
        for column in range(blocks_y):
            index = row * blocks_y + column
            whole = forcing[index]
            whole = whole + jnp.where(high_x, edge_row(0, row + 1, column), 0.0)
            whole = whole - jnp.where(low_x, edge_row(1, row - 1, column), 0.0)
            if column + 1 < blocks_y:
                whole = whole + jnp.where(high_y, corners[0:cols_x, column + 1 : column + 2], 0.0)
            if column > 0:
                beyond = corners[cols_x : 2 * cols_x, column - 1 : column]
                whole = whole - jnp.where(low_y, beyond, 0.0)
            inverse = inverses[index]
            lifted = lift(inverse, whole)
            residual[index] = whole
            lifted_0[index] = lifted
            smooth_0[index] = inverse * lifted
        return carry

    def operate(lifted, smooth, image):
        def load(index, rows=slice(None)):
            return smooth[index, rows]

        def step(row, carry):
            inner, curvature = carry
            tiles = [smooth[row * blocks_y + c] for c in range(blocks_y)]
            beside = along_y(tiles)
            for column in range(blocks_y):
                index = row * blocks_y + column
                result = lifted[index] - (along_x(load, row, column) + beside[column])
                if image is not None:
                    image[index] = result
                inner = inner + residual[index] * tiles[column]
                curvature = curvature + tiles[column] * result
            return inner, curvature

        inner, curvature = each_row(step, (zero, zero))
        return total(inner), total(curvature)

    each_row(begin, 0)
    inner_0, curvature_0 = operate(lifted_0, smooth_0, image_0)
    step_0 = inner_0 / curvature_0

    def advance_0(row, carry):
        for column in range(blocks_y):
            index = row * blocks_y + column
            left = residual[index] - step_0 * image_0[index]
            inverse = inverses[index]
            lifted = lift(inverse, left)
            residual[index] = left
            lifted_1[index] = lifted
            smooth_1[index] = inverse * lifted
        return carry

    each_row(advance_0, 0)
    image_1 = lifted_1
    inner_1, curvature_1 = operate(lifted_1, smooth_1, image_1)
    turn_1 = inner_1 / inner_0
    step_1 = inner_1 / (curvature_1 - turn_1 * inner_1 / step_0)

    def advance_1(row, carry):
        for column in range(blocks_y):
            index = row * blocks_y + column
            direction_1[index] = smooth_1[index] + turn_1 * smooth_0[index]
            left = residual[index] - step_1 * (image_1[index] + turn_1 * image_0[index])
            inverse = inverses[index]
            lifted = lift(inverse, left)
            residual[index] = left
            lifted_0[index] = lifted
            smooth_2[index] = inverse * lifted
        return carry

    each_row(advance_1, 0)
    inner_2, curvature_2 = operate(lifted_0, smooth_2, None)
    turn_2 = inner_2 / inner_1
    step_2 = inner_2 / (curvature_2 - turn_2 * inner_2 / step_1)

    def iterate(index):
        previous = direction_1[index]
        result = step_0 * smooth_0[index] + step_1 * previous
        return result + step_2 * (smooth_2[index] + turn_2 * previous)

    own_x, own_y = (position_x(), lax.axis_index("by"))

    def block(shift_x, shift_y):
        row, column = (own_x + shift_x, own_y + shift_y)
        inside = (row >= 0) & (row < blocks_x) & (column >= 0) & (column < blocks_y)
        row, column = (jnp.clip(row, 0, blocks_x - 1), jnp.clip(column, 0, blocks_y - 1))
        return jnp.where(inside, iterate(row * blocks_y + column), 0.0)

    own = iterate(own_x * blocks_y + own_y)
    pressure[...] = own
    upper = jnp.where(high_x, pltpu.roll(block(1, 0), cols_x - 1, 0), pltpu.roll(own, cols_x - 1, 0))
    lower = jnp.where(low_x, pltpu.roll(block(-1, 0), 1, 0), pltpu.roll(own, 1, 0))
    slope_x = GRAVITY * ((upper - lower) * 0.5)
    upper = jnp.where(high_y, pltpu.roll(block(0, 1), rows_y - 1, 1), pltpu.roll(own, rows_y - 1, 1))
    lower = jnp.where(low_y, pltpu.roll(block(0, -1), 1, 1), pltpu.roll(own, 1, 1))
    slope_y = GRAVITY * ((upper - lower) * 0.5)
    counts = wet[...]
    for level in range(levels):
        here = counts > level
        new_velocity[0, level] = moved_velocity[0, level] - jnp.where(here, slope_x, 0.0)
        new_velocity[1, level] = moved_velocity[1, level] - jnp.where(here, slope_y, 0.0)


def latitude_rate(positions, total_rows):
    return 1.5 * jnp.sin(math.pi * ((positions + 0.5) / total_rows - 0.5))


def body(tracers, velocity, wet_levels, thickness, diagonal):
    levels = tracers.shape[1]
    cols_x, rows_y = wet_levels.shape
    chips_z, cores, blocks_y = (lax.axis_size("z"), lax.axis_size("core"), lax.axis_size("by"))
    blocks_x = chips_z * cores
    shape = (cols_x, rows_y)
    height = 2 * cols_x + 3
    rim_rows = 4 * levels + 1

    def like(*dims):
        return jax.ShapeDtypeStruct(dims, jnp.float32)

    def held(*dims):
        return pltpu.VMEM(dims, jnp.float32) if math.prod(dims) <= HELD_SIZE else like(*dims)

    def kept(array):
        if array.size > HELD_SIZE:
            return array
        return pltpu.with_memory_space_constraint(array, pltpu.VMEM)

    fields = (tracers, velocity, wet_levels, diagonal, thickness)
    rows_a, rows_b, cols_a, cols_b, *block = pl.pallas_call(
        pack_rims,
        out_shape=[
            held(rim_rows, rows_y), held(rim_rows, rows_y), held(*shape), held(*shape),
            held(*tracers.shape), held(*velocity.shape), pltpu.VMEM(shape, wet_levels.dtype),
            held(*shape), held(levels, rows_y),
        ],
        in_specs=[ANY] * 5,
        out_specs=[VMEM] * 9,
        scratch_shapes=[pltpu.SMEM(thickness.shape, jnp.float32), pltpu.SemaphoreType.DMA((5,))],
    )(*(pltpu.with_memory_space_constraint(array, pltpu.HBM) for array in fields))
    block = [kept(array) for array in block]

    def exchange(message, axis, first):
        size = blocks_x if axis == "bx" else blocks_y
        pairs = [(i, i + 1) for i in range(first, size - 1, 2)]
        axes = ("z", "core") if axis == "bx" else axis
        return lax.ppermute(message, axes, pairs + [(j, i) for i, j in pairs])

    sent_b, sent_a = (rows_b, rows_a)
    rows_b, rows_a = (exchange(rows_b, "bx", 1), exchange(rows_a, "bx", 0))
    cols_b, cols_a = (exchange(cols_b, "by", 1), exchange(cols_a, "by", 0))
    positions = (lax.axis_index("by") * rows_y + jnp.arange(rows_y, dtype=jnp.int32)).astype(jnp.float32)
    latitude = latitude_rate(positions, blocks_y * rows_y)[None]

    tracers, velocity, wet, diagonal, weights = block
    sent_b, sent_a = (kept(sent_b), kept(sent_a))
    rows_a, rows_b, cols_a, cols_b = (kept(array) for array in (rows_a, rows_b, cols_a, cols_b))
    moved, flows, inner_b, inner_a = pl.pallas_call(
        level_kernel,
        out_shape=[held(*velocity.shape), held(2, *shape)] + [held(levels, rows_y)] * 2,
        in_specs=[VMEM] * 7,
        out_specs=[VMEM] * 4,
    )(tracers, velocity, wet, weights, kept(latitude), cols_b, cols_a)
    inner_b, inner_a, flows = (kept(inner_b), kept(inner_a), kept(flows))
    surface, change_b, change_a = pl.pallas_call(
        edge_kernel,
        out_shape=[held(chips_z * blocks_y, height, 1, rows_y)] + [held(2, levels, rows_y)] * 2,
        in_specs=[VMEM] * 10,
        out_specs=[VMEM] * 3,
    )(sent_b, rows_b, inner_b, sent_a, rows_a, inner_a, weights, wet, diagonal, flows)

    gathered = lax.all_to_all(surface, ("by", "z"), split_axis=0, concat_axis=0, tiled=True)
    swapped = lax.ppermute(gathered, "core", [(0, 1), (1, 0)])
    new_tracers, moved_velocity = pl.pallas_call(
        tracer_kernel,
        out_shape=[like(*tracers.shape), held(*velocity.shape)],
        in_specs=[VMEM] * 10,
        out_specs=[VMEM] * 2,
    )(
        tracers, wet, kept(moved), kept(change_b), kept(change_a),
        cols_b, cols_a, rows_b, rows_a, kept(gathered),
    )
    gathered, swapped = (array.reshape(-1, rows_y) for array in (gathered, swapped))

    def solve(*refs):
        solve_kernel(blocks_x, blocks_y, *refs)

    blocks = blocks_x * blocks_y
    new_velocity, pressure = pl.pallas_call(
        solve,
        out_shape=[like(*velocity.shape), like(*shape)],
        in_specs=[VMEM] * 4,
        out_specs=[VMEM] * 2,
        scratch_shapes=[pltpu.VMEM((blocks, *shape), jnp.float32)] * 11,
        compiler_params=pltpu.CompilerParams(vmem_limit_bytes=(4 + 52 * blocks // 1024) * 2**20),
    )(kept(gathered), kept(swapped), kept(moved_velocity), wet)
    return new_tracers, new_velocity, pressure


def solution(mesh):
    size_x, size_y = (mesh.shape["bx"], mesh.shape["by"])
    chips = jax.sharding.Mesh(mesh.devices.reshape(size_x // 2, 2, size_y), ("z", "core", "by"))
    along_x = ("z", "core")
    placed = (
        P(None, None, along_x, "by"),
        P(None, None, along_x, "by"),
        P(along_x, "by"),
        P(),
        P(along_x, None),
    )
    return jax.shard_map(
        body,
        mesh=chips,
        in_specs=placed,
        out_specs=(P(None, None, along_x, "by"), P(None, None, along_x, "by"), P(along_x, "by")),
        check_vma=False,
    )
```

```python
import math

import jax
import jax.numpy as jnp
from jax import lax
from jax.experimental import pallas as pl
from jax.experimental.pallas import tpu as pltpu
from jax.sharding import PartitionSpec as P

ITERS = 3

HEAT_ALPHA = 0.5
SALINITY_BETA = 0.8
KAPPA_SPREAD = 0.15
VISCOSITY = 0.1
TIME_INCREMENT = 0.2
GRAVITY = 1.0

HELD_SIZE = 2**18

VMEM = pl.BlockSpec(memory_space=pltpu.VMEM)
ANY = pl.BlockSpec(memory_space=pl.ANY)


def lanes_of(shape):
    return lax.broadcasted_iota(jnp.int32, shape, 1)


def sublanes_of(shape):
    return lax.broadcasted_iota(jnp.int32, shape, 0)


def position_x():
    return lax.axis_index("z") * lax.axis_size("core") + lax.axis_index("core")


def pack_rims(
    tracers_in, velocity_in, wet_in, diagonal_in, thickness_in,
    rows_a, rows_b, cols_a, cols_b, tracers, velocity, wet, diagonal, weights,
    thickness, semaphores,
):
    levels, cols_x, rows_y = tracers.shape[1:]
    row_start = pl.multiple_of(lax.axis_index("by") * rows_y, rows_y)
    copies = [
        pltpu.make_async_copy(source, target, semaphores.at[number])
        for number, (source, target) in enumerate((
            (tracers_in, tracers),
            (velocity_in, velocity),
            (wet_in, wet),
            (thickness_in, thickness),
            (diagonal_in.at[:, pl.ds(row_start, rows_y)], diagonal),
        ))
    ]
    for copy in copies:
        copy.start()
    even_x, even_y = (lax.axis_index("core") == 0, lax.axis_index("by") % 2 == 0)
    lane = lanes_of((cols_x, rows_y))
    for copy in copies:
        copy.wait()
    for level in range(levels):
        weights[level : level + 1, :] = jnp.full((1, rows_y), thickness[level], jnp.float32)
    counts = wet[...].astype(jnp.float32)
    first, last = jnp.zeros_like(counts), jnp.zeros_like(counts)
    for index in range(4 * levels + 1):
        field, level = divmod(index, levels)
        if field < 4:
            tile = (tracers if field < 2 else velocity)[field % 2, level]
        else:
            tile = counts
        top, bottom = (tile[0:1, :], tile[cols_x - 1 : cols_x, :])
        rows_a[index : index + 1, :] = jnp.where(even_x, bottom, top)
        rows_b[index : index + 1, :] = jnp.where(even_x, top, bottom)
        first = jnp.where(lane == index, tile[:, 0:1], first)
        last = jnp.where(lane == index, tile[:, rows_y - 1 : rows_y], last)
    cols_a[...] = jnp.where(even_y, last, first)
    cols_b[...] = jnp.where(even_y, first, last)


def edges_of(shape):
    sublane, lane = (sublanes_of(shape), lanes_of(shape))
    return sublane == 0, sublane == shape[0] - 1, lane == 0, lane == shape[1] - 1


def neighbours_of(tile, after_row, before_row, after_col, before_col):
    low_x, high_x, low_y, high_y = edges_of(tile.shape)
    cols_x, rows_y = tile.shape
    return (
        jnp.where(high_x, after_row, pltpu.roll(tile, cols_x - 1, 0)),
        jnp.where(low_x, before_row, pltpu.roll(tile, 1, 0)),
        jnp.where(high_y, after_col, pltpu.roll(tile, rows_y - 1, 1)),
        jnp.where(low_y, before_col, pltpu.roll(tile, 1, 1)),
    )


def laplacian(tile, others, shared, level):
    total = jnp.zeros_like(tile)
    for other, limit in zip(others, shared):
        total = total + jnp.where(limit > level, other - tile, 0.0)
    return total


def side_columns(cols_b, cols_a):
    even_y = lax.axis_index("by") % 2 == 0
    a, b = (cols_a[...], cols_b[...])
    return jnp.where(even_y, a, b), jnp.where(even_y, b, a)


def level_kernel(
    tracers, velocity, wet, weights, latitude, cols_b, cols_a,
    moved_velocity, flows, inner_b, inner_a,
):
    levels, cols_x, rows_y = tracers.shape[1:]
    shape = (cols_x, rows_y)
    even_x = lax.axis_index("core") == 0
    after_cols, before_cols = side_columns(cols_b, cols_a)

    def neighbours(tile, index):
        sides = (after_cols[:, index : index + 1], before_cols[:, index : index + 1])
        return neighbours_of(tile, 0.0, 0.0, *sides)

    counts = wet[...].astype(jnp.float32)
    around = neighbours(counts, 4 * levels)
    shared = [jnp.minimum(counts, other) for other in around]
    both_x = jnp.minimum(shared[0], shared[1])
    both_y = jnp.minimum(shared[2], shared[3])
    zero = jnp.zeros(shape, jnp.float32)
    coriolis = jnp.broadcast_to(latitude[...], shape)
    difference_x, difference_y, flow_x, flow_y = (zero, zero, zero, zero)
    for level in range(levels):
        here = counts > level
        weight = weights[level : level + 1, :]
        heat_around = neighbours(tracers[0, level], level)
        salt_around = neighbours(tracers[1, level], levels + level)
        loads = [
            jnp.where(count > level, SALINITY_BETA * s - HEAT_ALPHA * t, 0.0)
            for count, s, t in zip(around, salt_around, heat_around)
        ]
        difference_x = difference_x + weight * (loads[0] - loads[1])
        difference_y = difference_y + weight * (loads[2] - loads[3])
        low, high = (difference_x[0:1, :], difference_x[cols_x - 1 : cols_x, :])
        inner_b[level : level + 1, :] = jnp.where(even_x, low, high)
        inner_a[level : level + 1, :] = jnp.where(even_x, high, low)
        gradient_x = jnp.where(both_x > level, difference_x * 0.5, 0.0)
        gradient_y = jnp.where(both_y > level, difference_y * 0.5, 0.0)
        zonal, merid = (velocity[0, level], velocity[1, level])
        spread_x = laplacian(zonal, neighbours(zonal, 2 * levels + level), shared, level)
        spread_y = laplacian(merid, neighbours(merid, 3 * levels + level), shared, level)
        zonal_rate = coriolis * merid - gradient_x + VISCOSITY * spread_x
        merid_rate = -coriolis * zonal - gradient_y + VISCOSITY * spread_y
        next_zonal = zonal + jnp.where(here, TIME_INCREMENT * zonal_rate, 0.0)
        next_merid = merid + jnp.where(here, TIME_INCREMENT * merid_rate, 0.0)
        moved_velocity[0, level] = next_zonal
        moved_velocity[1, level] = next_merid
        flow_x = flow_x + jnp.where(here, weight * next_zonal, 0.0)
        flow_y = flow_y + jnp.where(here, weight * next_merid, 0.0)
    flows[0] = flow_x
    flows[1] = flow_y


def edge_change(own, across, inner, within, weights, sign, change):
    levels, rows_y = weights.shape
    count = across[4 * levels : 4 * levels + 1, :]
    shared = jnp.minimum(count, own[4 * levels : 4 * levels + 1, :])
    both = jnp.minimum(shared, within)
    pressure = jnp.zeros((1, rows_y), jnp.float32)
    added_x, added_y = (pressure, pressure)
    for level in range(levels):
        heat, salt, zonal, merid = (
            across[field * levels + level : field * levels + level + 1, :] for field in range(4)
        )
        own_zonal, own_merid = (
            own[field * levels + level : field * levels + level + 1, :] for field in (2, 3)
        )
        weight = weights[level : level + 1, :]
        load = jnp.where(count > level, SALINITY_BETA * salt - HEAT_ALPHA * heat, 0.0)
        pressure = pressure + weight * load
        slope = (inner[level : level + 1, :] + sign * pressure) * 0.5
        spread_x = jnp.where(shared > level, zonal - own_zonal, 0.0)
        spread_y = jnp.where(shared > level, merid - own_merid, 0.0)
        rate = VISCOSITY * spread_x - jnp.where(both > level, slope, 0.0)
        change_x = TIME_INCREMENT * rate
        change_y = (TIME_INCREMENT * VISCOSITY) * spread_y
        change[0, level : level + 1, :] = change_x
        change[1, level : level + 1, :] = change_y
        added_x = added_x + weight * change_x
        added_y = added_y + weight * change_y
    return added_x, added_y


def edge_masks(shape):
    even_x = lax.axis_index("core") == 0
    sublane = sublanes_of(shape)
    last = shape[0] - 1
    return sublane == jnp.where(even_x, 0, last), sublane == jnp.where(even_x, last, 0)


def edge_kernel(
    own_b, across_b, inner_b, own_a, across_a, inner_a, weights, wet, diagonal, flows,
    surface, change_b, change_a,
):
    cols_x, rows_y = shape = wet.shape
    low_x, high_x, low_y, high_y = edges_of(shape)
    lane, sublane = (lanes_of(shape), sublanes_of(shape))
    even_x = lax.axis_index("core") == 0
    sign = jnp.where(even_x, -1.0, 1.0)
    counts = wet[...].astype(jnp.float32)
    second, last_but_one = (counts[1:2, :], counts[cols_x - 2 : cols_x - 1, :])
    within_b = jnp.where(even_x, second, last_but_one)
    within_a = jnp.where(even_x, last_but_one, second)
    added_b = edge_change(own_b, across_b, inner_b, within_b, weights, sign, change_b)
    added_a = edge_change(own_a, across_a, inner_a, within_a, weights, -sign, change_a)
    edge_b, edge_a = edge_masks(shape)
    flow_x, flow_y = (
        flows[part] + jnp.where(edge_b, added_b[part], 0.0) + jnp.where(edge_a, added_a[part], 0.0)
        for part in range(2)
    )
    inverse = jnp.where(counts > 0, 1.0, 0.0) / (4.0 + diagonal[...])
    ahead = jnp.where(high_x, 0.0, pltpu.roll(flow_x, cols_x - 1, 0))
    behind = jnp.where(low_x, 0.0, pltpu.roll(flow_x, 1, 0))
    slope = ahead - behind
    ahead = jnp.where(high_y, 0.0, pltpu.roll(flow_y, rows_y - 1, 1))
    behind = jnp.where(low_y, 0.0, pltpu.roll(flow_y, 1, 1))
    divergence = (slope + (ahead - behind)) * 0.5
    edge_x = flow_x * 0.5
    edge_y = flow_y * 0.5
    first = jnp.where(lane == sublane, edge_y[:, 0:1], 0.0)
    last = jnp.where(lane == sublane + cols_x, edge_y[:, rows_y - 1 : rows_y], 0.0)
    corner = jnp.sum(first + last, axis=0, keepdims=True)

    def place(target):
        surface[target, 0:cols_x, 0, :] = divergence
        surface[target, cols_x : 2 * cols_x, 0, :] = inverse
        surface[target, 2 * cols_x : 2 * cols_x + 1, 0, :] = edge_x[0:1, :]
        surface[target, 2 * cols_x + 1 : 2 * cols_x + 2, 0, :] = edge_x[cols_x - 1 : cols_x, :]
        surface[target, 2 * cols_x + 2 : 2 * cols_x + 3, 0, :] = corner

    pl.loop(0, surface.shape[0], unroll=8)(place)


def tracer_kernel(
    tracers, wet, moved, change_b, change_a, cols_b, cols_a, rows_b, rows_a, after_gather,
    new_tracers, moved_velocity,
):
    del after_gather
    levels, cols_x, rows_y = tracers.shape[1:]
    even_x = lax.axis_index("core") == 0
    after_cols, before_cols = side_columns(cols_b, cols_a)

    def neighbours(tile, index):
        row_a, row_b = (rows_a[index : index + 1, :], rows_b[index : index + 1, :])
        rows = (jnp.where(even_x, row_a, row_b), jnp.where(even_x, row_b, row_a))
        sides = (after_cols[:, index : index + 1], before_cols[:, index : index + 1])
        return neighbours_of(tile, *rows, *sides)

    counts = wet[...].astype(jnp.float32)
    shared = [jnp.minimum(counts, other) for other in neighbours(counts, 4 * levels)]
    diffusivity = TIME_INCREMENT * KAPPA_SPREAD
    edge_b, edge_a = edge_masks((cols_x, rows_y))
    for level in range(levels):
        for part in range(2):
            tile = tracers[part, level]
            spread = laplacian(tile, neighbours(tile, part * levels + level), shared, level)
            new_tracers[part, level] = tile + diffusivity * spread
            added = jnp.where(edge_b, change_b[part, level : level + 1, :], 0.0)
            added = added + jnp.where(edge_a, change_a[part, level : level + 1, :], 0.0)
            moved_velocity[part, level] = moved[part, level] + added


def solve_kernel(
    blocks_x, blocks_y, gathered, swapped, moved_velocity, wet,
    new_velocity, pressure,
    forcing, edges, residual, inverses, lifted_0, lifted_1, smooth_0, smooth_1, smooth_2, image_0, direction_1,
):
    levels, cols_x, rows_y = moved_velocity.shape[1:]
    shape = (cols_x, rows_y)
    lane, sublane = (lanes_of(shape), sublanes_of(shape))
    low_x, high_x = (sublane == 0, sublane == cols_x - 1)
    low_y, high_y = (lane == 0, lane == rows_y - 1)
    zero = jnp.zeros(shape, jnp.float32)

    def each(count, step, carry):
        if blocks_x <= 8:
            for number in range(count):
                carry = step(number, carry)
            return carry
        return lax.fori_loop(0, count, step, carry)

    def each_row(step, carry):
        return each(blocks_x, step, carry)

    def guarded(load, row, column):
        if isinstance(row, int):
            return load(row * blocks_y + column) if 0 <= row < blocks_x else 0.0
        inside = jnp.logical_and(row >= 0, row < blocks_x)
        return load(jnp.clip(row, 0, blocks_x - 1) * blocks_y + column) * inside.astype(jnp.float32)

    def along_x(load, row, column):
        tile = load(row * blocks_y + column)
        other = guarded(lambda i: load(i, slice(0, 1)), row + 1, column)
        after = jnp.where(high_x, other, pltpu.roll(tile, cols_x - 1, 0))
        other = guarded(lambda i: load(i, slice(cols_x - 1, cols_x)), row - 1, column)
        before = jnp.where(low_x, other, pltpu.roll(tile, 1, 0))
        return after + before

    def along_y(tiles):
        ahead = [pltpu.roll(tile, rows_y - 1, 1) for tile in tiles] + [0.0]
        behind = [0.0] + [pltpu.roll(tile, 1, 1) for tile in tiles]
        return [
            jnp.where(high_y, ahead[c + 1], ahead[c]) + jnp.where(low_y, behind[c], behind[c + 1])
            for c in range(blocks_y)
        ]

    def lift(inverse, tile):
        first = inverse * tile
        near = jnp.where(high_x, 0.0, pltpu.roll(first, cols_x - 1, 0))
        near = near + jnp.where(low_x, 0.0, pltpu.roll(first, 1, 0))
        near = near + jnp.where(high_y, 0.0, pltpu.roll(first, rows_y - 1, 1))
        near = near + jnp.where(low_y, 0.0, pltpu.roll(first, 1, 1))
        return tile + near

    def total(values):
        return jnp.sum(values, axis=(0, 1), keepdims=True)

    height = 2 * cols_x + 3

    own_core = lax.axis_index("core")

    def unpack(chip, carry):
        for column in range(blocks_y):
            place = (column * (blocks_x // 2) + chip) * height
            for blocks, core in ((gathered, own_core), (swapped, 1 - own_core)):
                index = (2 * chip + core) * blocks_y + column
                forcing[index] = blocks[pl.ds(place, cols_x), :]
                inverses[index] = blocks[pl.ds(place + cols_x, cols_x), :]
                edges[index, 0:3] = blocks[pl.ds(place + 2 * cols_x, 3), :]
        return carry

    each(blocks_x // 2, unpack, 0)

    def edge_row(which, row, column):
        return guarded(lambda i: edges[i, which : which + 1], row, column)

    def columns_of(first, count):
        corners = [edges[first + number, 2:3] for number in range(count)]
        filler = [jnp.zeros((1, rows_y), jnp.float32)] * (-count % 8)
        return jnp.transpose(jnp.concatenate(corners + filler, axis=0))[0 : 2 * cols_x]

    turned = columns_of(0, blocks_x * blocks_y) if blocks_x <= 8 else None

    def begin(row, carry):
        if turned is None:
            corners = columns_of(row * blocks_y, blocks_y)
        else:
            corners = turned[:, row * blocks_y : (row + 1) * blocks_y]
        for column in range(blocks_y):
            index = row * blocks_y + column
            whole = forcing[index]
            whole = whole + jnp.where(high_x, edge_row(0, row + 1, column), 0.0)
            whole = whole - jnp.where(low_x, edge_row(1, row - 1, column), 0.0)
            if column + 1 < blocks_y:
                whole = whole + jnp.where(high_y, corners[0:cols_x, column + 1 : column + 2], 0.0)
            if column > 0:
                beyond = corners[cols_x : 2 * cols_x, column - 1 : column]
                whole = whole - jnp.where(low_y, beyond, 0.0)
            inverse = inverses[index]
            lifted = lift(inverse, whole)
            residual[index] = whole
            lifted_0[index] = lifted
            smooth_0[index] = inverse * lifted
        return carry

    def operate(lifted, smooth, image):
        def load(index, rows=slice(None)):
            return smooth[index, rows]

        def step(row, carry):
            inner, curvature = carry
            tiles = [smooth[row * blocks_y + c] for c in range(blocks_y)]
            beside = along_y(tiles)
            for column in range(blocks_y):
                index = row * blocks_y + column
                result = lifted[index] - (along_x(load, row, column) + beside[column])
                image[index] = result
                inner = inner + residual[index] * tiles[column]
                curvature = curvature + tiles[column] * result
            return inner, curvature

        inner, curvature = each_row(step, (zero, zero))
        return total(inner), total(curvature)

    def measure_last(lifted, smooth):
        def step(row, carry):
            inner, curvature = carry
            tiles = [smooth[row * blocks_y + c] for c in range(blocks_y)]
            ahead = [pltpu.roll(tile, rows_y - 1, 1) for tile in tiles] + [0.0]
            for column in range(blocks_y):
                index = row * blocks_y + column
                tile = tiles[column]
                other = guarded(lambda i: smooth[i, 0:1], row + 1, column)
                near = jnp.where(high_x, other, pltpu.roll(tile, cols_x - 1, 0))
                near = near + jnp.where(high_y, ahead[column + 1], ahead[column])
                inner = inner + residual[index] * tile
                curvature = curvature + tile * (lifted[index] - 2.0 * near)
            return inner, curvature

        inner, curvature = each_row(step, (zero, zero))
        return total(inner), total(curvature)

    each_row(begin, 0)
    inner_0, curvature_0 = operate(lifted_0, smooth_0, image_0)
    step_0 = inner_0 / curvature_0

    def advance_0(row, carry):
        for column in range(blocks_y):
            index = row * blocks_y + column
            left = residual[index] - step_0 * image_0[index]
            inverse = inverses[index]
            lifted = lift(inverse, left)
            residual[index] = left
            lifted_1[index] = lifted
            smooth_1[index] = inverse * lifted
        return carry

    each_row(advance_0, 0)
    image_1 = lifted_1
    inner_1, curvature_1 = operate(lifted_1, smooth_1, image_1)
    turn_1 = inner_1 / inner_0
    step_1 = inner_1 / (curvature_1 - turn_1 * inner_1 / step_0)

    def advance_1(row, carry):
        for column in range(blocks_y):
            index = row * blocks_y + column
            direction_1[index] = smooth_1[index] + turn_1 * smooth_0[index]
            left = residual[index] - step_1 * (image_1[index] + turn_1 * image_0[index])
            inverse = inverses[index]
            lifted = lift(inverse, left)
            residual[index] = left
            lifted_0[index] = lifted
            smooth_2[index] = inverse * lifted
        return carry

    each_row(advance_1, 0)
    inner_2, curvature_2 = measure_last(lifted_0, smooth_2)
    turn_2 = inner_2 / inner_1
    step_2 = inner_2 / (curvature_2 - turn_2 * inner_2 / step_1)

    def iterate(index):
        previous = direction_1[index]
        result = step_0 * smooth_0[index] + step_1 * previous
        return result + step_2 * (smooth_2[index] + turn_2 * previous)

    own_x, own_y = (position_x(), lax.axis_index("by"))

    def block(shift_x, shift_y):
        row, column = (own_x + shift_x, own_y + shift_y)
        inside = (row >= 0) & (row < blocks_x) & (column >= 0) & (column < blocks_y)
        row, column = (jnp.clip(row, 0, blocks_x - 1), jnp.clip(column, 0, blocks_y - 1))
        return jnp.where(inside, iterate(row * blocks_y + column), 0.0)

    own = iterate(own_x * blocks_y + own_y)
    pressure[...] = own
    upper = jnp.where(high_x, pltpu.roll(block(1, 0), cols_x - 1, 0), pltpu.roll(own, cols_x - 1, 0))
    lower = jnp.where(low_x, pltpu.roll(block(-1, 0), 1, 0), pltpu.roll(own, 1, 0))
    slope_x = GRAVITY * ((upper - lower) * 0.5)
    upper = jnp.where(high_y, pltpu.roll(block(0, 1), rows_y - 1, 1), pltpu.roll(own, rows_y - 1, 1))
    lower = jnp.where(low_y, pltpu.roll(block(0, -1), 1, 1), pltpu.roll(own, 1, 1))
    slope_y = GRAVITY * ((upper - lower) * 0.5)
    counts = wet[...]
    for level in range(levels):
        here = counts > level
        new_velocity[0, level] = moved_velocity[0, level] - jnp.where(here, slope_x, 0.0)
        new_velocity[1, level] = moved_velocity[1, level] - jnp.where(here, slope_y, 0.0)


def latitude_rate(positions, total_rows):
    return 1.5 * jnp.sin(math.pi * ((positions + 0.5) / total_rows - 0.5))


def body(tracers, velocity, wet_levels, thickness, diagonal):
    levels = tracers.shape[1]
    cols_x, rows_y = wet_levels.shape
    chips_z, cores, blocks_y = (lax.axis_size("z"), lax.axis_size("core"), lax.axis_size("by"))
    blocks_x = chips_z * cores
    shape = (cols_x, rows_y)
    height = 2 * cols_x + 3
    rim_rows = 4 * levels + 1

    def like(*dims):
        return jax.ShapeDtypeStruct(dims, jnp.float32)

    def held(*dims):
        return pltpu.VMEM(dims, jnp.float32) if math.prod(dims) <= HELD_SIZE else like(*dims)

    def kept(array):
        if array.size > HELD_SIZE:
            return array
        return pltpu.with_memory_space_constraint(array, pltpu.VMEM)

    fields = (tracers, velocity, wet_levels, diagonal, thickness)
    rows_a, rows_b, cols_a, cols_b, *block = pl.pallas_call(
        pack_rims,
        out_shape=[
            held(rim_rows, rows_y), held(rim_rows, rows_y), held(*shape), held(*shape),
            held(*tracers.shape), held(*velocity.shape), pltpu.VMEM(shape, wet_levels.dtype),
            held(*shape), held(levels, rows_y),
        ],
        in_specs=[ANY] * 5,
        out_specs=[VMEM] * 9,
        scratch_shapes=[pltpu.SMEM(thickness.shape, jnp.float32), pltpu.SemaphoreType.DMA((5,))],
    )(*(pltpu.with_memory_space_constraint(array, pltpu.HBM) for array in fields))
    block = [kept(array) for array in block]

    def exchange(message, axis, first):
        size = blocks_x if axis == "bx" else blocks_y
        pairs = [(i, i + 1) for i in range(first, size - 1, 2)]
        axes = ("z", "core") if axis == "bx" else axis
        return lax.ppermute(message, axes, pairs + [(j, i) for i, j in pairs])

    sent_b, sent_a = (rows_b, rows_a)
    rows_b, rows_a = (exchange(rows_b, "bx", 1), exchange(rows_a, "bx", 0))
    cols_b, cols_a = (exchange(cols_b, "by", 1), exchange(cols_a, "by", 0))
    positions = (lax.axis_index("by") * rows_y + jnp.arange(rows_y, dtype=jnp.int32)).astype(jnp.float32)
    latitude = latitude_rate(positions, blocks_y * rows_y)[None]

    tracers, velocity, wet, diagonal, weights = block
    sent_b, sent_a = (kept(sent_b), kept(sent_a))
    rows_a, rows_b, cols_a, cols_b = (kept(array) for array in (rows_a, rows_b, cols_a, cols_b))
    moved, flows, inner_b, inner_a = pl.pallas_call(
        level_kernel,
        out_shape=[held(*velocity.shape), held(2, *shape)] + [held(levels, rows_y)] * 2,
        in_specs=[VMEM] * 7,
        out_specs=[VMEM] * 4,
    )(tracers, velocity, wet, weights, kept(latitude), cols_b, cols_a)
    inner_b, inner_a, flows = (kept(inner_b), kept(inner_a), kept(flows))
    surface, change_b, change_a = pl.pallas_call(
        edge_kernel,
        out_shape=[held(chips_z * blocks_y, height, 1, rows_y)] + [held(2, levels, rows_y)] * 2,
        in_specs=[VMEM] * 10,
        out_specs=[VMEM] * 3,
    )(sent_b, rows_b, inner_b, sent_a, rows_a, inner_a, weights, wet, diagonal, flows)

    gathered = lax.all_to_all(surface, ("by", "z"), split_axis=0, concat_axis=0, tiled=True)
    swapped = lax.ppermute(gathered, "core", [(0, 1), (1, 0)])
    new_tracers, moved_velocity = pl.pallas_call(
        tracer_kernel,
        out_shape=[like(*tracers.shape), held(*velocity.shape)],
        in_specs=[VMEM] * 10,
        out_specs=[VMEM] * 2,
    )(
        tracers, wet, kept(moved), kept(change_b), kept(change_a),
        cols_b, cols_a, rows_b, rows_a, kept(gathered),
    )
    gathered, swapped = (array.reshape(-1, rows_y) for array in (gathered, swapped))

    def solve(*refs):
        solve_kernel(blocks_x, blocks_y, *refs)

    blocks = blocks_x * blocks_y
    new_velocity, pressure = pl.pallas_call(
        solve,
        out_shape=[like(*velocity.shape), like(*shape)],
        in_specs=[VMEM] * 4,
        out_specs=[VMEM] * 2,
        scratch_shapes=[pltpu.VMEM((blocks, *shape), jnp.float32)] * 11,
        compiler_params=pltpu.CompilerParams(vmem_limit_bytes=(4 + 52 * blocks // 1024) * 2**20),
    )(kept(gathered), kept(swapped), kept(moved_velocity), wet)
    return new_tracers, new_velocity, pressure


def solution(mesh):
    size_x, size_y = (mesh.shape["bx"], mesh.shape["by"])
    chips = jax.sharding.Mesh(mesh.devices.reshape(size_x // 2, 2, size_y), ("z", "core", "by"))
    along_x = ("z", "core")
    placed = (
        P(None, None, along_x, "by"),
        P(None, None, along_x, "by"),
        P(along_x, "by"),
        P(),
        P(along_x, None),
    )
    return jax.shard_map(
        body,
        mesh=chips,
        in_specs=placed,
        out_specs=(P(None, None, along_x, "by"), P(None, None, along_x, "by"), P(along_x, "by")),
        check_vma=False,
    )
```

```python
import math

import jax
import jax.numpy as jnp
from jax import lax
from jax.experimental import pallas as pl
from jax.experimental.pallas import tpu as pltpu
from jax.sharding import PartitionSpec as P

ITERS = 3

HEAT_ALPHA = 0.5
SALINITY_BETA = 0.8
KAPPA_SPREAD = 0.15
VISCOSITY = 0.1
TIME_INCREMENT = 0.2
GRAVITY = 1.0

HELD_SIZE = 2**18

VMEM = pl.BlockSpec(memory_space=pltpu.VMEM)
ANY = pl.BlockSpec(memory_space=pl.ANY)


def lanes_of(shape):
    return lax.broadcasted_iota(jnp.int32, shape, 1)


def sublanes_of(shape):
    return lax.broadcasted_iota(jnp.int32, shape, 0)


def position_x():
    return lax.axis_index("z") * lax.axis_size("core") + lax.axis_index("core")


def pack_rims(
    tracers_in, velocity_in, wet_in, diagonal_in, thickness_in,
    rows_a, rows_b, cols_a, cols_b, tracers, velocity, wet, diagonal, weights,
    thickness, semaphores,
):
    levels, cols_x, rows_y = tracers.shape[1:]
    row_start = pl.multiple_of(lax.axis_index("by") * rows_y, rows_y)
    copies = [
        pltpu.make_async_copy(source, target, semaphores.at[number])
        for number, (source, target) in enumerate((
            (tracers_in, tracers),
            (velocity_in, velocity),
            (wet_in, wet),
            (thickness_in, thickness),
            (diagonal_in.at[:, pl.ds(row_start, rows_y)], diagonal),
        ))
    ]
    for copy in copies:
        copy.start()
    even_x, even_y = (lax.axis_index("core") == 0, lax.axis_index("by") % 2 == 0)
    lane = lanes_of((cols_x, rows_y))
    of_tracers, of_velocity, of_wet, *others = copies
    of_wet.wait()
    of_tracers.wait()
    counts = wet[...].astype(jnp.float32)
    first, last = jnp.zeros_like(counts), jnp.zeros_like(counts)
    for index in range(4 * levels + 1):
        field, level = divmod(index, levels)
        if index == 2 * levels:
            of_velocity.wait()
        if field < 4:
            tile = (tracers if field < 2 else velocity)[field % 2, level]
        else:
            tile = counts
        top, bottom = (tile[0:1, :], tile[cols_x - 1 : cols_x, :])
        rows_a[index : index + 1, :] = jnp.where(even_x, bottom, top)
        rows_b[index : index + 1, :] = jnp.where(even_x, top, bottom)
        first = jnp.where(lane == index, tile[:, 0:1], first)
        last = jnp.where(lane == index, tile[:, rows_y - 1 : rows_y], last)
    cols_a[...] = jnp.where(even_y, last, first)
    cols_b[...] = jnp.where(even_y, first, last)
    for copy in others:
        copy.wait()
    for level in range(levels):
        weights[level : level + 1, :] = jnp.full((1, rows_y), thickness[level], jnp.float32)


def edges_of(shape):
    sublane, lane = (sublanes_of(shape), lanes_of(shape))
    return sublane == 0, sublane == shape[0] - 1, lane == 0, lane == shape[1] - 1


def neighbours_of(tile, after_row, before_row, after_col, before_col):
    low_x, high_x, low_y, high_y = edges_of(tile.shape)
    cols_x, rows_y = tile.shape
    return (
        jnp.where(high_x, after_row, pltpu.roll(tile, cols_x - 1, 0)),
        jnp.where(low_x, before_row, pltpu.roll(tile, 1, 0)),
        jnp.where(high_y, after_col, pltpu.roll(tile, rows_y - 1, 1)),
        jnp.where(low_y, before_col, pltpu.roll(tile, 1, 1)),
    )


def laplacian(tile, others, shared, level):
    total = jnp.zeros_like(tile)
    for other, limit in zip(others, shared):
        total = total + jnp.where(limit > level, other - tile, 0.0)
    return total


def side_columns(cols_b, cols_a):
    even_y = lax.axis_index("by") % 2 == 0
    a, b = (cols_a[...], cols_b[...])
    return jnp.where(even_y, a, b), jnp.where(even_y, b, a)


def level_kernel(
    tracers, velocity, wet, weights, latitude, cols_b, cols_a,
    moved_velocity, flows, inner_b, inner_a,
):
    levels, cols_x, rows_y = tracers.shape[1:]
    shape = (cols_x, rows_y)
    even_x = lax.axis_index("core") == 0
    after_cols, before_cols = side_columns(cols_b, cols_a)

    def neighbours(tile, index):
        sides = (after_cols[:, index : index + 1], before_cols[:, index : index + 1])
        return neighbours_of(tile, 0.0, 0.0, *sides)

    counts = wet[...].astype(jnp.float32)
    around = neighbours(counts, 4 * levels)
    shared = [jnp.minimum(counts, other) for other in around]
    both_x = jnp.minimum(shared[0], shared[1])
    both_y = jnp.minimum(shared[2], shared[3])
    zero = jnp.zeros(shape, jnp.float32)
    coriolis = jnp.broadcast_to(latitude[...], shape)
    difference_x, difference_y, flow_x, flow_y = (zero, zero, zero, zero)
    for level in range(levels):
        here = counts > level
        weight = weights[level : level + 1, :]
        heat_around = neighbours(tracers[0, level], level)
        salt_around = neighbours(tracers[1, level], levels + level)
        loads = [
            jnp.where(count > level, SALINITY_BETA * s - HEAT_ALPHA * t, 0.0)
            for count, s, t in zip(around, salt_around, heat_around)
        ]
        difference_x = difference_x + weight * (loads[0] - loads[1])
        difference_y = difference_y + weight * (loads[2] - loads[3])
        low, high = (difference_x[0:1, :], difference_x[cols_x - 1 : cols_x, :])
        inner_b[level : level + 1, :] = jnp.where(even_x, low, high)
        inner_a[level : level + 1, :] = jnp.where(even_x, high, low)
        gradient_x = jnp.where(both_x > level, difference_x * 0.5, 0.0)
        gradient_y = jnp.where(both_y > level, difference_y * 0.5, 0.0)
        zonal, merid = (velocity[0, level], velocity[1, level])
        spread_x = laplacian(zonal, neighbours(zonal, 2 * levels + level), shared, level)
        spread_y = laplacian(merid, neighbours(merid, 3 * levels + level), shared, level)
        zonal_rate = coriolis * merid - gradient_x + VISCOSITY * spread_x
        merid_rate = -coriolis * zonal - gradient_y + VISCOSITY * spread_y
        next_zonal = zonal + jnp.where(here, TIME_INCREMENT * zonal_rate, 0.0)
        next_merid = merid + jnp.where(here, TIME_INCREMENT * merid_rate, 0.0)
        moved_velocity[0, level] = next_zonal
        moved_velocity[1, level] = next_merid
        flow_x = flow_x + jnp.where(here, weight * next_zonal, 0.0)
        flow_y = flow_y + jnp.where(here, weight * next_merid, 0.0)
    flows[0] = flow_x
    flows[1] = flow_y


def edge_change(own, across, inner, within, weights, sign, change):
    levels, rows_y = weights.shape
    count = across[4 * levels : 4 * levels + 1, :]
    shared = jnp.minimum(count, own[4 * levels : 4 * levels + 1, :])
    both = jnp.minimum(shared, within)
    pressure = jnp.zeros((1, rows_y), jnp.float32)
    added_x, added_y = (pressure, pressure)
    for level in range(levels):
        heat, salt, zonal, merid = (
            across[field * levels + level : field * levels + level + 1, :] for field in range(4)
        )
        own_zonal, own_merid = (
            own[field * levels + level : field * levels + level + 1, :] for field in (2, 3)
        )
        weight = weights[level : level + 1, :]
        load = jnp.where(count > level, SALINITY_BETA * salt - HEAT_ALPHA * heat, 0.0)
        pressure = pressure + weight * load
        slope = (inner[level : level + 1, :] + sign * pressure) * 0.5
        spread_x = jnp.where(shared > level, zonal - own_zonal, 0.0)
        spread_y = jnp.where(shared > level, merid - own_merid, 0.0)
        rate = VISCOSITY * spread_x - jnp.where(both > level, slope, 0.0)
        change_x = TIME_INCREMENT * rate
        change_y = (TIME_INCREMENT * VISCOSITY) * spread_y
        change[0, level : level + 1, :] = change_x
        change[1, level : level + 1, :] = change_y
        added_x = added_x + weight * change_x
        added_y = added_y + weight * change_y
    return added_x, added_y


def edge_masks(shape):
    even_x = lax.axis_index("core") == 0
    sublane = sublanes_of(shape)
    last = shape[0] - 1
    return sublane == jnp.where(even_x, 0, last), sublane == jnp.where(even_x, last, 0)


def edge_kernel(
    own_b, across_b, inner_b, own_a, across_a, inner_a, weights, wet, diagonal, flows,
    surface, change_b, change_a,
):
    cols_x, rows_y = shape = wet.shape
    low_x, high_x, low_y, high_y = edges_of(shape)
    lane, sublane = (lanes_of(shape), sublanes_of(shape))
    even_x = lax.axis_index("core") == 0
    sign = jnp.where(even_x, -1.0, 1.0)
    counts = wet[...].astype(jnp.float32)
    second, last_but_one = (counts[1:2, :], counts[cols_x - 2 : cols_x - 1, :])
    within_b = jnp.where(even_x, second, last_but_one)
    within_a = jnp.where(even_x, last_but_one, second)
    added_b = edge_change(own_b, across_b, inner_b, within_b, weights, sign, change_b)
    added_a = edge_change(own_a, across_a, inner_a, within_a, weights, -sign, change_a)
    edge_b, edge_a = edge_masks(shape)
    flow_x, flow_y = (
        flows[part] + jnp.where(edge_b, added_b[part], 0.0) + jnp.where(edge_a, added_a[part], 0.0)
        for part in range(2)
    )
    inverse = jnp.where(counts > 0, 1.0, 0.0) / (4.0 + diagonal[...])
    ahead = jnp.where(high_x, 0.0, pltpu.roll(flow_x, cols_x - 1, 0))
    behind = jnp.where(low_x, 0.0, pltpu.roll(flow_x, 1, 0))
    slope = ahead - behind
    ahead = jnp.where(high_y, 0.0, pltpu.roll(flow_y, rows_y - 1, 1))
    behind = jnp.where(low_y, 0.0, pltpu.roll(flow_y, 1, 1))
    divergence = (slope + (ahead - behind)) * 0.5
    edge_x = flow_x * 0.5
    edge_y = flow_y * 0.5
    first = jnp.where(lane == sublane, edge_y[:, 0:1], 0.0)
    last = jnp.where(lane == sublane + cols_x, edge_y[:, rows_y - 1 : rows_y], 0.0)
    corner = jnp.sum(first + last, axis=0, keepdims=True)

    def place(target):
        surface[target, 0:cols_x, 0, :] = divergence
        surface[target, cols_x : 2 * cols_x, 0, :] = inverse
        surface[target, 2 * cols_x : 2 * cols_x + 1, 0, :] = edge_x[0:1, :]
        surface[target, 2 * cols_x + 1 : 2 * cols_x + 2, 0, :] = edge_x[cols_x - 1 : cols_x, :]
        surface[target, 2 * cols_x + 2 : 2 * cols_x + 3, 0, :] = corner

    pl.loop(0, surface.shape[0], unroll=8)(place)


def tracer_kernel(
    tracers, wet, moved, change_b, change_a, cols_b, cols_a, rows_b, rows_a, after_gather,
    new_tracers, moved_velocity,
):
    del after_gather
    levels, cols_x, rows_y = tracers.shape[1:]
    even_x = lax.axis_index("core") == 0
    after_cols, before_cols = side_columns(cols_b, cols_a)

    def neighbours(tile, index):
        row_a, row_b = (rows_a[index : index + 1, :], rows_b[index : index + 1, :])
        rows = (jnp.where(even_x, row_a, row_b), jnp.where(even_x, row_b, row_a))
        sides = (after_cols[:, index : index + 1], before_cols[:, index : index + 1])
        return neighbours_of(tile, *rows, *sides)

    counts = wet[...].astype(jnp.float32)
    shared = [jnp.minimum(counts, other) for other in neighbours(counts, 4 * levels)]
    diffusivity = TIME_INCREMENT * KAPPA_SPREAD
    edge_b, edge_a = edge_masks((cols_x, rows_y))
    for level in range(levels):
        for part in range(2):
            tile = tracers[part, level]
            spread = laplacian(tile, neighbours(tile, part * levels + level), shared, level)
            new_tracers[part, level] = tile + diffusivity * spread
            added = jnp.where(edge_b, change_b[part, level : level + 1, :], 0.0)
            added = added + jnp.where(edge_a, change_a[part, level : level + 1, :], 0.0)
            moved_velocity[part, level] = moved[part, level] + added


def solve_kernel(
    blocks_x, blocks_y, gathered, swapped, moved_velocity, wet,
    new_velocity, pressure,
    forcing, edges, residual, inverses, lifted_0, lifted_1, smooth_0, smooth_1, smooth_2, image_0, direction_1,
):
    levels, cols_x, rows_y = moved_velocity.shape[1:]
    shape = (cols_x, rows_y)
    lane, sublane = (lanes_of(shape), sublanes_of(shape))
    low_x, high_x = (sublane == 0, sublane == cols_x - 1)
    low_y, high_y = (lane == 0, lane == rows_y - 1)
    zero = jnp.zeros(shape, jnp.float32)

    def each(count, step, carry):
        if blocks_x <= 8:
            for number in range(count):
                carry = step(number, carry)
            return carry
        return lax.fori_loop(0, count, step, carry)

    def each_row(step, carry):
        return each(blocks_x, step, carry)

    def guarded(load, row, column):
        if isinstance(row, int):
            return load(row * blocks_y + column) if 0 <= row < blocks_x else 0.0
        inside = jnp.logical_and(row >= 0, row < blocks_x)
        return load(jnp.clip(row, 0, blocks_x - 1) * blocks_y + column) * inside.astype(jnp.float32)

    def along_x(load, row, column):
        tile = load(row * blocks_y + column)
        other = guarded(lambda i: load(i, slice(0, 1)), row + 1, column)
        after = jnp.where(high_x, other, pltpu.roll(tile, cols_x - 1, 0))
        other = guarded(lambda i: load(i, slice(cols_x - 1, cols_x)), row - 1, column)
        before = jnp.where(low_x, other, pltpu.roll(tile, 1, 0))
        return after + before

    def along_y(tiles):
        ahead = [pltpu.roll(tile, rows_y - 1, 1) for tile in tiles] + [0.0]
        behind = [0.0] + [pltpu.roll(tile, 1, 1) for tile in tiles]
        return [
            jnp.where(high_y, ahead[c + 1], ahead[c]) + jnp.where(low_y, behind[c], behind[c + 1])
            for c in range(blocks_y)
        ]

    def lift(inverse, tile):
        first = inverse * tile
        near = jnp.where(high_x, 0.0, pltpu.roll(first, cols_x - 1, 0))
        near = near + jnp.where(low_x, 0.0, pltpu.roll(first, 1, 0))
        near = near + jnp.where(high_y, 0.0, pltpu.roll(first, rows_y - 1, 1))
        near = near + jnp.where(low_y, 0.0, pltpu.roll(first, 1, 1))
        return tile + near

    def total(values):
        return jnp.sum(values, axis=(0, 1), keepdims=True)

    height = 2 * cols_x + 3

    own_core = lax.axis_index("core")

    def unpack(chip, carry):
        for column in range(blocks_y):
            place = (column * (blocks_x // 2) + chip) * height
            for blocks, core in ((gathered, own_core), (swapped, 1 - own_core)):
                index = (2 * chip + core) * blocks_y + column
                forcing[index] = blocks[pl.ds(place, cols_x), :]
                inverses[index] = blocks[pl.ds(place + cols_x, cols_x), :]
                edges[index, 0:3] = blocks[pl.ds(place + 2 * cols_x, 3), :]
        return carry

    each(blocks_x // 2, unpack, 0)

    def edge_row(which, row, column):
        return guarded(lambda i: edges[i, which : which + 1], row, column)

    def columns_of(first, count):
        corners = [edges[first + number, 2:3] for number in range(count)]
        filler = [jnp.zeros((1, rows_y), jnp.float32)] * (-count % 8)
        return jnp.transpose(jnp.concatenate(corners + filler, axis=0))[0 : 2 * cols_x]

    turned = columns_of(0, blocks_x * blocks_y) if blocks_x <= 8 else None

    def begin(row, carry):
        if turned is None:
            corners = columns_of(row * blocks_y, blocks_y)
        else:
            corners = turned[:, row * blocks_y : (row + 1) * blocks_y]
        for column in range(blocks_y):
            index = row * blocks_y + column
            whole = forcing[index]
            whole = whole + jnp.where(high_x, edge_row(0, row + 1, column), 0.0)
            whole = whole - jnp.where(low_x, edge_row(1, row - 1, column), 0.0)
            if column + 1 < blocks_y:
                whole = whole + jnp.where(high_y, corners[0:cols_x, column + 1 : column + 2], 0.0)
            if column > 0:
                beyond = corners[cols_x : 2 * cols_x, column - 1 : column]
                whole = whole - jnp.where(low_y, beyond, 0.0)
            inverse = inverses[index]
            lifted = lift(inverse, whole)
            residual[index] = whole
            lifted_0[index] = lifted
            smooth_0[index] = inverse * lifted
        return carry

    def operate(lifted, smooth, image):
        def load(index, rows=slice(None)):
            return smooth[index, rows]

        def step(row, carry):
            inner, curvature = carry
            tiles = [smooth[row * blocks_y + c] for c in range(blocks_y)]
            beside = along_y(tiles)
            for column in range(blocks_y):
                index = row * blocks_y + column
                result = lifted[index] - (along_x(load, row, column) + beside[column])
                image[index] = result
                inner = inner + residual[index] * tiles[column]
                curvature = curvature + tiles[column] * result
            return inner, curvature

        inner, curvature = each_row(step, (zero, zero))
        return total(inner), total(curvature)

    def measure_last(lifted, smooth):
        def step(row, carry):
            inner, curvature = carry
            tiles = [smooth[row * blocks_y + c] for c in range(blocks_y)]
            ahead = [pltpu.roll(tile, rows_y - 1, 1) for tile in tiles] + [0.0]
            for column in range(blocks_y):
                index = row * blocks_y + column
                tile = tiles[column]
                other = guarded(lambda i: smooth[i, 0:1], row + 1, column)
                near = jnp.where(high_x, other, pltpu.roll(tile, cols_x - 1, 0))
                near = near + jnp.where(high_y, ahead[column + 1], ahead[column])
                inner = inner + residual[index] * tile
                curvature = curvature + tile * (lifted[index] - 2.0 * near)
            return inner, curvature

        inner, curvature = each_row(step, (zero, zero))
        return total(inner), total(curvature)

    each_row(begin, 0)
    inner_0, curvature_0 = operate(lifted_0, smooth_0, image_0)
    step_0 = inner_0 / curvature_0

    def advance_0(row, carry):
        for column in range(blocks_y):
            index = row * blocks_y + column
            left = residual[index] - step_0 * image_0[index]
            inverse = inverses[index]
            lifted = lift(inverse, left)
            residual[index] = left
            lifted_1[index] = lifted
            smooth_1[index] = inverse * lifted
        return carry

    each_row(advance_0, 0)
    image_1 = lifted_1
    inner_1, curvature_1 = operate(lifted_1, smooth_1, image_1)
    turn_1 = inner_1 / inner_0
    step_1 = inner_1 / (curvature_1 - turn_1 * inner_1 / step_0)

    def advance_1(row, carry):
        for column in range(blocks_y):
            index = row * blocks_y + column
            direction_1[index] = smooth_1[index] + turn_1 * smooth_0[index]
            left = residual[index] - step_1 * (image_1[index] + turn_1 * image_0[index])
            inverse = inverses[index]
            lifted = lift(inverse, left)
            residual[index] = left
            lifted_0[index] = lifted
            smooth_2[index] = inverse * lifted
        return carry

    each_row(advance_1, 0)
    inner_2, curvature_2 = measure_last(lifted_0, smooth_2)
    turn_2 = inner_2 / inner_1
    step_2 = inner_2 / (curvature_2 - turn_2 * inner_2 / step_1)

    def iterate(index):
        previous = direction_1[index]
        result = step_0 * smooth_0[index] + step_1 * previous
        return result + step_2 * (smooth_2[index] + turn_2 * previous)

    own_x, own_y = (position_x(), lax.axis_index("by"))

    def block(shift_x, shift_y):
        row, column = (own_x + shift_x, own_y + shift_y)
        inside = (row >= 0) & (row < blocks_x) & (column >= 0) & (column < blocks_y)
        row, column = (jnp.clip(row, 0, blocks_x - 1), jnp.clip(column, 0, blocks_y - 1))
        return jnp.where(inside, iterate(row * blocks_y + column), 0.0)

    own = iterate(own_x * blocks_y + own_y)
    pressure[...] = own
    upper = jnp.where(high_x, pltpu.roll(block(1, 0), cols_x - 1, 0), pltpu.roll(own, cols_x - 1, 0))
    lower = jnp.where(low_x, pltpu.roll(block(-1, 0), 1, 0), pltpu.roll(own, 1, 0))
    slope_x = GRAVITY * ((upper - lower) * 0.5)
    upper = jnp.where(high_y, pltpu.roll(block(0, 1), rows_y - 1, 1), pltpu.roll(own, rows_y - 1, 1))
    lower = jnp.where(low_y, pltpu.roll(block(0, -1), 1, 1), pltpu.roll(own, 1, 1))
    slope_y = GRAVITY * ((upper - lower) * 0.5)
    counts = wet[...]
    for level in range(levels):
        here = counts > level
        new_velocity[0, level] = moved_velocity[0, level] - jnp.where(here, slope_x, 0.0)
        new_velocity[1, level] = moved_velocity[1, level] - jnp.where(here, slope_y, 0.0)


def latitude_rate(positions, total_rows):
    return 1.5 * jnp.sin(math.pi * ((positions + 0.5) / total_rows - 0.5))


def body(tracers, velocity, wet_levels, thickness, diagonal):
    levels = tracers.shape[1]
    cols_x, rows_y = wet_levels.shape
    chips_z, cores, blocks_y = (lax.axis_size("z"), lax.axis_size("core"), lax.axis_size("by"))
    blocks_x = chips_z * cores
    shape = (cols_x, rows_y)
    height = 2 * cols_x + 3
    rim_rows = 4 * levels + 1

    def like(*dims):
        return jax.ShapeDtypeStruct(dims, jnp.float32)

    def held(*dims):
        return pltpu.VMEM(dims, jnp.float32) if math.prod(dims) <= HELD_SIZE else like(*dims)

    def kept(array):
        if array.size > HELD_SIZE:
            return array
        return pltpu.with_memory_space_constraint(array, pltpu.VMEM)

    fields = (tracers, velocity, wet_levels, diagonal, thickness)
    rows_a, rows_b, cols_a, cols_b, *block = pl.pallas_call(
        pack_rims,
        out_shape=[
            held(rim_rows, rows_y), held(rim_rows, rows_y), held(*shape), held(*shape),
            held(*tracers.shape), held(*velocity.shape), pltpu.VMEM(shape, wet_levels.dtype),
            held(*shape), held(levels, rows_y),
        ],
        in_specs=[ANY] * 5,
        out_specs=[VMEM] * 9,
        scratch_shapes=[pltpu.SMEM(thickness.shape, jnp.float32), pltpu.SemaphoreType.DMA((5,))],
    )(*(pltpu.with_memory_space_constraint(array, pltpu.HBM) for array in fields))
    block = [kept(array) for array in block]

    def exchange(message, axis, first):
        size = blocks_x if axis == "bx" else blocks_y
        pairs = [(i, i + 1) for i in range(first, size - 1, 2)]
        axes = ("z", "core") if axis == "bx" else axis
        return lax.ppermute(message, axes, pairs + [(j, i) for i, j in pairs])

    sent_b, sent_a = (rows_b, rows_a)
    rows_b, rows_a = (exchange(rows_b, "bx", 1), exchange(rows_a, "bx", 0))
    cols_b, cols_a = (exchange(cols_b, "by", 1), exchange(cols_a, "by", 0))
    positions = (lax.axis_index("by") * rows_y + jnp.arange(rows_y, dtype=jnp.int32)).astype(jnp.float32)
    latitude = latitude_rate(positions, blocks_y * rows_y)[None]

    tracers, velocity, wet, diagonal, weights = block
    sent_b, sent_a = (kept(sent_b), kept(sent_a))
    rows_a, rows_b, cols_a, cols_b = (kept(array) for array in (rows_a, rows_b, cols_a, cols_b))
    moved, flows, inner_b, inner_a = pl.pallas_call(
        level_kernel,
        out_shape=[held(*velocity.shape), held(2, *shape)] + [held(levels, rows_y)] * 2,
        in_specs=[VMEM] * 7,
        out_specs=[VMEM] * 4,
    )(tracers, velocity, wet, weights, kept(latitude), cols_b, cols_a)
    inner_b, inner_a, flows = (kept(inner_b), kept(inner_a), kept(flows))
    surface, change_b, change_a = pl.pallas_call(
        edge_kernel,
        out_shape=[held(chips_z * blocks_y, height, 1, rows_y)] + [held(2, levels, rows_y)] * 2,
        in_specs=[VMEM] * 10,
        out_specs=[VMEM] * 3,
    )(sent_b, rows_b, inner_b, sent_a, rows_a, inner_a, weights, wet, diagonal, flows)

    gathered = lax.all_to_all(surface, ("by", "z"), split_axis=0, concat_axis=0, tiled=True)
    swapped = lax.ppermute(gathered, "core", [(0, 1), (1, 0)])
    new_tracers, moved_velocity = pl.pallas_call(
        tracer_kernel,
        out_shape=[like(*tracers.shape), held(*velocity.shape)],
        in_specs=[VMEM] * 10,
        out_specs=[VMEM] * 2,
    )(
        tracers, wet, kept(moved), kept(change_b), kept(change_a),
        cols_b, cols_a, rows_b, rows_a, kept(gathered),
    )
    gathered, swapped = (array.reshape(-1, rows_y) for array in (gathered, swapped))

    def solve(*refs):
        solve_kernel(blocks_x, blocks_y, *refs)

    blocks = blocks_x * blocks_y
    new_velocity, pressure = pl.pallas_call(
        solve,
        out_shape=[like(*velocity.shape), like(*shape)],
        in_specs=[VMEM] * 4,
        out_specs=[VMEM] * 2,
        scratch_shapes=[pltpu.VMEM((blocks, *shape), jnp.float32)] * 11,
        compiler_params=pltpu.CompilerParams(vmem_limit_bytes=(4 + 52 * blocks // 1024) * 2**20),
    )(kept(gathered), kept(swapped), kept(moved_velocity), wet)
    return new_tracers, new_velocity, pressure


def solution(mesh):
    size_x, size_y = (mesh.shape["bx"], mesh.shape["by"])
    chips = jax.sharding.Mesh(mesh.devices.reshape(size_x // 2, 2, size_y), ("z", "core", "by"))
    along_x = ("z", "core")
    placed = (
        P(None, None, along_x, "by"),
        P(None, None, along_x, "by"),
        P(along_x, "by"),
        P(),
        P(along_x, None),
    )
    return jax.shard_map(
        body,
        mesh=chips,
        in_specs=placed,
        out_specs=(P(None, None, along_x, "by"), P(None, None, along_x, "by"), P(along_x, "by")),
        check_vma=False,
    )
```
